32 devices in a mesh: dp: 4 (over y, core), fsdp: 8 (over z, x).
Axes of the slice: x: 2, y: 2, z: 4, core: 2. Of those that a mesh axis runs over, the one named last changes fastest.
Arguments:
- tokens: bfloat16 [16384, 768], P(('dp', 'fsdp')), may hold values from -6 to 6
- segment_ids: int32 [16384], P(('dp', 'fsdp')), may hold values from 0 to 3, as said below
- ln1_gain: bfloat16 [768], P(('dp', 'fsdp')), may hold values from 0.5 to 1.5
- ln1_bias: bfloat16 [768], P(('dp', 'fsdp')), may hold values from -1 to 1
- qkv_weight: bfloat16 [768, 2304], P(('dp', 'fsdp')), may hold values from -0.21875 to 0.21875
- qkv_bias: bfloat16 [2304], P(('dp', 'fsdp')), may hold values from -1 to 1
- out_weight: bfloat16 [768, 768], P(('dp', 'fsdp')), may hold values from -1.75 to 1.75
- out_bias: bfloat16 [768], P(('dp', 'fsdp')), may hold values from -1 to 1
- ln2_gain: bfloat16 [768], P(('dp', 'fsdp')), may hold values from 0.5 to 1.5
- ln2_bias: bfloat16 [768], P(('dp', 'fsdp')), may hold values from -1 to 1
- fc1_weight: bfloat16 [768, 3072], P(('dp', 'fsdp')), may hold values from -0.21875 to 0.21875
- fc1_bias: bfloat16 [3072], P(('dp', 'fsdp')), may hold values from -1 to 1
- fc2_weight: bfloat16 [3072, 768], P(('dp', 'fsdp')), may hold values from -0.109375 to 0.109375
- fc2_bias: bfloat16 [768], P(('dp', 'fsdp')), may hold values from -1 to 1
- output_grad: bfloat16 [16384, 768], P(('dp', 'fsdp')), may hold values from -6 to 6
Outputs:
- output: bfloat16 [16384, 768], P(('dp', 'fsdp'))
- input_grad: float32 [16384, 768], P(('dp', 'fsdp'))
- ln1_gain_grad: float32 [768], P(('dp', 'fsdp'))
- ln1_bias_grad: float32 [768], P(('dp', 'fsdp'))
- qkv_weight_grad: float32 [768, 2304], P(('dp', 'fsdp'))
- qkv_bias_grad: float32 [2304], P(('dp', 'fsdp'))
- out_weight_grad: float32 [768, 768], P(('dp', 'fsdp'))
- out_bias_grad: float32 [768], P(('dp', 'fsdp'))
- ln2_gain_grad: float32 [768], P(('dp', 'fsdp'))
- ln2_bias_grad: float32 [768], P(('dp', 'fsdp'))
- fc1_weight_grad: float32 [768, 3072], P(('dp', 'fsdp'))
- fc1_bias_grad: float32 [3072], P(('dp', 'fsdp'))
- fc2_weight_grad: float32 [3072, 768], P(('dp', 'fsdp'))
- fc2_bias_grad: float32 [768], P(('dp', 'fsdp'))
The draws below stay inside these ranges and needn't reach their ends.
Inputs may be any that keep to these rules, and one draw needn't show every extreme that they name: `segment_ids`: within each sequence of 1024 tokens the numbers never fall and every one of 0, 1, 2, 3 occurs.
All inputs are finite; a program needn't handle non-finite values.
Results may differ from the reference program's by a relative error of at most 0.01.
Values may be sent and summed in bfloat16 or wider, within the bound.
No kernel may reach another device: no remote copies, remote signals or barrier semaphores. Data moves between devices by JAX's collectives and lax.ppermute only.
A program may use at most 192 MiB of HBM per device.

```python
import math
import jax
import jax.numpy as jnp
from jax import lax

D = 768
HEADS = 12
HEAD = 64
FF = 3072
LENGTH = 1024
TOKENS = 16384
SEQS = 16


def draw_segment_ids(key, part):
    key = jax.random.fold_in(key, 11)
    keys_three = jax.random.split(key, 3)
    number = TOKENS // LENGTH
    first_cut = jax.random.randint(keys_three[0], (number, 1), LENGTH // 8, 3 * LENGTH // 8 + 1)
    second_cut = jax.random.randint(keys_three[1], (number, 1), 5 * LENGTH // 8, 7 * LENGTH // 8 + 1)
    third_cut = jax.random.randint(keys_three[2], (number, 1), second_cut + LENGTH // 16, LENGTH - LENGTH // 16 + 1)
    position = jnp.arange(LENGTH, dtype=jnp.int32)[None, :]
    numbers = (position >= first_cut).astype(jnp.int32) + (position >= second_cut).astype(jnp.int32) + (position >= third_cut).astype(jnp.int32)
    return numbers.reshape(TOKENS)


def block_scale(rng, dims, cuts, smallest, largest):
    gain = 1.0
    for axis_at, blocks in cuts:
        draws = jax.random.uniform(jax.random.fold_in(jax.random.fold_in(rng, 6), axis_at), (blocks,), jnp.float32, smallest / len(cuts), largest / len(cuts))
        gain = gain * jnp.repeat(jnp.exp(draws), dims[axis_at] // blocks).reshape((-1,) + (1,) * (len(dims) - 1 - axis_at))
    return gain


def normal_values(rng, extent, deviation, bound, cuts=(), held_as=jnp.bfloat16):
    level = block_scale(rng, extent, cuts, -0.22, 0.18) if cuts else 1.0
    entries = jax.random.normal(rng, extent, jnp.float32) * deviation * level
    return jnp.minimum(jnp.maximum(entries, -bound), bound).astype(held_as)


def setup_inputs(seed: int = 0) -> dict:
    arg_keys = jax.random.split(jax.random.key(seed), 16)
    tokens = normal_values(arg_keys[0], (TOKENS, D), 1.0, 6.0, ((0, 32),))
    segment_ids = draw_segment_ids(jax.random.fold_in(arg_keys[15], 71), 0)
    ln1_gain = jnp.clip(1.0 + 0.1 * jax.random.normal(arg_keys[2], (D,), jnp.float32), 0.5, 1.5).astype(jnp.bfloat16)
    ln1_bias = normal_values(arg_keys[3], (D,), 0.2, 1.0, ((0, 32),))
    qkv_weight = normal_values(arg_keys[4], (D, 3 * D), D ** -0.5, 0.21875, ((0, 32),))
    qkv_bias = normal_values(arg_keys[5], (3 * D,), 0.2, 1.0, ((0, 32),))
    out_weight = normal_values(arg_keys[6], (D, D), (D // 64) ** -0.5, 1.75, ((0, 32),))
    out_bias = normal_values(arg_keys[7], (D,), 0.2, 1.0, ((0, 32),))
    ln2_gain = jnp.clip(1.0 + 0.1 * jax.random.normal(arg_keys[8], (D,), jnp.float32), 0.5, 1.5).astype(jnp.bfloat16)
    ln2_bias = normal_values(arg_keys[9], (D,), 0.2, 1.0, ((0, 32),))
    fc1_weight = normal_values(arg_keys[10], (D, FF), D ** -0.5, 0.21875, ((0, 32),))
    fc1_bias = normal_values(arg_keys[11], (FF,), 0.2, 1.0, ((0, 32),))
    fc2_weight = normal_values(arg_keys[12], (FF, D), FF ** -0.5, 0.109375, ((0, 32),))
    fc2_bias = normal_values(arg_keys[13], (D,), 0.2, 1.0, ((0, 32),))
    output_grad = normal_values(arg_keys[14], (TOKENS, D), 1.0, 6.0, ((0, 32),))
    return {"tokens": tokens, "segment_ids": segment_ids, "ln1_gain": ln1_gain, "ln1_bias": ln1_bias, "qkv_weight": qkv_weight, "qkv_bias": qkv_bias, "out_weight": out_weight, "out_bias": out_bias, "ln2_gain": ln2_gain, "ln2_bias": ln2_bias, "fc1_weight": fc1_weight, "fc1_bias": fc1_bias, "fc2_weight": fc2_weight, "fc2_bias": fc2_bias, "output_grad": output_grad}


EPSILON = 1e-05
FULL_PRECISION = lax.Precision.HIGHEST

@jax.custom_vjp
def low(v):
    return lax.optimization_barrier(v.astype(jnp.bfloat16)).astype(jnp.float32)

@jax.custom_vjp
def low_back(v):
    return v

def low_keep(v):
    return (low(v), None)

def low_pass(kept, grad):
    return (grad,)

def back_keep(v):
    return (v, None)

def back_low(kept, grad):
    return (low(grad),)
low.defvjp(low_keep, low_pass)
low_back.defvjp(back_keep, back_low)

def layer_norm(inputs, gain_vec, bias_vec):
    average = lax.optimization_barrier(jnp.mean(inputs, -1, keepdims=True))
    centred = inputs - average
    spread = lax.optimization_barrier(jnp.mean(centred * centred, -1, keepdims=True))
    return centred * lax.rsqrt(spread + EPSILON) * gain_vec + bias_vec

def product(left_side, right_side):
    return jnp.matmul(left_side, right_side, precision=FULL_PRECISION)

def block_forward(block_rows, segments, weights):
    ln1_gain, ln1_bias, qkv_weight, qkv_bias, out_weight, out_bias, ln2_gain, ln2_bias, fc1_weight, fc1_bias, fc2_weight, fc2_bias = weights
    number = block_rows.shape[0]
    normed = low(layer_norm(block_rows, ln1_gain, ln1_bias))
    packed = low(low_back(product(normed, qkv_weight) + qkv_bias))
    queries = packed[..., :D].reshape(number, LENGTH, HEADS, HEAD)
    key_rows = packed[..., D:2 * D].reshape(number, LENGTH, HEADS, HEAD)
    value_rows = packed[..., 2 * D:].reshape(number, LENGTH, HEADS, HEAD)
    scores = low_back(jnp.einsum('slhe,smhe->shlm', queries, key_rows, precision=FULL_PRECISION) * HEAD ** (-0.5))
    position = jnp.arange(LENGTH, dtype=jnp.int32)
    allowed = (segments[:, :, None] == segments[:, None, :]) & (position[None, :, None] >= position[None, None, :])
    allowed = allowed[:, None]
    magnitude = jnp.sqrt(scores * scores + 1.0)
    row_max = lax.optimization_barrier(jnp.max(jnp.where(allowed, magnitude, -1e+30), -1, keepdims=True))
    raised = jnp.where(allowed, jnp.exp(magnitude - row_max), 0.0)
    attention = low(scores / magnitude * (raised / lax.optimization_barrier(jnp.sum(raised, -1, keepdims=True))))
    mixture = jnp.einsum('shlm,smhe->slhe', attention, value_rows, precision=FULL_PRECISION).reshape(number, LENGTH, D)
    mixture = low(low_back(mixture))
    middle = block_rows + low_back(product(mixture, out_weight)) + out_bias
    normed_two = low(layer_norm(middle, ln2_gain, ln2_bias))
    hidden = low(jax.nn.gelu(low_back(product(normed_two, fc1_weight) + fc1_bias)))
    return middle + low_back(product(hidden, fc2_weight)) + fc2_bias

def reference(tokens, segment_ids, ln1_gain, ln1_bias, qkv_weight, qkv_bias, out_weight, out_bias, ln2_gain, ln2_bias, fc1_weight, fc1_bias, fc2_weight, fc2_bias, output_grad):
    weights = tuple((tensor.astype(jnp.float32) for tensor in (ln1_gain, ln1_bias, qkv_weight, qkv_bias, out_weight, out_bias, ln2_gain, ln2_bias, fc1_weight, fc1_bias, fc2_weight, fc2_bias)))
    bundle = math.gcd(SEQS, max(1, 2048 // LENGTH))
    segments = segment_ids.reshape(SEQS // bundle, bundle, LENGTH)

    def forward(all_rows, params):
        blocks = all_rows.reshape(SEQS // bundle, bundle, LENGTH, D)

        def advance(carried, inputs):
            return (carried, jax.checkpoint(block_forward)(inputs[0], inputs[1], params))
        result_rows = lax.scan(advance, jnp.zeros((), jnp.float32), (blocks, segments))[1]
        return result_rows.reshape(TOKENS, D)
    result, pullback = jax.vjp(forward, tokens.astype(jnp.float32), weights)
    grad_rows, gradients = pullback(output_grad.astype(jnp.float32))
    return (result.astype(jnp.bfloat16), grad_rows, gradients[0], gradients[1], gradients[2], gradients[3], gradients[4], gradients[5], gradients[6], gradients[7], gradients[8], gradients[9], gradients[10], gradients[11])
```

```python
import functools

import jax
import jax.numpy as jnp
from jax import lax
from jax.experimental import pallas as pl
from jax.experimental.pallas import tpu as pltpu
from jax.sharding import Mesh, PartitionSpec as P

D = 768
HEAD = 64
PAIR = 2 * HEAD
EPSILON = 1e-05
NEG = -1e30
TILE = 256
BF = jnp.bfloat16
F32 = jnp.float32
MIB = 1 << 20


def nn(a, b):
    return jnp.dot(a, b, preferred_element_type=F32)


def nt(a, b):
    return lax.dot_general(a, b, (((1,), (1,)), ((), ())), preferred_element_type=F32)


def tn(a, b):
    return lax.dot_general(a, b, (((0,), (0,)), ((), ())), preferred_element_type=F32)


def normalise(rows):
    average = jnp.mean(rows, -1, keepdims=True)
    centred = rows - average
    inverse = lax.rsqrt(jnp.mean(centred * centred, -1, keepdims=True) + EPSILON)
    return centred * inverse, inverse


def norm_grad(grad, hat, inverse, gain):
    scaled = grad * gain
    return inverse * (
        scaled
        - jnp.mean(scaled, -1, keepdims=True)
        - hat * jnp.mean(scaled * hat, -1, keepdims=True)
    )


def total(rows):
    return jnp.sum(rows, 0, keepdims=True)


def project_kernel(place_ref, own_ref, other_ref, gain_ref, shift_ref, weight_ref, bias_ref, normed_ref, qkv_ref):
    mine = (pl.program_id(0) // 2) == place_ref[0]
    rows = jnp.where(mine, own_ref[...].astype(F32), other_ref[...].astype(F32))
    hat, _ = normalise(rows)
    normed = (hat * gain_ref[...] + shift_ref[...]).astype(BF)
    normed_ref[...] = normed
    qkv_ref[...] = (nn(normed, weight_ref[...]) + bias_ref[...]).astype(BF)


def project(place, own, other, gain, shift, weight, bias):
    rows, width = own.shape
    columns = weight.shape[1]
    step = rows // 2
    half = pl.BlockSpec((step, width), lambda i, s: (i % 2, 0))
    fixed = lambda r, c: pl.BlockSpec((r, c), lambda i, s: (0, 0))
    return pl.pallas_call(
        project_kernel,
        grid_spec=pltpu.PrefetchScalarGridSpec(
            num_scalar_prefetch=1,
            grid=(4,),
            in_specs=[half, half, fixed(1, width), fixed(1, width), fixed(width, columns), fixed(1, columns)],
            out_specs=[
                pl.BlockSpec((step, width), lambda i, s: (i, 0)),
                pl.BlockSpec((step, columns), lambda i, s: (i, 0)),
            ],
        ),
        out_shape=[
            jax.ShapeDtypeStruct((2 * rows, width), BF),
            jax.ShapeDtypeStruct((2 * rows, columns), BF),
        ],
        compiler_params=pltpu.CompilerParams(vmem_limit_bytes=48 * MIB),
        cost_estimate=pl.CostEstimate(
            flops=4 * rows * width * columns, bytes_accessed=8 * MIB, transcendentals=0
        ),
        name="norm_and_qkv",
    )(place, own, other, gain, shift, weight, bias)


def forward_kernel(q_ref, k_ref, v_ref, first_ref, o_ref, lse_ref, mag_buf, sign_buf):
    count = q_ref.shape[0] // TILE
    lane = lax.broadcasted_iota(jnp.int32, (1, PAIR), 1)
    values = jnp.transpose(v_ref[...].astype(F32)).astype(BF)
    key_at = lax.broadcasted_iota(jnp.int32, (TILE, TILE), 0)
    causal = key_at <= lax.broadcasted_iota(jnp.int32, (TILE, TILE), 1)
    for j in range(count):
        qs = slice(j * TILE, (j + 1) * TILE)
        q = q_ref[qs, :] * BF(HEAD**-0.5)
        first = first_ref[:, qs]
        heads = []
        for h in range(2):
            qh = jnp.where((lane >= HEAD) == (h == 1), q, BF(0))
            top = None
            for i in range(j + 1):
                ks = slice(i * TILE, (i + 1) * TILE)
                s = nt(k_ref[ks, :], qh)
                square = s * s + 1.0
                inverse = lax.rsqrt(square)
                allowed = key_at + i * TILE >= first
                if i == j:
                    allowed = allowed & causal
                mag = jnp.where(allowed, square * inverse, NEG)
                mag_buf[h, ks, :] = mag
                sign_buf[h, ks, :] = s * inverse
                best = jnp.max(mag, 0, keepdims=True)
                top = best if top is None else jnp.maximum(top, best)
            weight_sum = jnp.zeros((1, TILE), F32)
            mixture = jnp.zeros((HEAD, TILE), F32)
            for i in range(j + 1):
                ks = slice(i * TILE, (i + 1) * TILE)
                raised = jnp.exp(mag_buf[h, ks, :] - top)
                weight_sum = weight_sum + total(raised)
                mixture = mixture + nn(
                    values[h * HEAD : (h + 1) * HEAD, ks], (sign_buf[h, ks, :] * raised).astype(BF)
                )
            heads.append(mixture * (1.0 / weight_sum))
            lse_ref[0, h : h + 1, qs] = top + jnp.log(weight_sum)
        o_ref[qs, :] = jnp.transpose(jnp.concatenate(heads, 0)).astype(BF)


def attend(qkv, firsts):
    length, columns = qkv.shape
    pairs = columns // 3 // PAIR
    block = lambda part: pl.BlockSpec((length, PAIR), lambda p: (0, part * pairs + p))
    return pl.pallas_call(
        forward_kernel,
        grid=(pairs,),
        in_specs=[block(0), block(1), block(2), pl.BlockSpec((1, length), lambda p: (0, 0))],
        out_specs=[block(0), pl.BlockSpec((1, 2, length), lambda p: (p, 0, 0))],
        out_shape=[
            jax.ShapeDtypeStruct((length, columns // 3), BF),
            jax.ShapeDtypeStruct((pairs, 2, length), F32),
        ],
        scratch_shapes=[pltpu.VMEM((2, length, TILE), F32)] * 2,
        compiler_params=pltpu.CompilerParams(vmem_limit_bytes=48 * MIB),
        cost_estimate=pl.CostEstimate(
            flops=12 * MIB * 1024, bytes_accessed=4 * MIB, transcendentals=0
        ),
        name="attention_forward",
    )(qkv, qkv, qkv, firsts)


def backward_kernel(
    q_ref, k_ref, v_ref, do_ref, lse_ref, first_ref, dq_ref, dk_ref, dv_ref, dk_sum, dv_sum, part_buf, weight_buf
):
    count = q_ref.shape[0] // TILE
    lane = lax.broadcasted_iota(jnp.int32, (1, PAIR), 1)
    keys = jnp.transpose(k_ref[...].astype(F32)).astype(BF)
    key_at = lax.broadcasted_iota(jnp.int32, (TILE, TILE), 0)
    causal = key_at <= lax.broadcasted_iota(jnp.int32, (TILE, TILE), 1)
    for j in range(count):
        qs = slice(j * TILE, (j + 1) * TILE)
        q = q_ref[qs, :] * BF(HEAD**-0.5)
        do = do_ref[qs, :]
        first = first_ref[:, qs]
        heads = []
        for h in range(2):
            chosen = (lane >= HEAD) == (h == 1)
            qh = jnp.where(chosen, q, BF(0))
            doh = jnp.where(chosen, do, BF(0))
            lse = lse_ref[0, h : h + 1, qs]
            centre = jnp.zeros((1, TILE), F32)
            for i in range(j + 1):
                ks = slice(i * TILE, (i + 1) * TILE)
                s = nt(k_ref[ks, :], qh)
                dw = nt(v_ref[ks, :], doh)
                square = s * s + 1.0
                inverse = lax.rsqrt(square)
                allowed = key_at + i * TILE >= first
                if i == j:
                    allowed = allowed & causal
                p = jnp.exp(jnp.where(allowed, square * inverse - lse, NEG))
                w = s * inverse * p
                centre = centre + total(w * dw)
                part_buf[h, ks, :] = p * dw * (1.0 + inverse * inverse * (inverse - 1.0))
                weight_buf[h, ks, :] = w
                dv = nn(w.astype(BF), doh)
                if i == j and h == 0:
                    dv_sum[ks, :] = dv
                else:
                    dv_sum[ks, :] += dv
            dq = jnp.zeros((HEAD, TILE), F32)
            for i in range(j + 1):
                ks = slice(i * TILE, (i + 1) * TILE)
                ds = (part_buf[h, ks, :] - weight_buf[h, ks, :] * centre).astype(BF)
                dk = nn(ds, qh)
                if i == j and h == 0:
                    dk_sum[ks, :] = dk
                else:
                    dk_sum[ks, :] += dk
                dq = dq + nn(keys[h * HEAD : (h + 1) * HEAD, ks], ds)
            heads.append(dq)
        dq_ref[qs, :] = (jnp.transpose(jnp.concatenate(heads, 0)) * HEAD**-0.5).astype(BF)
    dk_ref[...] = dk_sum[...].astype(BF)
    dv_ref[...] = dv_sum[...].astype(BF)


def attend_back(qkv, do, lse, firsts):
    length, columns = qkv.shape
    pairs = columns // 3 // PAIR
    block = lambda part: pl.BlockSpec((length, PAIR), lambda p: (0, part * pairs + p))
    shape = jax.ShapeDtypeStruct((length, columns // 3), BF)
    return pl.pallas_call(
        backward_kernel,
        grid=(pairs,),
        in_specs=[
            block(0),
            block(1),
            block(2),
            block(0),
            pl.BlockSpec((1, 2, length), lambda p: (p, 0, 0)),
            pl.BlockSpec((1, length), lambda p: (0, 0)),
        ],
        out_specs=[block(0)] * 3,
        out_shape=[shape] * 3,
        scratch_shapes=[pltpu.VMEM((length, PAIR), F32)] * 2 + [pltpu.VMEM((2, length, TILE), F32)] * 2,
        compiler_params=pltpu.CompilerParams(vmem_limit_bytes=48 * MIB),
        cost_estimate=pl.CostEstimate(
            flops=24 * MIB * 1024, bytes_accessed=6 * MIB, transcendentals=0
        ),
        name="attention_backward",
    )(qkv, qkv, qkv, do, lse, firsts)


FF_STEP = 768
OUT_BIAS, GAIN, SHIFT, LAST_BIAS = range(4)
D_OUT_BIAS, D_GAIN, D_SHIFT, D_LAST_BIAS = range(4)


def middle_kernel(
    tok_ref, o_ref, g_ref, wo_ref, w1_ref, w2_ref, b1_ref, vec_ref,
    out_ref, dx_ref, do_ref, gone_ref, gtwo_ref, db1_ref, sums_ref,
    x_buf, h_buf, y_sum, dh_sum,
):
    step = pl.program_id(0)
    last = pl.num_programs(0) - 1

    @pl.when(step == 0)
    def _():
        x = tok_ref[...].astype(F32) + nn(o_ref[...], wo_ref[...]) + vec_ref[OUT_BIAS : OUT_BIAS + 1, :]
        x_buf[...] = x
        hat, _ = normalise(x)
        h_buf[...] = (hat * vec_ref[GAIN : GAIN + 1, :] + vec_ref[SHIFT : SHIFT + 1, :]).astype(BF)
        y_sum[...] = jnp.zeros_like(y_sum)
        dh_sum[...] = jnp.zeros_like(dh_sum)

    @pl.when(step < last)
    def _():
        h = h_buf[...]
        g = g_ref[...]
        u = nn(h, w1_ref[...]) + b1_ref[...]
        root = 0.7978845608028654
        u2 = u * u
        bent = jnp.tanh(root * u * (1.0 + 0.044715 * u2))
        a = (0.5 * u * (1.0 + bent)).astype(BF)
        slope = 0.5 * (1.0 + bent) + 0.5 * u * (1.0 - bent * bent) * (root * (1.0 + 0.134145 * u2))
        y_sum[...] += nn(a, w2_ref[...])
        du = (nt(g, w2_ref[...]) * slope).astype(BF)
        db1_ref[...] = total(du.astype(F32))
        dh_sum[...] += nt(du, w1_ref[...])
        gone_ref[...] = tn(h, du).astype(BF)
        gtwo_ref[...] = tn(a, g).astype(BF)

    @pl.when(step == last)
    def _():
        x = x_buf[...]
        g = g_ref[...].astype(F32)
        out_ref[...] = (x + y_sum[...] + vec_ref[LAST_BIAS : LAST_BIAS + 1, :]).astype(BF)
        hat, inverse = normalise(x)
        dh = dh_sum[...]
        dx = g + norm_grad(dh, hat, inverse, vec_ref[GAIN : GAIN + 1, :])
        dx_ref[...] = dx
        dxr = dx.astype(BF)
        do_ref[...] = nt(dxr, wo_ref[...]).astype(BF)
        gone_ref[...] = tn(o_ref[...], dxr).astype(BF)
        sums_ref[...] = jnp.zeros_like(sums_ref)
        sums_ref[D_OUT_BIAS : D_OUT_BIAS + 1, :] = total(dx)
        sums_ref[D_GAIN : D_GAIN + 1, :] = total(dh * hat)
        sums_ref[D_SHIFT : D_SHIFT + 1, :] = total(dh)
        sums_ref[D_LAST_BIAS : D_LAST_BIAS + 1, :] = total(g)


def middle(tokens, mixture, grad, wo, w1, w2, b1, vectors):
    rows, width = tokens.shape
    hidden = w1.shape[1]
    steps = hidden // FF_STEP
    fixed = lambda r, c: pl.BlockSpec((r, c), lambda i: (0, 0))
    across = lambda r: pl.BlockSpec((r, FF_STEP), lambda i: (0, jnp.minimum(i, steps - 1)))
    down = pl.BlockSpec((FF_STEP, width), lambda i: (jnp.minimum(i, steps - 1), 0))
    return pl.pallas_call(
        middle_kernel,
        grid=(steps + 1,),
        in_specs=[
            fixed(rows, width), fixed(rows, width), fixed(rows, width), fixed(width, width),
            across(width), down, across(1), fixed(*vectors.shape),
        ],
        out_specs=[
            fixed(rows, width), fixed(rows, width), fixed(rows, width),
            pl.BlockSpec((width, FF_STEP), lambda i: (0, i)), down, across(1), fixed(8, width),
        ],
        out_shape=[
            jax.ShapeDtypeStruct((rows, width), BF),
            jax.ShapeDtypeStruct((rows, width), F32),
            jax.ShapeDtypeStruct((rows, width), BF),
            jax.ShapeDtypeStruct((width, hidden + FF_STEP), BF),
            jax.ShapeDtypeStruct((hidden, width), BF),
            jax.ShapeDtypeStruct((1, hidden), F32),
            jax.ShapeDtypeStruct((8, width), F32),
        ],
        scratch_shapes=[
            pltpu.VMEM((rows, width), F32),
            pltpu.VMEM((rows, width), BF),
            pltpu.VMEM((rows, width), F32),
            pltpu.VMEM((rows, width), F32),
        ],
        compiler_params=pltpu.CompilerParams(vmem_limit_bytes=56 * MIB),
        cost_estimate=pl.CostEstimate(
            flops=12 * rows * width * (hidden + width // 2), bytes_accessed=30 * MIB, transcendentals=0
        ),
        name="feed_forward_both_ways",
    )(tokens, mixture, grad, wo, w1, w2, b1, vectors)


def unproject_kernel(
    place_ref, own_ref, other_ref, dq_ref, dk_ref, dv_ref, weight_ref, keep_ref, send_ref, sums_ref, bias_ref
):
    step = pl.program_id(0)
    mine = (step // 2) == place_ref[0]
    rows = jnp.where(mine, own_ref[...].astype(F32), other_ref[...].astype(F32))
    hat, _ = normalise(rows)
    third = dq_ref.shape[1]
    grad = nt(dq_ref[...], weight_ref[:, :third])
    grad = grad + nt(dk_ref[...], weight_ref[:, third : 2 * third])
    grad = grad + nt(dv_ref[...], weight_ref[:, 2 * third :])

    @pl.when(step == 0)
    def _():
        sums_ref[...] = jnp.zeros_like(sums_ref)
        bias_ref[...] = jnp.zeros_like(bias_ref)

    sums_ref[0:1, :] += total(grad * hat)
    sums_ref[1:2, :] += total(grad)
    bias_ref[0:1, :] += total(dq_ref[...].astype(F32))
    bias_ref[1:2, :] += total(dk_ref[...].astype(F32))
    bias_ref[2:3, :] += total(dv_ref[...].astype(F32))

    @pl.when(mine)
    def _():
        keep_ref[...] = grad

    @pl.when(jnp.logical_not(mine))
    def _():
        send_ref[...] = grad.astype(BF)


def unproject(place, own, other, dq, dk, dv, weight):
    rows, width = own.shape
    third = dq.shape[1]
    step = rows // 2
    half = pl.BlockSpec((step, width), lambda i, s: (i % 2, 0))
    part = pl.BlockSpec((step, third), lambda i, s: (i, 0))
    fixed = lambda r, c: pl.BlockSpec((r, c), lambda i, s: (0, 0))
    return pl.pallas_call(
        unproject_kernel,
        grid_spec=pltpu.PrefetchScalarGridSpec(
            num_scalar_prefetch=1,
            grid=(4,),
            in_specs=[half, half, part, part, part, fixed(*weight.shape)],
            out_specs=[
                pl.BlockSpec((step, width), lambda i, s: (jnp.clip(i - 2 * s[0], 0, 1), 0)),
                pl.BlockSpec((step, width), lambda i, s: (jnp.clip(i - 2 * (1 - s[0]), 0, 1), 0)),
                fixed(8, width),
                fixed(8, third),
            ],
        ),
        out_shape=[
            jax.ShapeDtypeStruct((rows, width), F32),
            jax.ShapeDtypeStruct((rows, width), BF),
            jax.ShapeDtypeStruct((8, width), F32),
            jax.ShapeDtypeStruct((8, third), F32),
        ],
        compiler_params=pltpu.CompilerParams(vmem_limit_bytes=48 * MIB),
        cost_estimate=pl.CostEstimate(
            flops=12 * rows * width * third, bytes_accessed=10 * MIB, transcendentals=0
        ),
        name="grad_at_first_norm",
    )(place, own, other, dq, dk, dv, weight)


def swap(block, axis):
    return lax.ppermute(block, axis, [(0, 1), (1, 0)])


def on_device(
    tokens, segment_ids, ln1_gain, ln1_bias, qkv_weight, qkv_bias, out_weight, out_bias,
    ln2_gain, ln2_bias, fc1_weight, fc1_bias, fc2_weight, fc2_bias, output_grad,
):
    outer, inner = lax.axis_size("outer"), lax.axis_size("inner")
    core, side = lax.axis_index("core"), lax.axis_index("side")
    everyone = ("outer", "core", "inner", "side")
    chips = ("outer", "inner", "side")
    rows = tokens.shape[0]
    share = qkv_weight.shape[0]
    place = side.astype(jnp.int32).reshape(1)

    other = swap(tokens, "side")
    other_marks = swap(segment_ids, "side")
    marks = jnp.where(
        side == 0,
        jnp.concatenate([segment_ids, other_marks]),
        jnp.concatenate([other_marks, segment_ids]),
    )
    firsts = sum(jnp.where(marks > v, jnp.sum(marks == v), 0) for v in range(3))
    firsts = firsts.astype(jnp.int32)[None, :]

    parts = qkv_weight.reshape(share, 3, 2, D // 2).transpose(2, 0, 1, 3).reshape(2, share, 3 * D // 2)
    vectors = jnp.concatenate(
        [
            v.reshape(share, -1)
            for v in (ln1_gain, ln1_bias, qkv_bias, out_bias, ln2_gain, ln2_bias, fc1_bias, fc2_bias)
        ],
        1,
    )
    vectors = jnp.pad(vectors, ((0, 0), (0, 128 - vectors.shape[1])))
    parts = jnp.concatenate([parts, jnp.broadcast_to(vectors, (2, share, 128))], 2)
    parts = parts.reshape(2, share, 2, 5 * 128).transpose(2, 0, 1, 3)
    parts = jnp.broadcast_to(parts[None, :, None], (outer, 2, inner, 2, share, 5 * 128))
    got = lax.all_to_all(
        parts.reshape(outer * inner * 4, share, 5 * 128), everyone, split_axis=0, concat_axis=0, tiled=True
    ).reshape(D, 5 * 128)
    twin = swap(got, "core")
    packed = jnp.where(core == 0, jnp.concatenate([got, twin], 1), jnp.concatenate([twin, got], 1))
    w_qkv = packed[:, : 9 * 128]
    table = packed[:, 9 * 128 :].astype(F32)
    column = lambda i: table[:, i][None, :]
    qkv_bias_all = table[:, 2:5].reshape(3, 2, D // 2)
    qkv_bias_mine = lax.dynamic_index_in_dim(qkv_bias_all, side, 1, keepdims=False).reshape(1, -1)
    b1 = table[:, 8:12].reshape(1, -1)
    mid_vectors = jnp.concatenate([column(5), column(6), column(7), column(12)], 0)

    wide = lax.all_gather(jnp.concatenate([fc1_weight, out_weight], 1), everyone, axis=0, tiled=True)
    w2 = lax.all_gather(fc2_weight, everyone, axis=0, tiled=True)
    w1, wo = wide[:, : fc1_weight.shape[1]], wide[:, fc1_weight.shape[1] :]

    normed, qkv = project(place, tokens, other, column(0), column(1), w_qkv, qkv_bias_mine)
    mixed, lse = attend(qkv, firsts)
    theirs = lax.dynamic_slice_in_dim(mixed, (1 - side) * rows, rows, 0)
    mine = lax.dynamic_slice_in_dim(mixed, side * rows, rows, 0)
    theirs = swap(theirs, "side")
    mixture = jnp.where(side == 0, jnp.concatenate([mine, theirs], 1), jnp.concatenate([theirs, mine], 1))

    output, dx1, do, grad_wide, grad_two, db1, sums = middle(
        tokens, mixture, output_grad, wo, w1, w2, b1, mid_vectors
    )

    half = D // 2
    do_mine = lax.dynamic_slice_in_dim(do, side * half, half, 1)
    do_theirs = swap(lax.dynamic_slice_in_dim(do, (1 - side) * half, half, 1), "side")
    do_all = jnp.where(side == 0, jnp.concatenate([do_mine, do_theirs]), jnp.concatenate([do_theirs, do_mine]))

    def reduce_rows(grad):
        width = grad.shape[1]
        pieces = grad.reshape(outer, 2, inner * 2, grad.shape[0] // (4 * outer * inner), width)
        keep = lax.dynamic_index_in_dim(pieces, core, 1, keepdims=False)
        send = lax.dynamic_index_in_dim(pieces, 1 - core, 1, keepdims=False)
        both = (keep.astype(F32) + swap(send, "core").astype(F32)).astype(BF)
        both = both.reshape((outer * inner * 2,) + both.shape[2:])
        return lax.all_to_all(both, chips, split_axis=0, concat_axis=0, tiled=True)

    wide_total = jnp.sum(reduce_rows(grad_wide).astype(F32), 0)
    two_total = jnp.sum(reduce_rows(grad_two).astype(F32), 0)

    dq, dk, dv = attend_back(qkv, do_all, lse, firsts)
    kept, sent, first_sums, bias_sums = unproject(place, tokens, other, dq, dk, dv, w_qkv)
    back = swap(sent, "side")
    grad_qkv = jnp.concatenate([tn(normed, d).astype(BF) for d in (dq, dk, dv)], 1)
    bias_mine = jnp.zeros((3, 2, half), F32)
    bias_mine = lax.dynamic_update_slice(bias_mine, bias_sums[:3][:, None], (0, side, 0)).reshape(-1)
    small = jnp.concatenate(
        [
            v.reshape(D, -1)
            for v in (
                first_sums[0], first_sums[1], bias_mine, sums[D_OUT_BIAS], sums[D_GAIN],
                sums[D_SHIFT], db1, sums[D_LAST_BIAS],
            )
        ],
        1,
    )
    small = jnp.pad(small, ((0, 0), (0, 128 - small.shape[1]))).astype(BF)
    tail = reduce_rows(jnp.concatenate([grad_qkv, small], 1)).astype(F32)
    tail = tail.reshape(outer * inner, 2, share, 10 * 128)
    qkv_total = jnp.sum(tail[..., : 9 * 128], 0).reshape(2, share, 3, half)
    qkv_total = qkv_total.transpose(1, 2, 0, 3).reshape(share, 3 * D)
    small_total = jnp.sum(tail[..., 9 * 128 :], (0, 1))
    pick = lambda i, n=1: small_total[:, i : i + n].reshape(-1)

    hat, inverse = normalise(tokens.astype(F32))
    input_grad = dx1 + norm_grad(kept + back.astype(F32), hat, inverse, column(0))
    hidden = fc1_weight.shape[1]
    return (
        output,
        input_grad,
        pick(0),
        pick(1),
        qkv_total,
        pick(2, 3),
        wide_total[:, hidden:],
        pick(5),
        pick(6),
        pick(7),
        wide_total[:, :hidden],
        pick(8, 4),
        two_total,
        pick(12),
    )


def solution(mesh):
    dp, fsdp = mesh.devices.shape
    finer = Mesh(
        mesh.devices.reshape(dp // 2, 2, fsdp // 2, 2), ("outer", "core", "inner", "side")
    )
    every = ("outer", "core", "inner", "side")
    vec, mat = P(every), P(every, None)
    return jax.shard_map(
        on_device,
        mesh=finer,
        in_specs=(mat, vec, vec, vec, mat, vec, mat, vec, vec, vec, mat, vec, mat, vec, mat),
        out_specs=(mat, mat, vec, vec, mat, vec, mat, vec, vec, vec, mat, vec, mat, vec),
        check_vma=False,
    )
```

```python
import functools

import jax
import jax.numpy as jnp
import numpy as np
from jax import lax
from jax.experimental import pallas as pl
from jax.experimental.pallas import tpu as pltpu
from jax.sharding import Mesh, PartitionSpec as P

D = 768
HEAD = 64
PAIR = 2 * HEAD
EPSILON = 1e-05
NEG = -1e30
TILE = 256
BF = jnp.bfloat16
F32 = jnp.float32
MIB = 1 << 20


def nn(a, b):
    return jnp.dot(a, b, preferred_element_type=F32)


def nt(a, b):
    return lax.dot_general(a, b, (((1,), (1,)), ((), ())), preferred_element_type=F32)


def tn(a, b):
    return lax.dot_general(a, b, (((0,), (0,)), ((), ())), preferred_element_type=F32)


def normalise(rows):
    average = jnp.mean(rows, -1, keepdims=True)
    centred = rows - average
    inverse = lax.rsqrt(jnp.mean(centred * centred, -1, keepdims=True) + EPSILON)
    return centred * inverse, inverse


def norm_grad(grad, hat, inverse, gain):
    scaled = grad * gain
    return inverse * (
        scaled
        - jnp.mean(scaled, -1, keepdims=True)
        - hat * jnp.mean(scaled * hat, -1, keepdims=True)
    )


def total(rows):
    return jnp.sum(rows, 0, keepdims=True)


def project_kernel(place_ref, own_ref, other_ref, gain_ref, shift_ref, weight_ref, bias_ref, normed_ref, qkv_ref):
    mine = (pl.program_id(0) // 2) == place_ref[0]
    rows = jnp.where(mine, own_ref[...].astype(F32), other_ref[...].astype(F32))
    hat, _ = normalise(rows)
    normed = (hat * gain_ref[...] + shift_ref[...]).astype(BF)
    normed_ref[...] = normed
    qkv_ref[...] = (nn(normed, weight_ref[...]) + bias_ref[...]).astype(BF)


def project(place, own, other, gain, shift, weight, bias):
    rows, width = own.shape
    columns = weight.shape[1]
    step = rows // 2
    half = pl.BlockSpec((step, width), lambda i, s: (i % 2, 0))
    fixed = lambda r, c: pl.BlockSpec((r, c), lambda i, s: (0, 0))
    return pl.pallas_call(
        project_kernel,
        grid_spec=pltpu.PrefetchScalarGridSpec(
            num_scalar_prefetch=1,
            grid=(4,),
            in_specs=[half, half, fixed(1, width), fixed(1, width), fixed(width, columns), fixed(1, columns)],
            out_specs=[
                pl.BlockSpec((step, width), lambda i, s: (i, 0)),
                pl.BlockSpec((step, columns), lambda i, s: (i, 0)),
            ],
        ),
        out_shape=[
            jax.ShapeDtypeStruct((2 * rows, width), BF),
            jax.ShapeDtypeStruct((2 * rows, columns), BF),
        ],
        compiler_params=pltpu.CompilerParams(vmem_limit_bytes=60 * MIB),
        cost_estimate=pl.CostEstimate(
            flops=4 * rows * width * columns, bytes_accessed=8 * MIB, transcendentals=0
        ),
        name="norm_and_qkv",
    )(place, own, other, gain, shift, weight, bias)


def forward_kernel(
    place_ref, q_ref, k_ref, v_ref, first_ref, keep_ref, send_ref, lse_ref, mag_buf, sign_buf, o_ref
):
    count = q_ref.shape[0] // TILE
    lane = lax.broadcasted_iota(jnp.int32, (1, PAIR), 1)
    values = jnp.transpose(v_ref[...].astype(F32)).astype(BF)
    key_at = lax.broadcasted_iota(jnp.int32, (TILE, TILE), 0)
    causal = key_at <= lax.broadcasted_iota(jnp.int32, (TILE, TILE), 1)
    for j in range(count):
        qs = slice(j * TILE, (j + 1) * TILE)
        q = q_ref[qs, :] * BF(HEAD**-0.5)
        first = first_ref[:, qs]
        heads = []
        for h in range(2):
            qh = jnp.where((lane >= HEAD) == (h == 1), q, BF(0))
            top = None
            for i in range(j + 1):
                ks = slice(i * TILE, (i + 1) * TILE)
                s = nt(k_ref[ks, :], qh)
                square = s * s + 1.0
                inverse = lax.rsqrt(square)
                allowed = key_at + i * TILE >= first
                if i == j:
                    allowed = allowed & causal
                mag = jnp.where(allowed, square * inverse, NEG)
                mag_buf[h, ks, :] = mag
                sign_buf[h, ks, :] = s * inverse
                best = jnp.max(mag, 0, keepdims=True)
                top = best if top is None else jnp.maximum(top, best)
            weight_sum = jnp.zeros((1, TILE), F32)
            mixture = jnp.zeros((HEAD, TILE), F32)
            for i in range(j + 1):
                ks = slice(i * TILE, (i + 1) * TILE)
                raised = jnp.exp(mag_buf[h, ks, :] - top)
                weight_sum = weight_sum + total(raised)
                mixture = mixture + nn(
                    values[h * HEAD : (h + 1) * HEAD, ks], (sign_buf[h, ks, :] * raised).astype(BF)
                )
            heads.append(mixture * (1.0 / weight_sum))
            lse_ref[0, h : h + 1, qs] = top + jnp.log(weight_sum)
        o_ref[qs, :] = jnp.transpose(jnp.concatenate(heads, 0)).astype(BF)
    rows = keep_ref.shape[0]
    keep_ref[...] = o_ref[pl.ds(pl.multiple_of(place_ref[0] * rows, rows), rows), :]
    send_ref[...] = o_ref[pl.ds(pl.multiple_of((1 - place_ref[0]) * rows, rows), rows), :]


def attend(place, qkv, firsts, start=0, stop=None):
    length, columns = qkv.shape
    pairs = columns // 3 // PAIR
    count = (pairs if stop is None else stop) - start
    block = lambda part: pl.BlockSpec((length, PAIR), lambda p, s: (0, part * pairs + start + p))
    half = pl.BlockSpec((length // 2, PAIR), lambda p, s: (0, p))
    return pl.pallas_call(
        forward_kernel,
        grid_spec=pltpu.PrefetchScalarGridSpec(
            num_scalar_prefetch=1,
            grid=(count,),
            in_specs=[block(0), block(1), block(2), pl.BlockSpec((1, length), lambda p, s: (0, 0))],
            out_specs=[half, half, pl.BlockSpec((1, 2, length), lambda p, s: (p, 0, 0))],
            scratch_shapes=[pltpu.VMEM((2, length, TILE), F32)] * 2 + [pltpu.VMEM((length, PAIR), BF)],
        ),
        out_shape=[
            jax.ShapeDtypeStruct((length // 2, count * PAIR), BF),
            jax.ShapeDtypeStruct((length // 2, count * PAIR), BF),
            jax.ShapeDtypeStruct((count, 2, length), F32),
        ],
        compiler_params=pltpu.CompilerParams(vmem_limit_bytes=60 * MIB),
        cost_estimate=pl.CostEstimate(
            flops=12 * MIB * 1024, bytes_accessed=4 * MIB, transcendentals=0
        ),
        name="attention_forward",
    )(place, qkv, qkv, qkv, firsts)


def backward_kernel(
    place_ref, q_ref, k_ref, v_ref, own_ref, got_ref, lse_ref, first_ref,
    dq_ref, dk_ref, dv_ref, dk_sum, dv_sum, part_buf, weight_buf, do_ref,
):
    rows = own_ref.shape[0]
    do_ref[pl.ds(pl.multiple_of(place_ref[0] * rows, rows), rows), :] = own_ref[...]
    do_ref[pl.ds(pl.multiple_of((1 - place_ref[0]) * rows, rows), rows), :] = got_ref[...]
    count = q_ref.shape[0] // TILE
    lane = lax.broadcasted_iota(jnp.int32, (1, PAIR), 1)
    keys = jnp.transpose(k_ref[...].astype(F32)).astype(BF)
    key_at = lax.broadcasted_iota(jnp.int32, (TILE, TILE), 0)
    causal = key_at <= lax.broadcasted_iota(jnp.int32, (TILE, TILE), 1)
    for j in range(count):
        qs = slice(j * TILE, (j + 1) * TILE)
        q = q_ref[qs, :] * BF(HEAD**-0.5)
        do = do_ref[qs, :]
        first = first_ref[:, qs]
        heads = []
        for h in range(2):
            chosen = (lane >= HEAD) == (h == 1)
            qh = jnp.where(chosen, q, BF(0))
            doh = jnp.where(chosen, do, BF(0))
            lse = lse_ref[0, h : h + 1, qs]
            centre = jnp.zeros((1, TILE), F32)
            for i in range(j + 1):
                ks = slice(i * TILE, (i + 1) * TILE)
                s = nt(k_ref[ks, :], qh)
                dw = nt(v_ref[ks, :], doh)
                square = s * s + 1.0
                inverse = lax.rsqrt(square)
                allowed = key_at + i * TILE >= first
                if i == j:
                    allowed = allowed & causal
                p = jnp.exp(jnp.where(allowed, square * inverse - lse, NEG))
                w = s * inverse * p
                centre = centre + total(w * dw)
                part_buf[h, ks, :] = p * dw * (1.0 + inverse * inverse * (inverse - 1.0))
                weight_buf[h, ks, :] = w
                dv = nn(w.astype(BF), doh)
                if i == j and h == 0:
                    dv_sum[ks, :] = dv
                else:
                    dv_sum[ks, :] += dv
            dq = jnp.zeros((HEAD, TILE), F32)
            for i in range(j + 1):
                ks = slice(i * TILE, (i + 1) * TILE)
                ds = (part_buf[h, ks, :] - weight_buf[h, ks, :] * centre).astype(BF)
                dk = nn(ds, qh)
                if i == j and h == 0:
                    dk_sum[ks, :] = dk
                else:
                    dk_sum[ks, :] += dk
                dq = dq + nn(keys[h * HEAD : (h + 1) * HEAD, ks], ds)
            heads.append(dq)
        dq_ref[qs, :] = (jnp.transpose(jnp.concatenate(heads, 0)) * HEAD**-0.5).astype(BF)
    dk_ref[...] = dk_sum[...].astype(BF)
    dv_ref[...] = dv_sum[...].astype(BF)


def attend_back(place, qkv, own, got, lse, firsts):
    length, columns = qkv.shape
    pairs = columns // 3 // PAIR
    block = lambda part: pl.BlockSpec((length, PAIR), lambda p, s: (0, part * pairs + p))
    half = pl.BlockSpec((length // 2, PAIR), lambda p, s: (0, p))
    shape = jax.ShapeDtypeStruct((length, columns // 3), BF)
    return pl.pallas_call(
        backward_kernel,
        grid_spec=pltpu.PrefetchScalarGridSpec(
            num_scalar_prefetch=1,
            grid=(pairs,),
            in_specs=[
                block(0),
                block(1),
                block(2),
                half,
                half,
                pl.BlockSpec((1, 2, length), lambda p, s: (p, 0, 0)),
                pl.BlockSpec((1, length), lambda p, s: (0, 0)),
            ],
            out_specs=[block(0)] * 3,
            scratch_shapes=[pltpu.VMEM((length, PAIR), F32)] * 2
            + [pltpu.VMEM((2, length, TILE), F32)] * 2
            + [pltpu.VMEM((length, PAIR), BF)],
        ),
        out_shape=[shape] * 3,
        compiler_params=pltpu.CompilerParams(vmem_limit_bytes=60 * MIB),
        cost_estimate=pl.CostEstimate(
            flops=24 * MIB * 1024, bytes_accessed=6 * MIB, transcendentals=0
        ),
        name="attention_backward",
    )(place, qkv, qkv, qkv, own, got, lse, firsts)


FF_STEP = 768
OUT_BIAS, GAIN, SHIFT, LAST_BIAS = range(4)
D_OUT_BIAS, D_GAIN, D_SHIFT, D_LAST_BIAS = range(4)


def middle_kernel(
    tok_ref, o_ref, g_ref, wo_ref, w1_ref, w2_ref, b1_ref, vec_ref,
    out_ref, dx_ref, do_ref, gone_ref, gtwo_ref, db1_ref, sums_ref,
    x_buf, h_buf, y_sum, dh_sum,
):
    step = pl.program_id(0)
    last = pl.num_programs(0) - 1

    @pl.when(step == 0)
    def _():
        x = tok_ref[...].astype(F32) + nn(o_ref[...], wo_ref[...]) + vec_ref[OUT_BIAS : OUT_BIAS + 1, :]
        x_buf[...] = x
        hat, _ = normalise(x)
        h_buf[...] = (hat * vec_ref[GAIN : GAIN + 1, :] + vec_ref[SHIFT : SHIFT + 1, :]).astype(BF)
        y_sum[...] = jnp.zeros_like(y_sum)
        dh_sum[...] = jnp.zeros_like(dh_sum)

    @pl.when(step < last)
    def _():
        h = h_buf[...]
        g = g_ref[...]
        u = nn(h, w1_ref[...]) + b1_ref[...]
        root = 0.7978845608028654
        u2 = u * u
        bent = jnp.tanh(root * u * (1.0 + 0.044715 * u2))
        a = (0.5 * u * (1.0 + bent)).astype(BF)
        slope = 0.5 * (1.0 + bent) + 0.5 * u * (1.0 - bent * bent) * (root * (1.0 + 0.134145 * u2))
        y_sum[...] += nn(a, w2_ref[...])
        du = (nt(g, w2_ref[...]) * slope).astype(BF)
        db1_ref[...] = total(du.astype(F32))
        dh_sum[...] += nt(du, w1_ref[...])
        gone_ref[...] = tn(h, du).astype(BF)
        gtwo_ref[...] = tn(a, g).astype(BF)

    @pl.when(step == last)
    def _():
        x = x_buf[...]
        g = g_ref[...].astype(F32)
        out_ref[...] = (x + y_sum[...] + vec_ref[LAST_BIAS : LAST_BIAS + 1, :]).astype(BF)
        hat, inverse = normalise(x)
        dh = dh_sum[...]
        dx = g + norm_grad(dh, hat, inverse, vec_ref[GAIN : GAIN + 1, :])
        dx_ref[...] = dx
        dxr = dx.astype(BF)
        do_ref[...] = nt(dxr, wo_ref[...]).astype(BF)
        gone_ref[...] = tn(o_ref[...], dxr).astype(BF)
        sums_ref[...] = jnp.zeros_like(sums_ref)
        sums_ref[D_OUT_BIAS : D_OUT_BIAS + 1, :] = total(dx)
        sums_ref[D_GAIN : D_GAIN + 1, :] = total(dh * hat)
        sums_ref[D_SHIFT : D_SHIFT + 1, :] = total(dh)
        sums_ref[D_LAST_BIAS : D_LAST_BIAS + 1, :] = total(g)


def middle(tokens, mixture, grad, wo, w1, w2, b1, vectors):
    rows, width = tokens.shape
    hidden = w1.shape[1]
    steps = hidden // FF_STEP
    fixed = lambda r, c: pl.BlockSpec((r, c), lambda i: (0, 0))
    across = lambda r: pl.BlockSpec((r, FF_STEP), lambda i: (0, jnp.minimum(i, steps - 1)))
    down = pl.BlockSpec((FF_STEP, width), lambda i: (jnp.minimum(i, steps - 1), 0))
    return pl.pallas_call(
        middle_kernel,
        grid=(steps + 1,),
        in_specs=[
            fixed(rows, width), fixed(rows, width), fixed(rows, width), fixed(width, width),
            across(width), down, across(1), fixed(*vectors.shape),
        ],
        out_specs=[
            fixed(rows, width), fixed(rows, width), fixed(rows, width),
            pl.BlockSpec((width, FF_STEP), lambda i: (0, i)), down, across(1), fixed(8, width),
        ],
        out_shape=[
            jax.ShapeDtypeStruct((rows, width), BF),
            jax.ShapeDtypeStruct((rows, width), F32),
            jax.ShapeDtypeStruct((rows, width), BF),
            jax.ShapeDtypeStruct((width, hidden + FF_STEP), BF),
            jax.ShapeDtypeStruct((hidden, width), BF),
            jax.ShapeDtypeStruct((1, hidden), F32),
            jax.ShapeDtypeStruct((8, width), F32),
        ],
        scratch_shapes=[
            pltpu.VMEM((rows, width), F32),
            pltpu.VMEM((rows, width), BF),
            pltpu.VMEM((rows, width), F32),
            pltpu.VMEM((rows, width), F32),
        ],
        compiler_params=pltpu.CompilerParams(vmem_limit_bytes=60 * MIB),
        cost_estimate=pl.CostEstimate(
            flops=12 * rows * width * (hidden + width // 2), bytes_accessed=30 * MIB, transcendentals=0
        ),
        name="feed_forward_both_ways",
    )(tokens, mixture, grad, wo, w1, w2, b1, vectors)


def unproject_kernel(
    place_ref, own_ref, other_ref, dq_ref, dk_ref, dv_ref, weight_ref, keep_ref, send_ref, sums_ref, bias_ref
):
    step = pl.program_id(0)
    mine = (step // 2) == place_ref[0]
    rows = jnp.where(mine, own_ref[...].astype(F32), other_ref[...].astype(F32))
    hat, _ = normalise(rows)
    third = dq_ref.shape[1]
    grad = nt(dq_ref[...], weight_ref[:, :third])
    grad = grad + nt(dk_ref[...], weight_ref[:, third : 2 * third])
    grad = grad + nt(dv_ref[...], weight_ref[:, 2 * third :])

    @pl.when(step == 0)
    def _():
        sums_ref[...] = jnp.zeros_like(sums_ref)
        bias_ref[...] = jnp.zeros_like(bias_ref)

    sums_ref[0:1, :] += total(grad * hat)
    sums_ref[1:2, :] += total(grad)
    bias_ref[0:1, :] += total(dq_ref[...].astype(F32))
    bias_ref[1:2, :] += total(dk_ref[...].astype(F32))
    bias_ref[2:3, :] += total(dv_ref[...].astype(F32))

    @pl.when(mine)
    def _():
        keep_ref[...] = grad

    @pl.when(jnp.logical_not(mine))
    def _():
        send_ref[...] = grad.astype(BF)


def unproject(place, own, other, dq, dk, dv, weight):
    rows, width = own.shape
    third = dq.shape[1]
    step = rows // 2
    half = pl.BlockSpec((step, width), lambda i, s: (i % 2, 0))
    part = pl.BlockSpec((step, third), lambda i, s: (i, 0))
    fixed = lambda r, c: pl.BlockSpec((r, c), lambda i, s: (0, 0))
    return pl.pallas_call(
        unproject_kernel,
        grid_spec=pltpu.PrefetchScalarGridSpec(
            num_scalar_prefetch=1,
            grid=(4,),
            in_specs=[half, half, part, part, part, fixed(*weight.shape)],
            out_specs=[
                pl.BlockSpec((step, width), lambda i, s: (jnp.clip(i - 2 * s[0], 0, 1), 0)),
                pl.BlockSpec((step, width), lambda i, s: (jnp.clip(i - 2 * (1 - s[0]), 0, 1), 0)),
                fixed(8, width),
                fixed(8, third),
            ],
        ),
        out_shape=[
            jax.ShapeDtypeStruct((rows, width), F32),
            jax.ShapeDtypeStruct((rows, width), BF),
            jax.ShapeDtypeStruct((8, width), F32),
            jax.ShapeDtypeStruct((8, third), F32),
        ],
        compiler_params=pltpu.CompilerParams(vmem_limit_bytes=60 * MIB),
        cost_estimate=pl.CostEstimate(
            flops=12 * rows * width * third, bytes_accessed=10 * MIB, transcendentals=0
        ),
        name="grad_at_first_norm",
    )(place, own, other, dq, dk, dv, weight)


def tie(*blocks):
    return lax.optimization_barrier(blocks)


def swap(block, axis):
    return lax.ppermute(block, axis, [(0, 1), (1, 0)])


def general_plan(
    tokens, segment_ids, ln1_gain, ln1_bias, qkv_weight, qkv_bias, out_weight, out_bias,
    ln2_gain, ln2_bias, fc1_weight, fc1_bias, fc2_weight, fc2_bias, output_grad,
):
    outer, inner = lax.axis_size("outer"), lax.axis_size("inner")
    core, side = lax.axis_index("core"), lax.axis_index("side")
    everyone = ("outer", "core", "inner", "side")
    chips = ("outer", "inner", "side")
    rows = tokens.shape[0]
    share = qkv_weight.shape[0]
    place = side.astype(jnp.int32).reshape(1)

    other = swap(tokens, "side")
    other_marks = swap(segment_ids, "side")
    marks = jnp.where(
        side == 0,
        jnp.concatenate([segment_ids, other_marks]),
        jnp.concatenate([other_marks, segment_ids]),
    )
    firsts = sum(jnp.where(marks > v, jnp.sum(marks == v), 0) for v in range(3))
    firsts = firsts.astype(jnp.int32)[None, :]

    parts = qkv_weight.reshape(share, 3, 2, D // 2).transpose(2, 0, 1, 3).reshape(2, share, 3 * D // 2)
    vectors = jnp.concatenate(
        [
            v.reshape(share, -1)
            for v in (ln1_gain, ln1_bias, qkv_bias, out_bias, ln2_gain, ln2_bias, fc1_bias, fc2_bias)
        ],
        1,
    )
    vectors = jnp.pad(vectors, ((0, 0), (0, 128 - vectors.shape[1])))
    parts = jnp.concatenate([parts, jnp.broadcast_to(vectors, (2, share, 128))], 2)
    parts = parts.reshape(2, share, 2, 5 * 128).transpose(2, 0, 1, 3)
    parts = jnp.broadcast_to(parts[None, :, None], (outer, 2, inner, 2, share, 5 * 128))
    got = lax.all_to_all(
        parts.reshape(outer * inner * 4, share, 5 * 128), everyone, split_axis=0, concat_axis=0, tiled=True
    ).reshape(D, 5 * 128)
    twin = swap(got, "core")
    packed = jnp.where(core == 0, jnp.concatenate([got, twin], 1), jnp.concatenate([twin, got], 1))
    w_qkv = packed[:, : 9 * 128]
    table = packed[:, 9 * 128 :].astype(F32)
    column = lambda i: table[:, i][None, :]
    qkv_bias_all = table[:, 2:5].reshape(3, 2, D // 2)
    qkv_bias_mine = lax.dynamic_index_in_dim(qkv_bias_all, side, 1, keepdims=False).reshape(1, -1)
    b1 = table[:, 8:12].reshape(1, -1)
    mid_vectors = jnp.concatenate([column(5), column(6), column(7), column(12)], 0)

    wide = lax.all_gather(jnp.concatenate([fc1_weight, out_weight], 1), everyone, axis=0, tiled=True)
    w2 = lax.all_gather(fc2_weight, everyone, axis=0, tiled=True)
    w1, wo = wide[:, : fc1_weight.shape[1]], wide[:, fc1_weight.shape[1] :]

    normed, qkv = project(place, tokens, other, column(0), column(1), w_qkv, qkv_bias_mine)
    mine, theirs, lse = attend(place, qkv, firsts)
    theirs = swap(theirs, "side")
    mixture = jnp.where(side == 0, jnp.concatenate([mine, theirs], 1), jnp.concatenate([theirs, mine], 1))

    output, dx1, do, grad_wide, grad_two, db1, sums = middle(
        tokens, mixture, output_grad, wo, w1, w2, b1, mid_vectors
    )

    half = D // 2
    do_mine = lax.dynamic_slice_in_dim(do, side * half, half, 1)
    do_theirs = swap(lax.dynamic_slice_in_dim(do, (1 - side) * half, half, 1), "side")

    def reduce_rows(grad):
        width = grad.shape[1]
        pieces = grad.reshape(outer, 2, inner * 2, grad.shape[0] // (4 * outer * inner), width)
        keep = lax.dynamic_index_in_dim(pieces, core, 1, keepdims=False)
        send = lax.dynamic_index_in_dim(pieces, 1 - core, 1, keepdims=False)
        both = (keep.astype(F32) + swap(send, "core").astype(F32)).astype(BF)
        both = both.reshape((outer * inner * 2,) + both.shape[2:])
        return lax.all_to_all(both, chips, split_axis=0, concat_axis=0, tiled=True)

    wide_total = jnp.sum(reduce_rows(grad_wide).astype(F32), 0)
    two_total = jnp.sum(reduce_rows(grad_two).astype(F32), 0)

    dq, dk, dv = attend_back(place, qkv, do_mine, do_theirs, lse, firsts)
    kept, sent, first_sums, bias_sums = unproject(place, tokens, other, dq, dk, dv, w_qkv)
    back = swap(sent, "side")
    grad_qkv = jnp.concatenate([tn(normed, d).astype(BF) for d in (dq, dk, dv)], 1)
    bias_mine = jnp.zeros((3, 2, half), F32)
    bias_mine = lax.dynamic_update_slice(bias_mine, bias_sums[:3][:, None], (0, side, 0)).reshape(-1)
    small = jnp.concatenate(
        [
            v.reshape(D, -1)
            for v in (
                first_sums[0], first_sums[1], bias_mine, sums[D_OUT_BIAS], sums[D_GAIN],
                sums[D_SHIFT], db1, sums[D_LAST_BIAS],
            )
        ],
        1,
    )
    small = jnp.pad(small, ((0, 0), (0, 128 - small.shape[1]))).astype(BF)
    tail = reduce_rows(jnp.concatenate([grad_qkv, small], 1)).astype(F32)
    tail = tail.reshape(outer * inner, 2, share, 10 * 128)
    qkv_total = jnp.sum(tail[..., : 9 * 128], 0).reshape(2, share, 3, half)
    qkv_total = qkv_total.transpose(1, 2, 0, 3).reshape(share, 3 * D)
    small_total = jnp.sum(tail[..., 9 * 128 :], (0, 1))
    pick = lambda i, n=1: small_total[:, i : i + n].reshape(-1)

    hat, inverse = normalise(tokens.astype(F32))
    input_grad = dx1 + norm_grad(kept + back.astype(F32), hat, inverse, column(0))
    hidden = fc1_weight.shape[1]
    return (
        output,
        input_grad,
        pick(0),
        pick(1),
        qkv_total,
        pick(2, 3),
        wide_total[:, hidden:],
        pick(5),
        pick(6),
        pick(7),
        wide_total[:, :hidden],
        pick(8, 4),
        two_total,
        pick(12),
    )


SHARE = 24
FF_SHARE = 96
FF_HALF = 8 * FF_SHARE


def pack_kernel(weight_ref, *refs):
    *vector_refs, out_ref, buf = refs
    half = D // 2
    buf[...] = jnp.zeros_like(buf)
    for i, ref in enumerate(vector_refs):
        buf[i : i + 1, : ref.shape[1]] = ref[...].astype(F32)
    vectors = buf[...].astype(BF)
    for x in range(2):
        q, k, v = (weight_ref[:, part * D + x * half : part * D + (x + 1) * half] for part in range(3))
        low = jnp.concatenate([q, k[:, :256]], 1)
        high = jnp.concatenate([k[:, 256:], v, vectors], 1)
        for y in range(2):
            for z in range(4):
                out_ref[((2 * y) * 4 + z) * 2 + x] = low
                out_ref[((2 * y + 1) * 4 + z) * 2 + x] = high


def pack(weight, vectors):
    share = weight.shape[0]
    return pl.pallas_call(
        pack_kernel,
        out_shape=jax.ShapeDtypeStruct((32, share, 640), BF),
        scratch_shapes=[pltpu.VMEM((share, 128), F32)],
        compiler_params=pltpu.CompilerParams(vmem_limit_bytes=60 * MIB),
        name="pack_qkv_weights",
    )(weight, *(v.reshape(1, -1) for v in vectors))


ALL_VECTORS = 8
GAIN_ONE, SHIFT_ONE, QKV_BIAS = 0, 1, 2


def spread(rows, where):
    lanes = lax.broadcasted_iota(jnp.int32, (128, where.shape[1]), 0)
    chosen = jnp.where(lanes == where[1:2, :], 1.0, 0.0).astype(BF)
    found = nn(rows.astype(BF), chosen)
    owners = lax.broadcasted_iota(jnp.int32, found.shape, 0)
    return total(jnp.where(owners == where[0:1, :], found, 0.0))


def places(each, numbers):
    numbers = np.asarray(numbers)
    return np.stack([numbers // each, numbers % each]).astype(np.int32)


def plane_project_kernel(
    ids_ref, own_ref, other_ref, got_ref, twin_ref, at_d_ref, at_qkv_ref, at_ff_ref,
    normed_ref, qkv_ref, weight_ref, vec_ref, b1_ref, table, bias,
):
    @pl.when(pl.program_id(0) == 0)
    def _():
        first = ids_ref[1] == 0
        got, twin = got_ref[...], twin_ref[...]
        weight_ref[:, :640] = jnp.where(first, got, twin)
        high = jnp.where(first, twin, got)
        weight_ref[:, 640:] = high[:, :512]
        table[...] = high[:, 512:].astype(F32)
        rows = lambda i: table[pl.ds(i, 32, stride=SHARE), :]
        bias[...] = spread(rows(QKV_BIAS), at_qkv_ref[0])
        vec_ref[...] = jnp.zeros_like(vec_ref)
        for to, i in enumerate((3, 4, 5, 7, 0, 1)):
            vec_ref[to : to + 1, :] = spread(rows(i), at_d_ref[...])
        b1_ref[...] = spread(rows(6), at_ff_ref[...])

    mine = (pl.program_id(0) // 2) == ids_ref[3]
    rows = jnp.where(mine, own_ref[...], other_ref[...]).astype(F32)
    hat, _ = normalise(rows)
    normed = (hat * vec_ref[4:5, :] + vec_ref[5:6, :]).astype(BF)
    normed_ref[...] = normed
    qkv_ref[...] = (nn(normed, weight_ref[...]) + bias[...]).astype(BF)


def plane_project(ids, own, other, got, twin):
    rows, width = own.shape
    columns = 3 * width // 2
    hidden = 4 * width
    step = rows // 2
    at_d = places(SHARE, range(width))
    at_ff = places(FF_SHARE, range(hidden))
    at_qkv = [
        places(3 * SHARE, [part * width + x * width // 2 + m for part in range(3) for m in range(width // 2)])
        for x in range(2)
    ]
    at_qkv = jnp.stack([jnp.asarray(a) for a in at_qkv])
    half = pl.BlockSpec((step, width), lambda i, s: (i % 2, 0))
    fixed = lambda r, c: pl.BlockSpec((r, c), lambda i, s: (0, 0))
    return pl.pallas_call(
        plane_project_kernel,
        grid_spec=pltpu.PrefetchScalarGridSpec(
            num_scalar_prefetch=1,
            grid=(4,),
            in_specs=[
                half, half, fixed(*got.shape), fixed(*got.shape), fixed(2, width),
                pl.BlockSpec((1, 2, columns), lambda i, s: (s[3], 0, 0)), fixed(2, hidden),
            ],
            out_specs=[
                pl.BlockSpec((step, width), lambda i, s: (i, 0)),
                pl.BlockSpec((step, columns), lambda i, s: (i, 0)),
                fixed(width, columns),
                fixed(8, width),
                fixed(1, hidden),
            ],
            scratch_shapes=[pltpu.VMEM((width, 128), F32), pltpu.VMEM((1, columns), F32)],
        ),
        out_shape=[
            jax.ShapeDtypeStruct((2 * rows, width), BF),
            jax.ShapeDtypeStruct((2 * rows, columns), BF),
            jax.ShapeDtypeStruct((width, columns), BF),
            jax.ShapeDtypeStruct((8, width), F32),
            jax.ShapeDtypeStruct((1, hidden), F32),
        ],
        compiler_params=pltpu.CompilerParams(vmem_limit_bytes=60 * MIB),
        cost_estimate=pl.CostEstimate(
            flops=4 * rows * width * columns, bytes_accessed=8 * MIB, transcendentals=0
        ),
        name="norm_and_qkv",
    )(ids, own, other, got, twin, jnp.asarray(at_d), at_qkv, jnp.asarray(at_ff))


def out_project_kernel(ids_ref, tok_ref, own_ref, got_ref, wo_own_ref, wo_got_ref, vec_ref, x_ref, h_ref):
    x = tok_ref[...].astype(F32) + nn(own_ref[...], wo_own_ref[...]) + nn(got_ref[...], wo_got_ref[...])
    x = x + vec_ref[OUT_BIAS : OUT_BIAS + 1, :]
    x_ref[...] = x
    hat, _ = normalise(x)
    h_ref[...] = (hat * vec_ref[GAIN : GAIN + 1, :] + vec_ref[SHIFT : SHIFT + 1, :]).astype(BF)


def out_project(ids, tokens, own, got, wide, vectors):
    rows, width = tokens.shape
    half = width // 2
    step = rows // 2
    tile = lambda c: pl.BlockSpec((step, c), lambda i, s: (i, 0))
    return pl.pallas_call(
        out_project_kernel,
        grid_spec=pltpu.PrefetchScalarGridSpec(
            num_scalar_prefetch=1,
            grid=(2,),
            in_specs=[
                tile(width), tile(half), tile(half),
                pl.BlockSpec((half, width), lambda i, s: (s[3], wide.shape[1] // width - 1)),
                pl.BlockSpec((half, width), lambda i, s: (1 - s[3], wide.shape[1] // width - 1)),
                pl.BlockSpec(vectors.shape, lambda i, s: (0, 0)),
            ],
            out_specs=[tile(width), tile(width)],
        ),
        out_shape=[jax.ShapeDtypeStruct((rows, width), F32), jax.ShapeDtypeStruct((rows, width), BF)],
        compiler_params=pltpu.CompilerParams(vmem_limit_bytes=60 * MIB),
        cost_estimate=pl.CostEstimate(flops=2 * rows * width * width, bytes_accessed=6 * MIB, transcendentals=0),
        name="out_projection_and_second_norm",
    )(ids, tokens, own, got, wide, wide, vectors)


def gelu_both(u):
    root = 0.7978845608028654
    u2 = u * u
    bent = jnp.tanh(root * u * (1.0 + 0.044715 * u2))
    a = 0.5 * u * (1.0 + bent)
    slope = 0.5 * (1.0 + bent) + 0.5 * u * (1.0 - bent * bent) * (root * (1.0 + 0.134145 * u2))
    return a.astype(BF), slope


def feed_forward_kernel(plane, ids_ref, *refs):
    h_own_hbm, h_sib_hbm, g_own_hbm, g_sib_hbm, wide_hbm, own_hbm, far_hbm, b1_ref, *refs = refs
    earlier, refs = (refs[:4], refs[4:]) if plane else ((), refs)
    outs, db1_ref, refs = refs[:8], refs[8], refs[9:]
    h_own, h_sib, g_own, g_sib, w1, own, far, w2, *refs = refs
    y_own, y_sib, dh_own, dh_sib, q00, q10, q01, q11, *refs = refs
    send_y, send_dh, in_sems, out_sems = refs if plane else (None, None, *refs)
    my_y, my_c, my_z, my_x = (ids_ref[i] for i in range(4))
    unit = FF_SHARE

    column = pl.multiple_of(((my_y ^ plane) * 2 + my_c) * FF_HALF, FF_HALF)
    sources = [
        (wide_hbm.at[:, pl.ds(column, FF_HALF)], w1), (h_own_hbm, h_own), (g_own_hbm, g_own), (own_hbm, own),
        (far_hbm, far), (h_sib_hbm, h_sib), (g_sib_hbm, g_sib),
    ] + list(zip(earlier, (y_own, dh_own, y_sib, dh_sib)))
    loads = [pltpu.make_async_copy(src, dst, in_sems.at[i]) for i, (src, dst) in enumerate(sources)]
    for load in loads:
        load.start()
    loads[0].wait()
    loads[1].wait()
    a_own, slope_own = gelu_both(nn(h_own[...], w1[...]) + b1_ref[...])
    for load in loads[2:5]:
        load.wait()
    for z in range(4):
        near, distant = own[z ^ my_z], far[z ^ my_z]
        w2[2 * z * unit : (2 * z + 1) * unit, :] = jnp.where(my_x == 0, near, distant)
        w2[(2 * z + 1) * unit : (2 * z + 2) * unit, :] = jnp.where(my_x == 0, distant, near)
    du_own = (nt(g_own[...], w2[...]) * slope_own).astype(BF)
    loads[5].wait()
    a_sib, slope_sib = gelu_both(nn(h_sib[...], w1[...]) + b1_ref[...])
    loads[6].wait()
    du_sib = (nt(g_sib[...], w2[...]) * slope_sib).astype(BF)
    db1_ref[...] = total(du_own.astype(F32)) + total(du_sib.astype(F32))

    stores = []

    def store(src, at):
        copy = pltpu.make_async_copy(src, outs[at], out_sems.at[at])
        copy.start()
        stores.append(copy)

    for load in loads[7:]:
        load.wait()
    for at, du, sums, sent in ((2, du_own, dh_own, None), (3, du_sib, dh_sib, send_dh)):
        dh = nt(du, w1[...])
        if plane:
            dh = dh + sums[...]
        if sent is None:
            sums[...] = dh
            store(sums, at)
        else:
            sent[...] = dh.astype(BF)
            store(sent, at)
    for at, a, sums, sent in ((0, a_own, y_own, None), (1, a_sib, y_sib, send_y)):
        y = nn(a, w2[...])
        if plane:
            y = y + sums[...]
        if sent is None:
            sums[...] = y
            store(sums, at)
        else:
            sent[...] = y.astype(BF)
            store(sent, at)

    two = (tn(a_own, g_own[...]) + tn(a_sib, g_sib[...])).astype(BF)
    one = tn(h_own[...], du_own) + tn(h_sib[...], du_sib)
    for xr, yr, ref, at in ((1, 0, q10, 5), (1, 1, q11, 7), (0, 1, q01, 6), (0, 0, q00, 4)):
        low_y, low_x = (my_y ^ yr) == 0, (my_x ^ xr) == 0
        stride = 2 * SHARE + (unit if yr == plane else 0)
        for z in range(4):
            parts = []
            for c in range(2):
                cut = lambda yy, xx: one[(((yy * 2 + c) * 4 + z) * 2 + xx) * SHARE :][:SHARE]
                parts.append(
                    jnp.where(low_y, jnp.where(low_x, cut(0, 0), cut(0, 1)), jnp.where(low_x, cut(1, 0), cut(1, 1)))
                )
            ref[z * stride : z * stride + 2 * SHARE, :] = jnp.concatenate(parts, 0).astype(BF)
            if yr == plane:
                cut = lambda xx: two[(z * 2 + xx) * unit :][:unit]
                ref[z * stride + 2 * SHARE : (z + 1) * stride, :] = jnp.where(low_x, cut(0), cut(1))
        store(ref, at)
    for copy in stores:
        copy.wait()


def feed_forward(ids, plane, h_own, h_sib, g_own, g_sib, wide, own, far, b1, earlier=()):
    rows, width = h_own.shape
    anywhere = pl.BlockSpec(memory_space=pl.ANY)
    shape = jax.ShapeDtypeStruct
    f32, bf = shape((rows, width), F32), shape((rows, width), BF)
    short, tall = shape((8 * SHARE, width), BF), shape((8 * SHARE + 4 * FF_SHARE, width), BF)
    pieces = [short, short, tall, tall] if plane else [tall, tall, short, short]
    mixed = [f32, bf, f32, bf] if plane else [f32] * 4
    held = lambda s: pltpu.VMEM(s.shape, s.dtype)
    scratch = [held(bf)] * 4
    scratch += [pltpu.VMEM((width, FF_HALF), BF), held(own), held(far), pltpu.VMEM((FF_HALF, width), BF)]
    scratch += [held(f32)] * 4 + [held(s) for s in pieces]
    scratch += [held(bf)] * 2 if plane else []
    scratch += [pltpu.SemaphoreType.DMA((11,)), pltpu.SemaphoreType.DMA((8,))]
    return pl.pallas_call(
        functools.partial(feed_forward_kernel, plane),
        grid_spec=pltpu.PrefetchScalarGridSpec(
            num_scalar_prefetch=1,
            grid=(1,),
            in_specs=[anywhere] * 7
            + [pl.BlockSpec((1, FF_HALF), lambda i, s: (0, (s[0] ^ plane) * 2 + s[1]))]
            + [anywhere] * len(earlier),
            out_specs=[anywhere] * 8 + [pl.BlockSpec((1, FF_HALF), lambda i, s: (0, 0))],
            scratch_shapes=scratch,
        ),
        out_shape=mixed + pieces + [shape((1, FF_HALF), F32)],
        compiler_params=pltpu.CompilerParams(vmem_limit_bytes=60 * MIB),
        cost_estimate=pl.CostEstimate(
            flops=24 * rows * width * FF_HALF, bytes_accessed=16 * MIB, transcendentals=0
        ),
        name=f"feed_forward_both_ways_{plane}",
    )(ids, h_own, h_sib, g_own, g_sib, wide, own, far, b1, *earlier)


def second_norm_kernel(
    ids_ref, x_ref, y_ref, y_got_ref, dh_ref, dh_got_ref, g_ref, o_own_ref, o_got_ref, wo_ref, vec_ref,
    out_ref, dx_ref, do_own_ref, do_send_ref, gwo_ref, sums_ref, own_sum, got_sum,
):
    step = pl.program_id(0)
    x = x_ref[...]
    g = g_ref[...].astype(F32)
    hat, inverse = normalise(x)
    dh = dh_ref[...] + dh_got_ref[...].astype(F32)
    dx = g + norm_grad(dh, hat, inverse, vec_ref[GAIN : GAIN + 1, :])
    dx_ref[...] = dx
    dxr = dx.astype(BF)
    half = wo_ref.shape[0] // 2
    mine = pl.ds(pl.multiple_of(ids_ref[3] * half, half), half)
    theirs = pl.ds(pl.multiple_of((1 - ids_ref[3]) * half, half), half)
    do_send_ref[...] = nt(dxr, wo_ref[theirs, :]).astype(BF)
    do_own_ref[...] = nt(dxr, wo_ref[mine, :]).astype(BF)
    out_ref[...] = (x + y_ref[...] + y_got_ref[...].astype(F32) + vec_ref[LAST_BIAS : LAST_BIAS + 1, :]).astype(BF)

    @pl.when(step == 0)
    def _():
        sums_ref[...] = jnp.zeros_like(sums_ref)
        own_sum[...] = jnp.zeros_like(own_sum)
        got_sum[...] = jnp.zeros_like(got_sum)

    own_sum[...] += tn(o_own_ref[...], dxr)
    got_sum[...] += tn(o_got_ref[...], dxr)
    sums_ref[D_OUT_BIAS : D_OUT_BIAS + 1, :] += total(dx)
    sums_ref[D_GAIN : D_GAIN + 1, :] += total(dh * hat)
    sums_ref[D_SHIFT : D_SHIFT + 1, :] += total(dh)
    sums_ref[D_LAST_BIAS : D_LAST_BIAS + 1, :] += total(g)

    @pl.when(step == pl.num_programs(0) - 1)
    def _():
        gwo_ref[mine, :] = own_sum[...].astype(BF)
        gwo_ref[theirs, :] = got_sum[...].astype(BF)


def second_norm_back(ids, x, y, y_got, dh, dh_got, g, o_own, o_got, wide, vectors):
    rows, width = x.shape
    step = rows // 2
    tile = lambda c: pl.BlockSpec((step, c), lambda i, s: (i, 0))
    fixed = lambda r, c: pl.BlockSpec((r, c), lambda i, s: (0, 0))
    shape = jax.ShapeDtypeStruct
    half = width // 2
    return pl.pallas_call(
        second_norm_kernel,
        grid_spec=pltpu.PrefetchScalarGridSpec(
            num_scalar_prefetch=1,
            grid=(2,),
            in_specs=[tile(width)] * 6
            + [tile(half)] * 2
            + [
                pl.BlockSpec((width, width), lambda i, s: (0, wide.shape[1] // width - 1)),
                fixed(*vectors.shape),
            ],
            out_specs=[tile(width), tile(width), tile(half), tile(half), fixed(width, width), fixed(8, width)],
            scratch_shapes=[pltpu.VMEM((half, width), F32)] * 2,
        ),
        out_shape=[
            shape((rows, width), BF), shape((rows, width), F32), shape((rows, half), BF),
            shape((rows, half), BF), shape((width, width), BF), shape((8, width), F32),
        ],
        compiler_params=pltpu.CompilerParams(vmem_limit_bytes=60 * MIB),
        cost_estimate=pl.CostEstimate(flops=4 * rows * width * width, bytes_accessed=14 * MIB, transcendentals=0),
        name="second_norm_back",
    )(ids, x, y, y_got, dh, dh_got, g, o_own, o_got, wide, vectors)


def qkv_weight_kernel(ids_ref, h_ref, dq_ref, dk_ref, dv_ref, weight_ref, vec_ref, keep_ref, send_ref):
    first = ids_ref[1] == 0
    width = h_ref.shape[1]
    block = width // 4
    third = dq_ref.shape[1]
    vectors = jnp.transpose(vec_ref[...])
    gain, shift = vectors[:, 4:5], vectors[:, 5:6]
    by_shift = jnp.zeros((width, 1), F32)
    by_gain = jnp.zeros((width, 1), F32)
    bias = [jnp.zeros((width, 1), F32) for _ in range(3)]
    place = lax.broadcasted_iota(jnp.int32, (width, third), 1) - 3 * lax.broadcasted_iota(jnp.int32, (width, third), 0)

    def put(full, columns):
        full = full.astype(BF)
        for y in range(2):
            low, high = full[2 * y * block :][:block], full[(2 * y + 1) * block :][:block]
            keep_ref[y * block : (y + 1) * block, columns] = jnp.where(first, low, high)
            send_ref[y * block : (y + 1) * block, columns] = jnp.where(first, high, low)

    for part, ref in enumerate((dq_ref, dk_ref, dv_ref)):
        full = tn(h_ref[...], ref[...])
        columns = slice(part * third, (part + 1) * third)
        put(full, columns)
        weight = weight_ref[:, columns].astype(F32)
        sums = total(ref[...].astype(F32))
        by_gain = by_gain + jnp.sum(weight * full, 1, keepdims=True)
        by_shift = by_shift + jnp.sum(weight * sums, 1, keepdims=True)
        start = part * width + ids_ref[3] * third
        for j in range(3):
            chosen = jnp.where(place == j - start, sums, 0.0)
            bias[j] = bias[j] + jnp.sum(chosen, 1, keepdims=True)
    by_gain = (by_gain - shift * by_shift) / gain
    lane = lax.broadcasted_iota(jnp.int32, (width, 128), 1)
    table = jnp.zeros((width, 128), F32)
    for i, column in enumerate((by_gain, by_shift, *bias)):
        table = table + jnp.where(lane == i, column, 0.0)
    put(table, slice(3 * third, 3 * third + 128))


def qkv_weight_grad(ids, normed, dq, dk, dv, weight, vectors):
    width, third = normed.shape[1], dq.shape[1]
    whole = lambda a: pl.BlockSpec(a.shape, lambda i, s: (0, 0))
    out = jax.ShapeDtypeStruct((width // 2, 3 * third + 128), BF)
    args = (normed, dq, dk, dv, weight, vectors)
    return pl.pallas_call(
        qkv_weight_kernel,
        grid_spec=pltpu.PrefetchScalarGridSpec(
            num_scalar_prefetch=1, grid=(1,), in_specs=[whole(a) for a in args], out_specs=[whole(out)] * 2
        ),
        out_shape=[out, out],
        compiler_params=pltpu.CompilerParams(vmem_limit_bytes=60 * MIB),
        cost_estimate=pl.CostEstimate(
            flops=6 * normed.shape[0] * width * third, bytes_accessed=6 * MIB, transcendentals=0
        ),
        name="qkv_weight_grad",
    )(ids, *args)


def plane_unproject_kernel(place_ref, dq_ref, dk_ref, dv_ref, weight_ref, keep_ref, send_ref):
    mine = (pl.program_id(0) // 2) == place_ref[0]
    grads = jnp.concatenate([dq_ref[...], dk_ref[...], dv_ref[...]], 1)
    grad = nt(grads, weight_ref[...])

    @pl.when(mine)
    def _():
        keep_ref[...] = grad

    @pl.when(jnp.logical_not(mine))
    def _():
        send_ref[...] = grad.astype(BF)


def plane_unproject(place, dq, dk, dv, weight):
    rows, third = dq.shape
    width = weight.shape[0]
    step = rows // 4
    part = pl.BlockSpec((step, third), lambda i, s: (i, 0))
    return pl.pallas_call(
        plane_unproject_kernel,
        grid_spec=pltpu.PrefetchScalarGridSpec(
            num_scalar_prefetch=1,
            grid=(4,),
            in_specs=[part, part, part, pl.BlockSpec(weight.shape, lambda i, s: (0, 0))],
            out_specs=[
                pl.BlockSpec((step, width), lambda i, s: (jnp.clip(i - 2 * s[0], 0, 1), 0)),
                pl.BlockSpec((step, width), lambda i, s: (jnp.clip(i - 2 * (1 - s[0]), 0, 1), 0)),
            ],
        ),
        out_shape=[
            jax.ShapeDtypeStruct((rows // 2, width), F32),
            jax.ShapeDtypeStruct((rows // 2, width), BF),
        ],
        compiler_params=pltpu.CompilerParams(vmem_limit_bytes=60 * MIB),
        cost_estimate=pl.CostEstimate(flops=6 * rows * width * third, bytes_accessed=8 * MIB, transcendentals=0),
        name="grad_at_first_norm",
    )(place, dq, dk, dv, weight)


def plane_plan(
    tokens, segment_ids, ln1_gain, ln1_bias, qkv_weight, qkv_bias, out_weight, out_bias,
    ln2_gain, ln2_bias, fc1_weight, fc1_bias, fc2_weight, fc2_bias, output_grad,
):
    outer, inner = lax.axis_size("outer"), lax.axis_size("inner")
    core, side = lax.axis_index("core"), lax.axis_index("side")
    deep, line = lax.axis_index("outer"), lax.axis_index("inner")
    everyone = ("outer", "core", "inner", "side")
    chips = ("outer", "inner", "side")
    share = qkv_weight.shape[0]
    half = D // 2
    ids = jnp.stack([deep, core, line, side]).astype(jnp.int32)
    place = side.astype(jnp.int32).reshape(1)
    along = lambda block, d: lax.ppermute(block, "inner", [(i, i ^ d) for i in range(inner)])
    across = lambda block, d: lax.ppermute(block, ("outer", "side"), [(i, i ^ d) for i in range(4)])

    wide = lax.all_gather(jnp.concatenate([fc1_weight, out_weight], 1), everyone, axis=0, tiled=True)

    other_marks = swap(segment_ids, "side")
    marks = jnp.where(
        side == 0,
        jnp.concatenate([segment_ids, other_marks]),
        jnp.concatenate([other_marks, segment_ids]),
    )
    firsts = sum(jnp.where(marks > v, jnp.sum(marks == v), 0) for v in range(3))
    firsts = firsts.astype(jnp.int32)[None, :]
    other = swap(tie(tokens, other_marks)[0], "side")

    named = (ln1_gain, ln1_bias, qkv_bias, out_bias, ln2_gain, ln2_bias, fc1_bias, fc2_bias)
    parts = pack(qkv_weight, named)
    got = lax.all_to_all(parts, everyone, split_axis=0, concat_axis=0, tiled=True).reshape(D, 640)
    got, other, firsts = tie(got, other, firsts)
    twin = swap(got, "core")

    _, down = tie(got, fc2_weight)
    lined = [along(down, d) for d in range(1, inner)]

    normed, qkv, w_qkv, mid_vectors, b1 = plane_project(ids, tokens, other, got, twin)
    gain_one = mid_vectors[4:5]
    o_own, o_send, lse = attend(place, qkv, firsts, 0, 2)
    o_own, qkv, *lined = tie(o_own, qkv, *lined)
    stacked = jnp.stack([down, *lined])
    o_own_last, o_send_last, lse_last = attend(place, qkv, firsts, 2, 3)
    o_own = jnp.concatenate([o_own, o_own_last], 1)
    lse = jnp.concatenate([lse, lse_last], 0)
    o_got = swap(jnp.concatenate([o_send, o_send_last], 1), "side")
    o_got, far_x, far_y = tie(o_got, across(stacked, 1), across(stacked, 2))
    far_xy = across(stacked, 3)
    g_sib = swap(output_grad, "core")
    x1, h_own = out_project(ids, tokens, o_own, o_got, wide, mid_vectors)
    h_sib = swap(h_own, "core")

    acts = (h_own, h_sib, output_grad, g_sib, wide)
    y0, y0_sib, dh0, dh0_sib, a00, a10, a01, a11, db1_near = feed_forward(ids, 0, *acts, stacked, far_x, b1)
    got_a10 = across(a10, 1)
    got_a01, got_a11 = across(a01, 2), across(a11, 3)
    far_y, far_xy, dh0 = tie(far_y, far_xy, dh0)
    y, y_send, dh, dh_send, b00, b10, b01, b11, db1_far = feed_forward(
        ids, 1, *acts, far_y, far_xy, b1, (y0, dh0, y0_sib, dh0_sib)
    )
    dh_send, got_a01, got_a11 = tie(dh_send, got_a01, got_a11)
    dh_got, y_got = swap(dh_send, "core"), swap(y_send, "core")
    output, dx1, do_own, do_send, grad_out, sums = second_norm_back(
        ids, x1, y, y_got, dh, dh_got, output_grad, o_own, o_got, wide, mid_vectors
    )
    do_got = swap(do_send, "side")

    def by_core(grad):
        cut = grad.reshape(outer, 2, grad.shape[0] // 4, -1)
        keep = lax.dynamic_index_in_dim(cut, core, 1, keepdims=False)
        return keep, lax.dynamic_index_in_dim(cut, 1 - core, 1, keepdims=False)

    def columns_of(*vectors):
        table = jnp.concatenate([v.reshape(D, -1) for v in vectors], 1)
        return jnp.pad(table, ((0, 0), (0, 128 - table.shape[1]))).astype(BF)

    db1 = jnp.where(deep == 0, jnp.concatenate([db1_near, db1_far]), jnp.concatenate([db1_far, db1_near]))
    db1_mine = jnp.zeros((2, 2, D), F32)
    db1_mine = lax.dynamic_update_slice(db1_mine, db1.reshape(2, 1, D), (0, core, 0)).reshape(-1)
    known = columns_of(sums[D_OUT_BIAS], sums[D_GAIN], sums[D_SHIFT], db1_mine, sums[D_LAST_BIAS])
    out_keep, out_send = by_core(jnp.concatenate([grad_out, known], 1))
    out_both = (out_keep.astype(F32) + swap(out_send, "core").astype(F32)).astype(BF)
    out_both = out_both.reshape(outer, inner, 2 * share, -1).transpose(1, 0, 2, 3).reshape(D // 2, -1)
    out_line = lax.psum_scatter(out_both, "inner", scatter_dimension=0, tiled=True)

    dq, dk, dv = attend_back(place, qkv, do_own, do_got, lse, firsts)
    qkv_keep, qkv_send = qkv_weight_grad(ids, normed, dq, dk, dv, w_qkv, mid_vectors)
    qkv_keep, qkv_send, dq = tie(qkv_keep, qkv_send, dq)
    both = (qkv_keep.astype(F32) + swap(qkv_send, "core").astype(F32)).astype(BF)
    tail = lax.all_to_all(
        both.reshape(outer * inner * 2, share, -1), chips, split_axis=0, concat_axis=0, tiled=True
    )
    kept, sent = plane_unproject(place, dq, dk, dv, w_qkv)
    back = swap(sent, "side")

    got_b10, got_b01, got_b11 = across(b10, 1), across(b01, 2), across(b11, 3)
    got_a10, got_b10, got_b01, got_b11, _ = tie(got_a10, got_b10, got_b01, got_b11, sent)
    add = lambda *parts: sum(p.astype(F32) for p in parts).astype(BF).reshape(inner, -1, D)
    plane_sum = jnp.concatenate([add(a00, got_a10, got_b01, got_b11), add(b00, got_b10, got_a01, got_a11)], 1)
    hidden_sum = lax.psum_scatter(plane_sum.reshape(D, D), "inner", scatter_dimension=0, tiled=True)
    hidden_sum = hidden_sum.astype(F32)
    two_total = hidden_sum[2 * share : 6 * share]
    near, far = hidden_sum[: 2 * share], hidden_sum[6 * share :]
    one_parts = jnp.where(deep == 0, jnp.stack([near, far]), jnp.stack([far, near])).reshape(2, 2, share, D)
    one_keep = lax.dynamic_index_in_dim(one_parts, core, 1, keepdims=False)
    one_got = swap(lax.dynamic_index_in_dim(one_parts, 1 - core, 1, keepdims=False), "core")
    one_total = jnp.where(
        core == 0, jnp.stack([one_keep, one_got], 1), jnp.stack([one_got, one_keep], 1)
    )
    one_total = one_total.transpose(2, 0, 1, 3).reshape(share, 4 * D)

    out_line, _ = tie(out_line, sent)
    out_line = out_line.reshape(outer, 2, share, -1)
    part = lambda d: lax.dynamic_slice(
        out_line, (deep ^ (d >> 1), side ^ (d & 1), 0, 0), (1, 1) + out_line.shape[2:]
    )[0, 0]
    out_total = sum(p.astype(F32) for p in [part(0)] + [across(part(d), d) for d in range(1, 4)])
    known_total = out_total[:, D:]
    out_total = out_total[:, :D]

    tail = tail.astype(F32).reshape(outer * inner, 2, share, 10 * 128)
    qkv_total = jnp.sum(tail[..., : 9 * 128], 0).reshape(2, share, 3, half)
    qkv_total = qkv_total.transpose(1, 2, 0, 3).reshape(share, 3 * D)
    small_total = jnp.sum(tail[..., 9 * 128 :], (0, 1))
    pick = lambda i, n=1: small_total[:, i : i + n].reshape(-1)
    pick_known = lambda i, n=1: known_total[:, i : i + n].reshape(-1)

    hat, inverse = normalise(tokens.astype(F32))
    input_grad = dx1 + norm_grad(kept + back.astype(F32), hat, inverse, gain_one)
    return (
        output, input_grad, pick(0), pick(1), qkv_total, pick(2, 3), out_total, pick_known(0),
        pick_known(1), pick_known(2), one_total, pick_known(3, 4), two_total, pick_known(7),
    )


def solution(mesh):
    dp, fsdp = mesh.devices.shape
    finer = Mesh(
        mesh.devices.reshape(dp // 2, 2, fsdp // 2, 2), ("outer", "core", "inner", "side")
    )
    every = ("outer", "core", "inner", "side")
    vec, mat = P(every), P(every, None)
    plan = plane_plan if finer.devices.shape == (2, 2, 4, 2) else general_plan
    return jax.shard_map(
        plan,
        mesh=finer,
        in_specs=(mat, vec, vec, vec, mat, vec, mat, vec, vec, vec, mat, vec, mat, vec, mat),
        out_specs=(mat, mat, vec, vec, mat, vec, mat, vec, vec, vec, mat, vec, mat, vec),
        check_vma=False,
    )
```

```python
import functools

import jax
import jax.numpy as jnp
import numpy as np
from jax import lax
from jax.experimental import pallas as pl
from jax.experimental.pallas import tpu as pltpu
from jax.sharding import Mesh, PartitionSpec as P

D = 768
HEAD = 64
PAIR = 2 * HEAD
EPSILON = 1e-05
NEG = -1e30
TILE = 256
BF = jnp.bfloat16
F32 = jnp.float32
MIB = 1 << 20
LIGHT = pl.CostEstimate(flops=1 << 20, bytes_accessed=1 << 20, transcendentals=0)
HEAVY = pl.CostEstimate(flops=1 << 36, bytes_accessed=1 << 20, transcendentals=0)


def nn(a, b):
    return jnp.dot(a, b, preferred_element_type=F32)


def nt(a, b):
    return lax.dot_general(a, b, (((1,), (1,)), ((), ())), preferred_element_type=F32)


def tn(a, b):
    return lax.dot_general(a, b, (((0,), (0,)), ((), ())), preferred_element_type=F32)


def normalise(rows):
    average = jnp.mean(rows, -1, keepdims=True)
    centred = rows - average
    inverse = lax.rsqrt(jnp.mean(centred * centred, -1, keepdims=True) + EPSILON)
    return centred * inverse, inverse


def norm_grad(grad, hat, inverse, gain):
    scaled = grad * gain
    return inverse * (
        scaled
        - jnp.mean(scaled, -1, keepdims=True)
        - hat * jnp.mean(scaled * hat, -1, keepdims=True)
    )


def total(rows):
    return jnp.sum(rows, 0, keepdims=True)


def project_kernel(place_ref, own_ref, other_ref, gain_ref, shift_ref, weight_ref, bias_ref, normed_ref, qkv_ref):
    mine = (pl.program_id(0) // 2) == place_ref[0]
    rows = jnp.where(mine, own_ref[...].astype(F32), other_ref[...].astype(F32))
    hat, _ = normalise(rows)
    normed = (hat * gain_ref[...] + shift_ref[...]).astype(BF)
    normed_ref[...] = normed
    qkv_ref[...] = (nn(normed, weight_ref[...]) + bias_ref[...]).astype(BF)


def project(place, own, other, gain, shift, weight, bias):
    rows, width = own.shape
    columns = weight.shape[1]
    step = rows // 2
    half = pl.BlockSpec((step, width), lambda i, s: (i % 2, 0))
    fixed = lambda r, c: pl.BlockSpec((r, c), lambda i, s: (0, 0))
    return pl.pallas_call(
        project_kernel,
        grid_spec=pltpu.PrefetchScalarGridSpec(
            num_scalar_prefetch=1,
            grid=(4,),
            in_specs=[half, half, fixed(1, width), fixed(1, width), fixed(width, columns), fixed(1, columns)],
            out_specs=[
                pl.BlockSpec((step, width), lambda i, s: (i, 0)),
                pl.BlockSpec((step, columns), lambda i, s: (i, 0)),
            ],
        ),
        out_shape=[
            jax.ShapeDtypeStruct((2 * rows, width), BF),
            jax.ShapeDtypeStruct((2 * rows, columns), BF),
        ],
        compiler_params=pltpu.CompilerParams(vmem_limit_bytes=60 * MIB),
        cost_estimate=LIGHT,
        name="norm_and_qkv",
    )(place, own, other, gain, shift, weight, bias)


def forward_kernel(
    place_ref, q_ref, k_ref, v_ref, first_ref, keep_ref, send_ref, lse_ref, mag_buf, sign_buf, o_ref
):
    count = q_ref.shape[0] // TILE
    lane = lax.broadcasted_iota(jnp.int32, (1, PAIR), 1)
    values = jnp.transpose(v_ref[...].astype(F32)).astype(BF)
    key_at = lax.broadcasted_iota(jnp.int32, (TILE, TILE), 0)
    causal = key_at <= lax.broadcasted_iota(jnp.int32, (TILE, TILE), 1)
    for j in range(count):
        qs = slice(j * TILE, (j + 1) * TILE)
        q = q_ref[qs, :] * BF(HEAD**-0.5)
        first = first_ref[:, qs]
        heads = []
        for h in range(2):
            qh = jnp.where((lane >= HEAD) == (h == 1), q, BF(0))
            top = None
            for i in range(j + 1):
                ks = slice(i * TILE, (i + 1) * TILE)
                s = nt(k_ref[ks, :], qh)
                square = s * s + 1.0
                inverse = lax.rsqrt(square)
                allowed = key_at + i * TILE >= first
                if i == j:
                    allowed = allowed & causal
                mag = jnp.where(allowed, square * inverse, NEG)
                mag_buf[h, ks, :] = mag
                sign_buf[h, ks, :] = s * inverse
                best = jnp.max(mag, 0, keepdims=True)
                top = best if top is None else jnp.maximum(top, best)
            weight_sum = jnp.zeros((1, TILE), F32)
            mixture = jnp.zeros((HEAD, TILE), F32)
            for i in range(j + 1):
                ks = slice(i * TILE, (i + 1) * TILE)
                raised = jnp.exp(mag_buf[h, ks, :] - top)
                weight_sum = weight_sum + total(raised)
                mixture = mixture + nn(
                    values[h * HEAD : (h + 1) * HEAD, ks], (sign_buf[h, ks, :] * raised).astype(BF)
                )
            heads.append(mixture * (1.0 / weight_sum))
            lse_ref[0, h : h + 1, qs] = top + jnp.log(weight_sum)
        o_ref[qs, :] = jnp.transpose(jnp.concatenate(heads, 0)).astype(BF)
    rows = keep_ref.shape[0]
    keep_ref[...] = o_ref[pl.ds(pl.multiple_of(place_ref[0] * rows, rows), rows), :]
    send_ref[...] = o_ref[pl.ds(pl.multiple_of((1 - place_ref[0]) * rows, rows), rows), :]


def attend(place, qkv, firsts, start=0, stop=None):
    length, columns = qkv.shape
    pairs = columns // 3 // PAIR
    count = (pairs if stop is None else stop) - start
    block = lambda part: pl.BlockSpec((length, PAIR), lambda p, s: (0, part * pairs + start + p))
    half = pl.BlockSpec((length // 2, PAIR), lambda p, s: (0, p))
    return pl.pallas_call(
        forward_kernel,
        grid_spec=pltpu.PrefetchScalarGridSpec(
            num_scalar_prefetch=1,
            grid=(count,),
            in_specs=[block(0), block(1), block(2), pl.BlockSpec((1, length), lambda p, s: (0, 0))],
            out_specs=[half, half, pl.BlockSpec((1, 2, length), lambda p, s: (p, 0, 0))],
            scratch_shapes=[pltpu.VMEM((2, length, TILE), F32)] * 2 + [pltpu.VMEM((length, PAIR), BF)],
        ),
        out_shape=[
            jax.ShapeDtypeStruct((length // 2, count * PAIR), BF),
            jax.ShapeDtypeStruct((length // 2, count * PAIR), BF),
            jax.ShapeDtypeStruct((count, 2, length), F32),
        ],
        compiler_params=pltpu.CompilerParams(vmem_limit_bytes=60 * MIB),
        cost_estimate=LIGHT,
        name="attention_forward",
    )(place, qkv, qkv, qkv, firsts)


def backward_kernel(
    place_ref, q_ref, k_ref, v_ref, own_ref, got_ref, lse_ref, first_ref,
    dq_ref, dk_ref, dv_ref, dk_sum, dv_sum, part_buf, weight_buf, do_ref,
):
    rows = own_ref.shape[0]
    do_ref[pl.ds(pl.multiple_of(place_ref[0] * rows, rows), rows), :] = own_ref[...]
    do_ref[pl.ds(pl.multiple_of((1 - place_ref[0]) * rows, rows), rows), :] = got_ref[...]
    count = q_ref.shape[0] // TILE
    lane = lax.broadcasted_iota(jnp.int32, (1, PAIR), 1)
    keys = jnp.transpose(k_ref[...].astype(F32)).astype(BF)
    key_at = lax.broadcasted_iota(jnp.int32, (TILE, TILE), 0)
    causal = key_at <= lax.broadcasted_iota(jnp.int32, (TILE, TILE), 1)
    for j in range(count):
        qs = slice(j * TILE, (j + 1) * TILE)
        q = q_ref[qs, :] * BF(HEAD**-0.5)
        do = do_ref[qs, :]
        first = first_ref[:, qs]
        heads = []
        for h in range(2):
            chosen = (lane >= HEAD) == (h == 1)
            qh = jnp.where(chosen, q, BF(0))
            doh = jnp.where(chosen, do, BF(0))
            lse = lse_ref[0, h : h + 1, qs]
            centre = jnp.zeros((1, TILE), F32)
            for i in range(j + 1):
                ks = slice(i * TILE, (i + 1) * TILE)
                s = nt(k_ref[ks, :], qh)
                dw = nt(v_ref[ks, :], doh)
                square = s * s + 1.0
                inverse = lax.rsqrt(square)
                allowed = key_at + i * TILE >= first
                if i == j:
                    allowed = allowed & causal
                p = jnp.exp(jnp.where(allowed, square * inverse - lse, NEG))
                w = s * inverse * p
                centre = centre + total(w * dw)
                part_buf[h, ks, :] = p * dw * (1.0 + inverse * inverse * (inverse - 1.0))
                weight_buf[h, ks, :] = w
                dv = nn(w.astype(BF), doh)
                if i == j and h == 0:
                    dv_sum[ks, :] = dv
                else:
                    dv_sum[ks, :] += dv
            dq = jnp.zeros((HEAD, TILE), F32)
            for i in range(j + 1):
                ks = slice(i * TILE, (i + 1) * TILE)
                ds = (part_buf[h, ks, :] - weight_buf[h, ks, :] * centre).astype(BF)
                dk = nn(ds, qh)
                if i == j and h == 0:
                    dk_sum[ks, :] = dk
                else:
                    dk_sum[ks, :] += dk
                dq = dq + nn(keys[h * HEAD : (h + 1) * HEAD, ks], ds)
            heads.append(dq)
        dq_ref[qs, :] = (jnp.transpose(jnp.concatenate(heads, 0)) * HEAD**-0.5).astype(BF)
    dk_ref[...] = dk_sum[...].astype(BF)
    dv_ref[...] = dv_sum[...].astype(BF)


def attend_back(place, qkv, own, got, lse, firsts):
    length, columns = qkv.shape
    pairs = columns // 3 // PAIR
    block = lambda part: pl.BlockSpec((length, PAIR), lambda p, s: (0, part * pairs + p))
    half = pl.BlockSpec((length // 2, PAIR), lambda p, s: (0, p))
    shape = jax.ShapeDtypeStruct((length, columns // 3), BF)
    return pl.pallas_call(
        backward_kernel,
        grid_spec=pltpu.PrefetchScalarGridSpec(
            num_scalar_prefetch=1,
            grid=(pairs,),
            in_specs=[
                block(0),
                block(1),
                block(2),
                half,
                half,
                pl.BlockSpec((1, 2, length), lambda p, s: (p, 0, 0)),
                pl.BlockSpec((1, length), lambda p, s: (0, 0)),
            ],
            out_specs=[block(0)] * 3,
            scratch_shapes=[pltpu.VMEM((length, PAIR), F32)] * 2
            + [pltpu.VMEM((2, length, TILE), F32)] * 2
            + [pltpu.VMEM((length, PAIR), BF)],
        ),
        out_shape=[shape] * 3,
        compiler_params=pltpu.CompilerParams(vmem_limit_bytes=60 * MIB),
        cost_estimate=LIGHT,
        name="attention_backward",
    )(place, qkv, qkv, qkv, own, got, lse, firsts)


FF_STEP = 768
OUT_BIAS, GAIN, SHIFT, LAST_BIAS = range(4)
D_OUT_BIAS, D_GAIN, D_SHIFT, D_LAST_BIAS = range(4)


def middle_kernel(
    tok_ref, o_ref, g_ref, wo_ref, w1_ref, w2_ref, b1_ref, vec_ref,
    out_ref, dx_ref, do_ref, gone_ref, gtwo_ref, db1_ref, sums_ref,
    x_buf, h_buf, y_sum, dh_sum,
):
    step = pl.program_id(0)
    last = pl.num_programs(0) - 1

    @pl.when(step == 0)
    def _():
        x = tok_ref[...].astype(F32) + nn(o_ref[...], wo_ref[...]) + vec_ref[OUT_BIAS : OUT_BIAS + 1, :]
        x_buf[...] = x
        hat, _ = normalise(x)
        h_buf[...] = (hat * vec_ref[GAIN : GAIN + 1, :] + vec_ref[SHIFT : SHIFT + 1, :]).astype(BF)
        y_sum[...] = jnp.zeros_like(y_sum)
        dh_sum[...] = jnp.zeros_like(dh_sum)

    @pl.when(step < last)
    def _():
        h = h_buf[...]
        g = g_ref[...]
        u = nn(h, w1_ref[...]) + b1_ref[...]
        root = 0.7978845608028654
        u2 = u * u
        bent = jnp.tanh(root * u * (1.0 + 0.044715 * u2))
        a = (0.5 * u * (1.0 + bent)).astype(BF)
        slope = 0.5 * (1.0 + bent) + 0.5 * u * (1.0 - bent * bent) * (root * (1.0 + 0.134145 * u2))
        y_sum[...] += nn(a, w2_ref[...])
        du = (nt(g, w2_ref[...]) * slope).astype(BF)
        db1_ref[...] = total(du.astype(F32))
        dh_sum[...] += nt(du, w1_ref[...])
        gone_ref[...] = tn(h, du).astype(BF)
        gtwo_ref[...] = tn(a, g).astype(BF)

    @pl.when(step == last)
    def _():
        x = x_buf[...]
        g = g_ref[...].astype(F32)
        out_ref[...] = (x + y_sum[...] + vec_ref[LAST_BIAS : LAST_BIAS + 1, :]).astype(BF)
        hat, inverse = normalise(x)
        dh = dh_sum[...]
        dx = g + norm_grad(dh, hat, inverse, vec_ref[GAIN : GAIN + 1, :])
        dx_ref[...] = dx
        dxr = dx.astype(BF)
        do_ref[...] = nt(dxr, wo_ref[...]).astype(BF)
        gone_ref[...] = tn(o_ref[...], dxr).astype(BF)
        sums_ref[...] = jnp.zeros_like(sums_ref)
        sums_ref[D_OUT_BIAS : D_OUT_BIAS + 1, :] = total(dx)
        sums_ref[D_GAIN : D_GAIN + 1, :] = total(dh * hat)
        sums_ref[D_SHIFT : D_SHIFT + 1, :] = total(dh)
        sums_ref[D_LAST_BIAS : D_LAST_BIAS + 1, :] = total(g)


def middle(tokens, mixture, grad, wo, w1, w2, b1, vectors):
    rows, width = tokens.shape
    hidden = w1.shape[1]
    steps = hidden // FF_STEP
    fixed = lambda r, c: pl.BlockSpec((r, c), lambda i: (0, 0))
    across = lambda r: pl.BlockSpec((r, FF_STEP), lambda i: (0, jnp.minimum(i, steps - 1)))
    down = pl.BlockSpec((FF_STEP, width), lambda i: (jnp.minimum(i, steps - 1), 0))
    return pl.pallas_call(
        middle_kernel,
        grid=(steps + 1,),
        in_specs=[
            fixed(rows, width), fixed(rows, width), fixed(rows, width), fixed(width, width),
            across(width), down, across(1), fixed(*vectors.shape),
        ],
        out_specs=[
            fixed(rows, width), fixed(rows, width), fixed(rows, width),
            pl.BlockSpec((width, FF_STEP), lambda i: (0, i)), down, across(1), fixed(8, width),
        ],
        out_shape=[
            jax.ShapeDtypeStruct((rows, width), BF),
            jax.ShapeDtypeStruct((rows, width), F32),
            jax.ShapeDtypeStruct((rows, width), BF),
            jax.ShapeDtypeStruct((width, hidden + FF_STEP), BF),
            jax.ShapeDtypeStruct((hidden, width), BF),
            jax.ShapeDtypeStruct((1, hidden), F32),
            jax.ShapeDtypeStruct((8, width), F32),
        ],
        scratch_shapes=[
            pltpu.VMEM((rows, width), F32),
            pltpu.VMEM((rows, width), BF),
            pltpu.VMEM((rows, width), F32),
            pltpu.VMEM((rows, width), F32),
        ],
        compiler_params=pltpu.CompilerParams(vmem_limit_bytes=60 * MIB),
        cost_estimate=LIGHT,
        name="feed_forward_both_ways",
    )(tokens, mixture, grad, wo, w1, w2, b1, vectors)


def unproject_kernel(
    place_ref, own_ref, other_ref, dq_ref, dk_ref, dv_ref, weight_ref, keep_ref, send_ref, sums_ref, bias_ref
):
    step = pl.program_id(0)
    mine = (step // 2) == place_ref[0]
    rows = jnp.where(mine, own_ref[...].astype(F32), other_ref[...].astype(F32))
    hat, _ = normalise(rows)
    third = dq_ref.shape[1]
    grad = nt(dq_ref[...], weight_ref[:, :third])
    grad = grad + nt(dk_ref[...], weight_ref[:, third : 2 * third])
    grad = grad + nt(dv_ref[...], weight_ref[:, 2 * third :])

    @pl.when(step == 0)
    def _():
        sums_ref[...] = jnp.zeros_like(sums_ref)
        bias_ref[...] = jnp.zeros_like(bias_ref)

    sums_ref[0:1, :] += total(grad * hat)
    sums_ref[1:2, :] += total(grad)
    bias_ref[0:1, :] += total(dq_ref[...].astype(F32))
    bias_ref[1:2, :] += total(dk_ref[...].astype(F32))
    bias_ref[2:3, :] += total(dv_ref[...].astype(F32))

    @pl.when(mine)
    def _():
        keep_ref[...] = grad

    @pl.when(jnp.logical_not(mine))
    def _():
        send_ref[...] = grad.astype(BF)


def unproject(place, own, other, dq, dk, dv, weight):
    rows, width = own.shape
    third = dq.shape[1]
    step = rows // 2
    half = pl.BlockSpec((step, width), lambda i, s: (i % 2, 0))
    part = pl.BlockSpec((step, third), lambda i, s: (i, 0))
    fixed = lambda r, c: pl.BlockSpec((r, c), lambda i, s: (0, 0))
    return pl.pallas_call(
        unproject_kernel,
        grid_spec=pltpu.PrefetchScalarGridSpec(
            num_scalar_prefetch=1,
            grid=(4,),
            in_specs=[half, half, part, part, part, fixed(*weight.shape)],
            out_specs=[
                pl.BlockSpec((step, width), lambda i, s: (jnp.clip(i - 2 * s[0], 0, 1), 0)),
                pl.BlockSpec((step, width), lambda i, s: (jnp.clip(i - 2 * (1 - s[0]), 0, 1), 0)),
                fixed(8, width),
                fixed(8, third),
            ],
        ),
        out_shape=[
            jax.ShapeDtypeStruct((rows, width), F32),
            jax.ShapeDtypeStruct((rows, width), BF),
            jax.ShapeDtypeStruct((8, width), F32),
            jax.ShapeDtypeStruct((8, third), F32),
        ],
        compiler_params=pltpu.CompilerParams(vmem_limit_bytes=60 * MIB),
        cost_estimate=LIGHT,
        name="grad_at_first_norm",
    )(place, own, other, dq, dk, dv, weight)


def tie(*blocks):
    return lax.optimization_barrier(blocks)


def swap(block, axis):
    return lax.ppermute(block, axis, [(0, 1), (1, 0)])


def general_plan(
    tokens, segment_ids, ln1_gain, ln1_bias, qkv_weight, qkv_bias, out_weight, out_bias,
    ln2_gain, ln2_bias, fc1_weight, fc1_bias, fc2_weight, fc2_bias, output_grad,
):
    outer, inner = lax.axis_size("outer"), lax.axis_size("inner")
    core, side = lax.axis_index("core"), lax.axis_index("side")
    everyone = ("outer", "core", "inner", "side")
    chips = ("outer", "inner", "side")
    rows = tokens.shape[0]
    share = qkv_weight.shape[0]
    place = side.astype(jnp.int32).reshape(1)

    other = swap(tokens, "side")
    other_marks = swap(segment_ids, "side")
    marks = jnp.where(
        side == 0,
        jnp.concatenate([segment_ids, other_marks]),
        jnp.concatenate([other_marks, segment_ids]),
    )
    firsts = sum(jnp.where(marks > v, jnp.sum(marks == v), 0) for v in range(3))
    firsts = firsts.astype(jnp.int32)[None, :]

    parts = qkv_weight.reshape(share, 3, 2, D // 2).transpose(2, 0, 1, 3).reshape(2, share, 3 * D // 2)
    vectors = jnp.concatenate(
        [
            v.reshape(share, -1)
            for v in (ln1_gain, ln1_bias, qkv_bias, out_bias, ln2_gain, ln2_bias, fc1_bias, fc2_bias)
        ],
        1,
    )
    vectors = jnp.pad(vectors, ((0, 0), (0, 128 - vectors.shape[1])))
    parts = jnp.concatenate([parts, jnp.broadcast_to(vectors, (2, share, 128))], 2)
    parts = parts.reshape(2, share, 2, 5 * 128).transpose(2, 0, 1, 3)
    parts = jnp.broadcast_to(parts[None, :, None], (outer, 2, inner, 2, share, 5 * 128))
    got = lax.all_to_all(
        parts.reshape(outer * inner * 4, share, 5 * 128), everyone, split_axis=0, concat_axis=0, tiled=True
    ).reshape(D, 5 * 128)
    twin = swap(got, "core")
    packed = jnp.where(core == 0, jnp.concatenate([got, twin], 1), jnp.concatenate([twin, got], 1))
    w_qkv = packed[:, : 9 * 128]
    table = packed[:, 9 * 128 :].astype(F32)
    column = lambda i: table[:, i][None, :]
    qkv_bias_all = table[:, 2:5].reshape(3, 2, D // 2)
    qkv_bias_mine = lax.dynamic_index_in_dim(qkv_bias_all, side, 1, keepdims=False).reshape(1, -1)
    b1 = table[:, 8:12].reshape(1, -1)
    mid_vectors = jnp.concatenate([column(5), column(6), column(7), column(12)], 0)

    wide = lax.all_gather(jnp.concatenate([fc1_weight, out_weight], 1), everyone, axis=0, tiled=True)
    w2 = lax.all_gather(fc2_weight, everyone, axis=0, tiled=True)
    w1, wo = wide[:, : fc1_weight.shape[1]], wide[:, fc1_weight.shape[1] :]

    normed, qkv = project(place, tokens, other, column(0), column(1), w_qkv, qkv_bias_mine)
    mine, theirs, lse = attend(place, qkv, firsts)
    theirs = swap(theirs, "side")
    mixture = jnp.where(side == 0, jnp.concatenate([mine, theirs], 1), jnp.concatenate([theirs, mine], 1))

    output, dx1, do, grad_wide, grad_two, db1, sums = middle(
        tokens, mixture, output_grad, wo, w1, w2, b1, mid_vectors
    )

    half = D // 2
    do_mine = lax.dynamic_slice_in_dim(do, side * half, half, 1)
    do_theirs = swap(lax.dynamic_slice_in_dim(do, (1 - side) * half, half, 1), "side")

    def reduce_rows(grad):
        width = grad.shape[1]
        pieces = grad.reshape(outer, 2, inner * 2, grad.shape[0] // (4 * outer * inner), width)
        keep = lax.dynamic_index_in_dim(pieces, core, 1, keepdims=False)
        send = lax.dynamic_index_in_dim(pieces, 1 - core, 1, keepdims=False)
        both = (keep.astype(F32) + swap(send, "core").astype(F32)).astype(BF)
        both = both.reshape((outer * inner * 2,) + both.shape[2:])
        return lax.all_to_all(both, chips, split_axis=0, concat_axis=0, tiled=True)

    wide_total = jnp.sum(reduce_rows(grad_wide).astype(F32), 0)
    two_total = jnp.sum(reduce_rows(grad_two).astype(F32), 0)

    dq, dk, dv = attend_back(place, qkv, do_mine, do_theirs, lse, firsts)
    kept, sent, first_sums, bias_sums = unproject(place, tokens, other, dq, dk, dv, w_qkv)
    back = swap(sent, "side")
    grad_qkv = jnp.concatenate([tn(normed, d).astype(BF) for d in (dq, dk, dv)], 1)
    bias_mine = jnp.zeros((3, 2, half), F32)
    bias_mine = lax.dynamic_update_slice(bias_mine, bias_sums[:3][:, None], (0, side, 0)).reshape(-1)
    small = jnp.concatenate(
        [
            v.reshape(D, -1)
            for v in (
                first_sums[0], first_sums[1], bias_mine, sums[D_OUT_BIAS], sums[D_GAIN],
                sums[D_SHIFT], db1, sums[D_LAST_BIAS],
            )
        ],
        1,
    )
    small = jnp.pad(small, ((0, 0), (0, 128 - small.shape[1]))).astype(BF)
    tail = reduce_rows(jnp.concatenate([grad_qkv, small], 1)).astype(F32)
    tail = tail.reshape(outer * inner, 2, share, 10 * 128)
    qkv_total = jnp.sum(tail[..., : 9 * 128], 0).reshape(2, share, 3, half)
    qkv_total = qkv_total.transpose(1, 2, 0, 3).reshape(share, 3 * D)
    small_total = jnp.sum(tail[..., 9 * 128 :], (0, 1))
    pick = lambda i, n=1: small_total[:, i : i + n].reshape(-1)

    hat, inverse = normalise(tokens.astype(F32))
    input_grad = dx1 + norm_grad(kept + back.astype(F32), hat, inverse, column(0))
    hidden = fc1_weight.shape[1]
    return (
        output,
        input_grad,
        pick(0),
        pick(1),
        qkv_total,
        pick(2, 3),
        wide_total[:, hidden:],
        pick(5),
        pick(6),
        pick(7),
        wide_total[:, :hidden],
        pick(8, 4),
        two_total,
        pick(12),
    )


SHARE = 24
FF_SHARE = 96
FF_HALF = 8 * FF_SHARE


def pack_kernel(weight_ref, *refs):
    *vector_refs, out_ref, buf = refs
    half = D // 2
    buf[...] = jnp.zeros_like(buf)
    for i, ref in enumerate(vector_refs):
        buf[i : i + 1, : ref.shape[1]] = ref[...].astype(F32)
    vectors = buf[...].astype(BF)
    for x in range(2):
        q, k, v = (weight_ref[:, part * D + x * half : part * D + (x + 1) * half] for part in range(3))
        low = jnp.concatenate([q, k[:, :256]], 1)
        high = jnp.concatenate([k[:, 256:], v, vectors], 1)
        for y in range(2):
            for z in range(4):
                out_ref[((2 * y) * 4 + z) * 2 + x] = low
                out_ref[((2 * y + 1) * 4 + z) * 2 + x] = high


def pack(weight, vectors):
    share = weight.shape[0]
    return pl.pallas_call(
        pack_kernel,
        out_shape=jax.ShapeDtypeStruct((32, share, 640), BF),
        scratch_shapes=[pltpu.VMEM((share, 128), F32)],
        compiler_params=pltpu.CompilerParams(vmem_limit_bytes=60 * MIB),
        name="pack_qkv_weights",
    )(weight, *(v.reshape(1, -1) for v in vectors))


ALL_VECTORS = 8
GAIN_ONE, SHIFT_ONE, QKV_BIAS = 0, 1, 2


def spread(rows, where):
    lanes = lax.broadcasted_iota(jnp.int32, (128, where.shape[1]), 0)
    chosen = jnp.where(lanes == where[1:2, :], 1.0, 0.0).astype(BF)
    found = nn(rows.astype(BF), chosen)
    owners = lax.broadcasted_iota(jnp.int32, found.shape, 0)
    return total(jnp.where(owners == where[0:1, :], found, 0.0))


def places(each, numbers):
    numbers = np.asarray(numbers)
    return np.stack([numbers // each, numbers % each]).astype(np.int32)


def plane_project_kernel(
    ids_ref, own_ref, other_ref, got_ref, twin_ref, at_d_ref, at_qkv_ref, at_ff_ref,
    normed_ref, qkv_ref, weight_ref, vec_ref, b1_ref, table, bias,
):
    @pl.when(pl.program_id(0) == 0)
    def _():
        first = ids_ref[1] == 0
        got, twin = got_ref[...], twin_ref[...]
        weight_ref[:, :640] = jnp.where(first, got, twin)
        high = jnp.where(first, twin, got)
        weight_ref[:, 640:] = high[:, :512]
        table[...] = high[:, 512:].astype(F32)
        rows = lambda i: table[pl.ds(i, 32, stride=SHARE), :]
        bias[...] = spread(rows(QKV_BIAS), at_qkv_ref[0])
        vec_ref[...] = jnp.zeros_like(vec_ref)
        for to, i in enumerate((3, 4, 5, 7, 0, 1)):
            vec_ref[to : to + 1, :] = spread(rows(i), at_d_ref[...])
        b1_ref[...] = spread(rows(6), at_ff_ref[...])

    mine = (pl.program_id(0) // 2) == ids_ref[3]
    rows = jnp.where(mine, own_ref[...], other_ref[...]).astype(F32)
    hat, _ = normalise(rows)
    normed = (hat * vec_ref[4:5, :] + vec_ref[5:6, :]).astype(BF)
    normed_ref[...] = normed
    qkv_ref[...] = (nn(normed, weight_ref[...]) + bias[...]).astype(BF)


def plane_project(ids, own, other, got, twin):
    rows, width = own.shape
    columns = 3 * width // 2
    hidden = 4 * width
    step = rows // 2
    at_d = places(SHARE, range(width))
    at_ff = places(FF_SHARE, range(hidden))
    at_qkv = [
        places(3 * SHARE, [part * width + x * width // 2 + m for part in range(3) for m in range(width // 2)])
        for x in range(2)
    ]
    at_qkv = jnp.stack([jnp.asarray(a) for a in at_qkv])
    half = pl.BlockSpec((step, width), lambda i, s: (i % 2, 0))
    fixed = lambda r, c: pl.BlockSpec((r, c), lambda i, s: (0, 0))
    return pl.pallas_call(
        plane_project_kernel,
        grid_spec=pltpu.PrefetchScalarGridSpec(
            num_scalar_prefetch=1,
            grid=(4,),
            in_specs=[
                half, half, fixed(*got.shape), fixed(*got.shape), fixed(2, width),
                pl.BlockSpec((1, 2, columns), lambda i, s: (s[3], 0, 0)), fixed(2, hidden),
            ],
            out_specs=[
                pl.BlockSpec((step, width), lambda i, s: (i, 0)),
                pl.BlockSpec((step, columns), lambda i, s: (i, 0)),
                fixed(width, columns),
                fixed(8, width),
                fixed(1, hidden),
            ],
            scratch_shapes=[pltpu.VMEM((width, 128), F32), pltpu.VMEM((1, columns), F32)],
        ),
        out_shape=[
            jax.ShapeDtypeStruct((2 * rows, width), BF),
            jax.ShapeDtypeStruct((2 * rows, columns), BF),
            jax.ShapeDtypeStruct((width, columns), BF),
            jax.ShapeDtypeStruct((8, width), F32),
            jax.ShapeDtypeStruct((1, hidden), F32),
        ],
        compiler_params=pltpu.CompilerParams(vmem_limit_bytes=60 * MIB),
        cost_estimate=LIGHT,
        name="norm_and_qkv",
    )(ids, own, other, got, twin, jnp.asarray(at_d), at_qkv, jnp.asarray(at_ff))


def out_project_kernel(ids_ref, tok_ref, own_ref, got_ref, wo_own_ref, wo_got_ref, vec_ref, x_ref, h_ref):
    x = tok_ref[...].astype(F32) + nn(own_ref[...], wo_own_ref[...]) + nn(got_ref[...], wo_got_ref[...])
    x = x + vec_ref[OUT_BIAS : OUT_BIAS + 1, :]
    x_ref[...] = x
    hat, _ = normalise(x)
    h_ref[...] = (hat * vec_ref[GAIN : GAIN + 1, :] + vec_ref[SHIFT : SHIFT + 1, :]).astype(BF)


def out_project(ids, tokens, own, got, wide, vectors):
    rows, width = tokens.shape
    half = width // 2
    step = rows // 2
    tile = lambda c: pl.BlockSpec((step, c), lambda i, s: (i, 0))
    return pl.pallas_call(
        out_project_kernel,
        grid_spec=pltpu.PrefetchScalarGridSpec(
            num_scalar_prefetch=1,
            grid=(2,),
            in_specs=[
                tile(width), tile(half), tile(half),
                pl.BlockSpec((half, width), lambda i, s: (s[3], wide.shape[1] // width - 1)),
                pl.BlockSpec((half, width), lambda i, s: (1 - s[3], wide.shape[1] // width - 1)),
                pl.BlockSpec(vectors.shape, lambda i, s: (0, 0)),
            ],
            out_specs=[tile(width), tile(width)],
        ),
        out_shape=[jax.ShapeDtypeStruct((rows, width), F32), jax.ShapeDtypeStruct((rows, width), BF)],
        compiler_params=pltpu.CompilerParams(vmem_limit_bytes=60 * MIB),
        cost_estimate=LIGHT,
        name="out_projection_and_second_norm",
    )(ids, tokens, own, got, wide, wide, vectors)


def gelu_both(u):
    root = 0.7978845608028654
    u2 = u * u
    bent = jnp.tanh(root * u * (1.0 + 0.044715 * u2))
    a = 0.5 * u * (1.0 + bent)
    slope = 0.5 * (1.0 + bent) + 0.5 * u * (1.0 - bent * bent) * (root * (1.0 + 0.134145 * u2))
    return a.astype(BF), slope


FF_ROWS = 512


def feed_forward_kernel(plane, ids_ref, *refs):
    h_own_hbm, h_sib_hbm, g_own_hbm, g_sib_hbm, wide_hbm, own_hbm, far_hbm, b1_ref, *refs = refs
    earlier, refs = (refs[:2], refs[2:]) if plane else ((), refs)
    outs, db1_ref, refs = refs[:9], refs[9], refs[10:]
    h, g, w1, own, far, w2, y_all, dh_all, one, a_all, du_all, y_sib, dh_sib, *refs = refs
    q00, q10, q01, q11, two, *refs = refs
    y_old, dh_old, in_sems, out_sems = refs if plane else (None, None, *refs)
    my_y, my_c, my_z, my_x = (ids_ref[i] for i in range(4))
    unit = FF_SHARE
    rows = h_own_hbm.shape[0]

    column = pl.multiple_of(((my_y ^ plane) * 2 + my_c) * FF_HALF, FF_HALF)
    sources = [
        (wide_hbm.at[:, pl.ds(column, FF_HALF)], w1), (own_hbm, own), (far_hbm, far), (h_own_hbm, h.at[:rows]),
        (g_own_hbm, g.at[:rows]), (h_sib_hbm, h.at[rows:]), (g_sib_hbm, g.at[rows:]),
    ]
    if plane:
        sources += [(earlier[0], y_old), (earlier[1], dh_old)]
    loads = [pltpu.make_async_copy(src, dst, in_sems.at[i]) for i, (src, dst) in enumerate(sources)]
    for load in loads:
        load.start()
    for load in loads[:3]:
        load.wait()
    for z in range(4):
        near, distant = own[z ^ my_z], far[z ^ my_z]
        w2[2 * z * unit : (2 * z + 1) * unit, :] = jnp.where(my_x == 0, near, distant)
        w2[(2 * z + 1) * unit : (2 * z + 2) * unit, :] = jnp.where(my_x == 0, distant, near)
    for load in loads[3:5]:
        load.wait()

    def one_pass(i, carry):
        if FF_ROWS == rows:
            sib_next = i == 1
        else:
            sib_next = i * FF_ROWS == rows

        @pl.when(sib_next)
        def _():
            for load in loads[5:7]:
                load.wait()

        at = pl.ds(pl.multiple_of(i * FF_ROWS, FF_ROWS), FF_ROWS)
        hr, gr = h[at, :], g[at, :]
        a, slope = gelu_both(nn(hr, w1[...]) + b1_ref[...])
        du = (nt(gr, w2[...]) * slope).astype(BF)
        a_all[at, :] = a
        du_all[at, :] = du
        dh_all[at, :] = nt(du, w1[...])
        y_all[at, :] = nn(a, w2[...])
        return carry + total(du.astype(F32))

    db1_ref[...] = lax.fori_loop(0, 2 * rows // FF_ROWS, one_pass, jnp.zeros(db1_ref.shape, F32))

    stores = []

    def store(src, at):
        copy = pltpu.make_async_copy(src, outs[at], out_sems.at[at])
        copy.start()
        stores.append(copy)

    dh_sib[...] = dh_all[rows:, :].astype(BF)
    store(dh_sib, 3)
    if plane:
        for load in loads[7:]:
            load.wait()
        dh_all[:rows, :] += dh_old[...]
        y_all[:rows, :] += y_old[...]
    store(dh_all.at[:rows], 2)
    store(y_all.at[:rows], 0)
    y_sib[...] = y_all[rows:, :].astype(BF)
    store(y_sib, 1)

    one[...] = tn(h[...], du_all[...])
    two[...] = tn(a_all[...], g[...]).astype(BF)
    store(two, 8)
    for xr, yr, ref, at in ((1, 0, q10, 5), (1, 1, q11, 7), (0, 1, q01, 6), (0, 0, q00, 4)):
        half, share_at = my_y ^ yr, my_x ^ xr
        for z in range(4):
            parts = []
            for c in range(2):
                start = half * (16 * SHARE) + share_at * SHARE + (c * 4 + z) * 2 * SHARE
                parts.append(one[pl.ds(pl.multiple_of(start, 8), SHARE), :])
            ref[2 * z * SHARE : 2 * (z + 1) * SHARE, :] = jnp.concatenate(parts, 0).astype(BF)
        store(ref, at)
    for copy in stores:
        copy.wait()


def feed_forward(ids, plane, h_own, h_sib, g_own, g_sib, wide, own, far, b1, earlier=()):
    rows, width = h_own.shape
    anywhere = pl.BlockSpec(memory_space=pl.ANY)
    shape = jax.ShapeDtypeStruct
    f32, bf = shape((rows, width), F32), shape((rows, width), BF)
    pieces = [shape((8 * SHARE, width), BF)] * 4
    pieces += [shape((FF_HALF, width), BF)]
    held = lambda s: pltpu.VMEM(s.shape, s.dtype)
    scratch = [pltpu.VMEM((2 * rows, width), BF)] * 2
    scratch += [pltpu.VMEM((width, FF_HALF), BF), held(own), held(far), pltpu.VMEM((FF_HALF, width), BF)]
    scratch += [pltpu.VMEM((2 * rows, width), F32)] * 2 + [pltpu.VMEM((width, FF_HALF), F32)]
    scratch += [pltpu.VMEM((2 * rows, FF_HALF), BF)] * 2
    scratch += [held(bf)] * 2 + [held(s) for s in pieces]
    scratch += [held(f32)] * 2 if plane else []
    scratch += [pltpu.SemaphoreType.DMA((9,)), pltpu.SemaphoreType.DMA((9,))]
    return pl.pallas_call(
        functools.partial(feed_forward_kernel, plane),
        grid_spec=pltpu.PrefetchScalarGridSpec(
            num_scalar_prefetch=1,
            grid=(1,),
            in_specs=[anywhere] * 7
            + [pl.BlockSpec((1, FF_HALF), lambda i, s: (0, (s[0] ^ plane) * 2 + s[1]))]
            + [anywhere] * len(earlier),
            out_specs=[anywhere] * 9 + [pl.BlockSpec((1, FF_HALF), lambda i, s: (0, 0))],
            scratch_shapes=scratch,
        ),
        out_shape=[f32, bf, f32, bf] + pieces + [shape((1, FF_HALF), F32)],
        compiler_params=pltpu.CompilerParams(vmem_limit_bytes=60 * MIB),
        cost_estimate=LIGHT,
        name=f"feed_forward_both_ways_{plane}",
    )(ids, h_own, h_sib, g_own, g_sib, wide, own, far, b1, *earlier)


def second_norm_kernel(
    ids_ref, x_ref, dh_ref, dh0_ref, dh1_ref, g_ref, wo_ref, vec_ref, dx_ref, dxr_ref, do_own_ref, do_send_ref, sums
):
    x = x_ref[...]
    g = g_ref[...].astype(F32)
    hat, inverse = normalise(x)
    dh = dh_ref[...] + dh0_ref[...].astype(F32) + dh1_ref[...].astype(F32)
    dx = g + norm_grad(dh, hat, inverse, vec_ref[GAIN : GAIN + 1, :])
    dx_ref[...] = dx
    dxr = dx.astype(BF)
    dxr_ref[...] = dxr
    half = wo_ref.shape[0] // 2
    mine = pl.ds(pl.multiple_of(ids_ref[3] * half, half), half)
    theirs = pl.ds(pl.multiple_of((1 - ids_ref[3]) * half, half), half)
    do_send_ref[...] = nt(dxr, wo_ref[theirs, :]).astype(BF)
    do_own_ref[...] = nt(dxr, wo_ref[mine, :]).astype(BF)

    @pl.when(pl.program_id(0) == 0)
    def _():
        sums[...] = jnp.zeros_like(sums)

    sums[D_OUT_BIAS : D_OUT_BIAS + 1, :] += total(dx)
    sums[D_GAIN : D_GAIN + 1, :] += total(dh * hat)
    sums[D_SHIFT : D_SHIFT + 1, :] += total(dh)
    sums[D_LAST_BIAS : D_LAST_BIAS + 1, :] += total(g)


def second_norm_back(ids, x, dh, dh0, dh1, g, wide, vectors):
    rows, width = x.shape
    step = rows // 2
    tile = lambda c: pl.BlockSpec((step, c), lambda i, s: (i, 0))
    shape = jax.ShapeDtypeStruct
    half = width // 2
    return pl.pallas_call(
        second_norm_kernel,
        grid_spec=pltpu.PrefetchScalarGridSpec(
            num_scalar_prefetch=1,
            grid=(2,),
            in_specs=[tile(width)] * 5
            + [
                pl.BlockSpec((width, width), lambda i, s: (0, wide.shape[1] // width - 1)),
                pl.BlockSpec(vectors.shape, lambda i, s: (0, 0)),
            ],
            out_specs=[tile(width), tile(width), tile(half), tile(half), pl.BlockSpec((8, width), lambda i, s: (0, 0))],
        ),
        out_shape=[
            shape((rows, width), F32), shape((rows, width), BF), shape((rows, half), BF),
            shape((rows, half), BF), shape((8, width), F32),
        ],
        compiler_params=pltpu.CompilerParams(vmem_limit_bytes=60 * MIB),
        cost_estimate=LIGHT,
        name="second_norm_back",
    )(ids, x, dh, dh0, dh1, g, wide, vectors)


def out_weight_kernel(
    ids_ref, dxr_ref, o_own_ref, o_got_ref, sums_ref, near_ref, far_ref, keep_ref, send_ref, gwo
):
    width = dxr_ref.shape[1]
    half = width // 2
    mine = pl.ds(pl.multiple_of(ids_ref[3] * half, half), half)
    theirs = pl.ds(pl.multiple_of((1 - ids_ref[3]) * half, half), half)
    gwo[mine, :] = tn(o_own_ref[...], dxr_ref[...]).astype(BF)
    gwo[theirs, :] = tn(o_got_ref[...], dxr_ref[...]).astype(BF)
    lane = lax.broadcasted_iota(jnp.int32, (width, 128), 1)
    columns = jnp.transpose(sums_ref[...])
    table = jnp.zeros((width, 128), F32)
    for i in range(4):
        table = table + jnp.where(lane == i, columns[:, i : i + 1], 0.0)
    block = width // 4
    first, low = ids_ref[1] == 0, ids_ref[0] == 0
    near = jnp.transpose(jnp.broadcast_to(near_ref[...], (8, width)))[:, :1]
    far = jnp.transpose(jnp.broadcast_to(far_ref[...], (8, width)))[:, :1]
    halves = (jnp.where(low, near, far), jnp.where(low, far, near))
    for j in range(4):
        cut = lambda h: jnp.concatenate([h[k * FF_SHARE + j * SHARE :][:SHARE] for k in range(width // FF_SHARE)], 0)
        zero = jnp.zeros((block, 1), F32)
        column = []
        for h in halves:
            column += [jnp.where(first, cut(h), zero), jnp.where(first, zero, cut(h))]
        table = table + jnp.where(lane == 4 + j, jnp.concatenate(column, 0), 0.0)
    table = table.astype(BF)
    size = 2 * SHARE
    for y in range(2):
        for z in range(4):
            to = slice((z * 2 + y) * size, (z * 2 + y + 1) * size)
            for ref, here in ((keep_ref, ids_ref[1]), (send_ref, 1 - ids_ref[1])):
                start = pl.multiple_of(here * 4 * size + (y * 8 + z) * size, 16)
                ref[to, :width] = gwo[pl.ds(start, size), :]
            cut = lambda c: table[((y * 2 + c) * 4 + z) * size :][:size]
            keep_ref[to, width:] = jnp.where(first, cut(0), cut(1))
            send_ref[to, width:] = jnp.where(first, cut(1), cut(0))


def out_weight_grad(ids, dxr, o_own, o_got, sums, near, far):
    width = dxr.shape[1]
    whole = lambda a: pl.BlockSpec(a.shape, lambda i, s: (0, 0))
    out = jax.ShapeDtypeStruct((width // 2, width + 128), BF)
    args = (dxr, o_own, o_got, sums, near, far)
    return pl.pallas_call(
        out_weight_kernel,
        grid_spec=pltpu.PrefetchScalarGridSpec(
            num_scalar_prefetch=1, grid=(1,), in_specs=[whole(a) for a in args], out_specs=[whole(out)] * 2,
            scratch_shapes=[pltpu.VMEM((width, width), BF)],
        ),
        out_shape=[out, out],
        compiler_params=pltpu.CompilerParams(vmem_limit_bytes=60 * MIB),
        cost_estimate=LIGHT,
        name="out_weight_grad",
    )(ids, *args)


def qkv_back_kernel(
    ids_ref, h_ref, dq_ref, dk_ref, dv_ref, weight_ref, vec_ref, keep_ref, send_ref, dh_keep_ref, dh_send_ref, full
):
    first = ids_ref[1] == 0
    width = h_ref.shape[1]
    block = width // 4
    third = dq_ref.shape[1]
    grads = jnp.concatenate([dq_ref[...], dk_ref[...], dv_ref[...]], 1)
    weight = weight_ref[...]
    full[...] = tn(h_ref[...], grads)

    vectors = jnp.transpose(vec_ref[...])
    gain, shift = vectors[:, 4:5], vectors[:, 5:6]
    sums = total(grads.astype(F32))
    by_shift = nt(weight, jnp.broadcast_to(sums, (8, 3 * third)).astype(BF))[:, :1]
    by_gain = (jnp.sum(weight.astype(F32) * full[...], 1, keepdims=True) - shift * by_shift) / gain
    place = lax.broadcasted_iota(jnp.int32, (width, third), 1) - 3 * lax.broadcasted_iota(jnp.int32, (width, third), 0)
    chosen = []
    for part in range(3):
        low = -(part * width + ids_ref[3] * third)
        here = (place >= low) & (place < low + 3)
        chosen.append(jnp.where(here, sums[:, part * third : (part + 1) * third], 0.0).astype(BF))
    row = lax.broadcasted_iota(jnp.int32, (3 * third, 128), 0)
    spots = jnp.where(lax.rem(row, 3) + 2 == lax.broadcasted_iota(jnp.int32, (3 * third, 128), 1), 1.0, 0.0).astype(BF)
    table = nn(jnp.concatenate(chosen, 1), spots)
    lane = lax.broadcasted_iota(jnp.int32, (width, 128), 1)
    table = table + jnp.where(lane == 0, by_gain, 0.0) + jnp.where(lane == 1, by_shift, 0.0)

    table = table.astype(BF)
    for y in range(2):
        at = slice(y * block, (y + 1) * block)
        low, high = table[2 * y * block :][:block], table[(2 * y + 1) * block :][:block]
        keep_ref[at, 3 * third :] = jnp.where(first, low, high)
        send_ref[at, 3 * third :] = jnp.where(first, high, low)
        for ref, here in ((keep_ref, ids_ref[1]), (send_ref, 1 - ids_ref[1])):
            start = pl.multiple_of(here * block + 2 * y * block, 16)
            ref[at, : 3 * third] = full[pl.ds(start, block), :].astype(BF)

    dh = nt(grads, weight)
    rows = dh_keep_ref.shape[0]
    mine = ids_ref[3] == 0
    dh_keep_ref[...] = jnp.where(mine, dh[:rows], dh[rows:])
    dh_send_ref[...] = jnp.where(mine, dh[rows:], dh[:rows]).astype(BF)


def qkv_back(ids, normed, dq, dk, dv, weight, vectors):
    rows, width = normed.shape
    third = dq.shape[1]
    shape = jax.ShapeDtypeStruct
    whole = lambda a: pl.BlockSpec(a.shape, lambda i, s: (0, 0))
    part = shape((width // 2, 3 * third + 128), BF)
    outs = [part, part, shape((rows // 2, width), F32), shape((rows // 2, width), BF)]
    args = (normed, dq, dk, dv, weight, vectors)
    return pl.pallas_call(
        qkv_back_kernel,
        grid_spec=pltpu.PrefetchScalarGridSpec(
            num_scalar_prefetch=1, grid=(1,), in_specs=[whole(a) for a in args], out_specs=[whole(o) for o in outs],
            scratch_shapes=[pltpu.VMEM((width, 3 * third), F32)],
        ),
        out_shape=outs,
        compiler_params=pltpu.CompilerParams(vmem_limit_bytes=60 * MIB),
        cost_estimate=LIGHT,
        name="qkv_back",
    )(ids, *args)


def tail_kernel(tail_ref, qkv_ref, small_ref):
    half = D // 2
    small = jnp.zeros((SHARE, 128), F32)
    for x in range(2):
        sums = jnp.zeros((SHARE, 3 * half + 128), F32)
        for i in range(4):
            sums = sums + tail_ref[2 * i + x].astype(F32)
        for part in range(3):
            qkv_ref[:, part * D + x * half : part * D + (x + 1) * half] = sums[:, part * half : (part + 1) * half]
        small = small + sums[:, 3 * half :]
    small_ref[...] = small


def sum_tail(tail):
    shape = jax.ShapeDtypeStruct
    return pl.pallas_call(
        tail_kernel,
        out_shape=[shape((SHARE, 3 * D), F32), shape((SHARE, 128), F32)],
        compiler_params=pltpu.CompilerParams(vmem_limit_bytes=60 * MIB),
        cost_estimate=HEAVY,
        name="sum_of_qkv_gradients",
    )(tail)


def plane_plan(
    tokens, segment_ids, ln1_gain, ln1_bias, qkv_weight, qkv_bias, out_weight, out_bias,
    ln2_gain, ln2_bias, fc1_weight, fc1_bias, fc2_weight, fc2_bias, output_grad,
):
    outer, inner = lax.axis_size("outer"), lax.axis_size("inner")
    core, side = lax.axis_index("core"), lax.axis_index("side")
    deep, line = lax.axis_index("outer"), lax.axis_index("inner")
    everyone = ("outer", "core", "inner", "side")
    chips = ("outer", "inner", "side")
    share = qkv_weight.shape[0]
    half = D // 2
    ids = jnp.stack([deep, core, line, side]).astype(jnp.int32)
    place = side.astype(jnp.int32).reshape(1)
    along = lambda block, d: lax.ppermute(block, "inner", [(i, i ^ d) for i in range(inner)])
    across = lambda block, d: lax.ppermute(block, ("outer", "side"), [(i, i ^ d) for i in range(4)])

    wide = lax.all_gather(jnp.concatenate([fc1_weight, out_weight], 1), everyone, axis=0, tiled=True)

    other_marks = swap(segment_ids, "side")
    marks = jnp.where(
        side == 0,
        jnp.concatenate([segment_ids, other_marks]),
        jnp.concatenate([other_marks, segment_ids]),
    )
    firsts = sum(jnp.where(marks > v, jnp.sum(marks == v), 0) for v in range(3))
    firsts = firsts.astype(jnp.int32)[None, :]
    other = swap(tie(tokens, other_marks)[0], "side")

    named = (ln1_gain, ln1_bias, qkv_bias, out_bias, ln2_gain, ln2_bias, fc1_bias, fc2_bias)
    parts = pack(qkv_weight, named)
    got = lax.all_to_all(parts, everyone, split_axis=0, concat_axis=0, tiled=True).reshape(D, 640)
    got, other, firsts = tie(got, other, firsts)
    twin = swap(got, "core")

    _, down = tie(got, fc2_weight)
    lined = [along(down, d) for d in range(1, inner)]

    normed, qkv, w_qkv, mid_vectors, b1 = plane_project(ids, tokens, other, got, twin)
    gain_one = mid_vectors[4:5]
    o_own, o_send, lse = attend(place, qkv, firsts, 0, 2)
    o_own, qkv, *lined = tie(o_own, qkv, *lined)
    stacked = jnp.stack([down, *lined])
    o_own_last, o_send_last, lse_last = attend(place, qkv, firsts, 2, 3)
    o_own = jnp.concatenate([o_own, o_own_last], 1)
    lse = jnp.concatenate([lse, lse_last], 0)
    o_got = swap(jnp.concatenate([o_send, o_send_last], 1), "side")
    o_got, far_x, far_y = tie(o_got, across(stacked, 1), across(stacked, 2))
    far_xy = across(far_x, 2)
    g_sib = swap(output_grad, "core")
    x1, h_own = out_project(ids, tokens, o_own, o_got, wide, mid_vectors)
    h_sib = swap(h_own, "core")

    acts = (h_own, h_sib, output_grad, g_sib, wide)
    y0, y0_sib, dh0, dh0_sib, a00, a10, a01, a11, two_near, db1_near = feed_forward(
        ids, 0, *acts, stacked, far_x, b1
    )
    line = lambda block: lax.psum_scatter(block, "inner", scatter_dimension=0, tiled=True)
    dh0_got, y0_got = swap(dh0_sib, "core"), swap(y0_sib, "core")
    got_a10, got_a01, got_a11 = across(a10, 1), across(a01, 2), across(a11, 3)
    far_y, far_xy, dh0, two_near = tie(far_y, far_xy, dh0, two_near)
    two_near = line(two_near)
    y, y_send, dh, dh_send, b00, b10, b01, b11, two_far, db1_far = feed_forward(
        ids, 1, *acts, far_y, far_xy, b1, (y0, dh0)
    )
    dh_send, got_a10, got_a01, got_a11 = tie(dh_send, got_a10, got_a01, got_a11)
    dh_got, y_got = swap(dh_send, "core"), swap(y_send, "core")
    dh_got, dh0_got, y0_got, two_far = tie(dh_got, dh0_got, y0_got, two_far)
    two_far = line(two_far)
    dx1, dxr, do_own, do_send, sums = second_norm_back(
        ids, x1, dh, dh0_got, dh_got, output_grad, wide, mid_vectors
    )
    do_got = swap(do_send, "side")
    parts = (x1, y, y0_got.astype(F32), y_got.astype(F32), mid_vectors[LAST_BIAS : LAST_BIAS + 1])
    output = sum(parts).astype(BF)
    out_keep, out_send = out_weight_grad(ids, dxr, o_own, o_got, sums, db1_near, db1_far)

    out_got = swap(out_send, "core")
    out_got, b10, b01, b11 = tie(out_got, b10, b01, b11)
    out_both = (out_keep.astype(F32) + out_got.astype(F32)).astype(BF).reshape(inner, 4 * share, -1)
    got_b10, got_b01, got_b11 = across(b10, 1), across(b01, 2), across(b11, 3)

    dq, dk, dv = attend_back(place, qkv, do_own, do_got, lse, firsts)
    dq, got_b10, got_b01, got_b11 = tie(dq, got_b10, got_b01, got_b11)
    qkv_keep, qkv_send, kept, sent = qkv_back(ids, normed, dq, dk, dv, w_qkv, mid_vectors)
    qkv_send, two_near, two_far = tie(qkv_send, two_near, two_far)
    both = (qkv_keep.astype(F32) + swap(qkv_send, "core").astype(F32)).astype(BF)
    both = both.reshape(outer, D // 4, -1)
    mine, theirs = (lax.dynamic_index_in_dim(both, at, 0, keepdims=False) for at in (deep, 1 - deep))
    both = (mine.astype(F32) + across(theirs, 2).astype(F32)).astype(BF)
    tail = lax.all_to_all(
        both.reshape(inner * 2, share, -1), ("inner", "side"), split_axis=0, concat_axis=0, tiled=True
    )
    back = swap(sent, "side")

    add = lambda *parts: sum(p.astype(F32) for p in parts).astype(BF).reshape(inner, -1, D)
    plane_sum = jnp.concatenate([add(a00, got_a10, got_b01, got_b11), add(b00, got_b10, got_a01, got_a11)], 1)
    joined = jnp.concatenate([jnp.pad(plane_sum, ((0, 0), (0, 0), (0, 128))), out_both], 1)
    joined = line(joined.reshape(8 * inner * share, D + 128))
    one_sum, out_line = joined[: 4 * share, :D].astype(F32), joined[4 * share :]
    tail, back, one_sum = tie(tail, back, one_sum)
    near, far = one_sum[: 2 * share], one_sum[2 * share :]
    one_parts = jnp.where(deep == 0, jnp.stack([near, far]), jnp.stack([far, near])).reshape(2, 2, share, D)
    one_keep = lax.dynamic_index_in_dim(one_parts, core, 1, keepdims=False)
    one_got = swap(lax.dynamic_index_in_dim(one_parts, 1 - core, 1, keepdims=False), "core")
    one_total = jnp.where(
        core == 0, jnp.stack([one_keep, one_got], 1), jnp.stack([one_got, one_keep], 1)
    )
    one_total = one_total.transpose(2, 0, 1, 3).reshape(share, 4 * D)

    two = (two_near.reshape(2, FF_SHARE, D), two_far.reshape(2, FF_SHARE, D))
    side_of = lambda half, x: lax.dynamic_index_in_dim(two[half], x, 0, keepdims=False)
    two_parts = (
        side_of(0, side), across(side_of(0, 1 - side), 1),
        across(side_of(1, side), 2), across(side_of(1, 1 - side), 3),
    )
    two_total = sum(p.astype(F32) for p in two_parts)
    out_line = out_line.reshape(outer, 2, share, -1)
    part = lambda d: lax.dynamic_slice(
        out_line, (deep ^ (d >> 1), side ^ (d & 1), 0, 0), (1, 1) + out_line.shape[2:]
    )[0, 0]
    out_total = sum(p.astype(F32) for p in [part(0)] + [across(part(d), d) for d in range(1, 4)])
    known_total = out_total[:, D:]
    out_total = out_total[:, :D]

    qkv_total, small_total = sum_tail(tail)
    pick = lambda i, n=1: small_total[:, i : i + n].reshape(-1)
    pick_known = lambda i, n=1: known_total[:, i : i + n].reshape(-1)

    hat, inverse = normalise(tokens.astype(F32))
    input_grad = dx1 + norm_grad(kept + back.astype(F32), hat, inverse, gain_one)
    return (
        output, input_grad, pick(0), pick(1), qkv_total, pick(2, 3), out_total, pick_known(0),
        pick_known(1), pick_known(2), one_total, known_total[:, 4:8].T.reshape(-1), two_total, pick_known(3),
    )


def solution(mesh):
    dp, fsdp = mesh.devices.shape
    finer = Mesh(
        mesh.devices.reshape(dp // 2, 2, fsdp // 2, 2), ("outer", "core", "inner", "side")
    )
    every = ("outer", "core", "inner", "side")
    vec, mat = P(every), P(every, None)
    plan = plane_plan if finer.devices.shape == (2, 2, 4, 2) else general_plan
    return jax.shard_map(
        plan,
        mesh=finer,
        in_specs=(mat, vec, vec, vec, mat, vec, mat, vec, vec, vec, mat, vec, mat, vec, mat),
        out_specs=(mat, mat, vec, vec, mat, vec, mat, vec, vec, vec, mat, vec, mat, vec),
        check_vma=False,
    )
```

```python
import functools

import jax
import jax.numpy as jnp
import numpy as np
from jax import lax
from jax.experimental import pallas as pl
from jax.experimental.pallas import tpu as pltpu
from jax.sharding import Mesh, PartitionSpec as P

D = 768
HEAD = 64
PAIR = 2 * HEAD
EPSILON = 1e-05
NEG = -1e30
TILE = 256
BF = jnp.bfloat16
F32 = jnp.float32
MIB = 1 << 20
LIGHT = pl.CostEstimate(flops=1 << 20, bytes_accessed=1 << 20, transcendentals=0)
HEAVY = pl.CostEstimate(flops=1 << 36, bytes_accessed=1 << 20, transcendentals=0)


def nn(a, b):
    return jnp.dot(a, b, preferred_element_type=F32)


def nt(a, b):
    return lax.dot_general(a, b, (((1,), (1,)), ((), ())), preferred_element_type=F32)


def tn(a, b):
    return lax.dot_general(a, b, (((0,), (0,)), ((), ())), preferred_element_type=F32)


def normalise(rows):
    average = jnp.mean(rows, -1, keepdims=True)
    centred = rows - average
    inverse = lax.rsqrt(jnp.mean(centred * centred, -1, keepdims=True) + EPSILON)
    return centred * inverse, inverse


def norm_grad(grad, hat, inverse, gain):
    scaled = grad * gain
    return inverse * (
        scaled
        - jnp.mean(scaled, -1, keepdims=True)
        - hat * jnp.mean(scaled * hat, -1, keepdims=True)
    )


def total(rows):
    return jnp.sum(rows, 0, keepdims=True)


def project_kernel(place_ref, own_ref, other_ref, gain_ref, shift_ref, weight_ref, bias_ref, normed_ref, qkv_ref):
    mine = (pl.program_id(0) // 2) == place_ref[0]
    rows = jnp.where(mine, own_ref[...].astype(F32), other_ref[...].astype(F32))
    hat, _ = normalise(rows)
    normed = (hat * gain_ref[...] + shift_ref[...]).astype(BF)
    normed_ref[...] = normed
    qkv_ref[...] = (nn(normed, weight_ref[...]) + bias_ref[...]).astype(BF)


def project(place, own, other, gain, shift, weight, bias):
    rows, width = own.shape
    columns = weight.shape[1]
    step = rows // 2
    half = pl.BlockSpec((step, width), lambda i, s: (i % 2, 0))
    fixed = lambda r, c: pl.BlockSpec((r, c), lambda i, s: (0, 0))
    return pl.pallas_call(
        project_kernel,
        grid_spec=pltpu.PrefetchScalarGridSpec(
            num_scalar_prefetch=1,
            grid=(4,),
            in_specs=[half, half, fixed(1, width), fixed(1, width), fixed(width, columns), fixed(1, columns)],
            out_specs=[
                pl.BlockSpec((step, width), lambda i, s: (i, 0)),
                pl.BlockSpec((step, columns), lambda i, s: (i, 0)),
            ],
        ),
        out_shape=[
            jax.ShapeDtypeStruct((2 * rows, width), BF),
            jax.ShapeDtypeStruct((2 * rows, columns), BF),
        ],
        compiler_params=pltpu.CompilerParams(vmem_limit_bytes=60 * MIB),
        cost_estimate=LIGHT,
        name="norm_and_qkv",
    )(place, own, other, gain, shift, weight, bias)


def forward_kernel(
    place_ref, q_ref, k_ref, v_ref, first_ref, keep_ref, send_ref, lse_ref, mag_buf, sign_buf, o_ref
):
    count = q_ref.shape[0] // TILE
    lane = lax.broadcasted_iota(jnp.int32, (1, PAIR), 1)
    values = jnp.transpose(v_ref[...].astype(F32)).astype(BF)
    key_at = lax.broadcasted_iota(jnp.int32, (TILE, TILE), 0)
    causal = key_at <= lax.broadcasted_iota(jnp.int32, (TILE, TILE), 1)
    for j in range(count):
        qs = slice(j * TILE, (j + 1) * TILE)
        q = q_ref[qs, :] * BF(HEAD**-0.5)
        first = first_ref[:, qs]
        heads = []
        for h in range(2):
            qh = jnp.where((lane >= HEAD) == (h == 1), q, BF(0))
            top = None
            for i in range(j + 1):
                ks = slice(i * TILE, (i + 1) * TILE)
                s = nt(k_ref[ks, :], qh)
                square = s * s + 1.0
                inverse = lax.rsqrt(square)
                allowed = key_at + i * TILE >= first
                if i == j:
                    allowed = allowed & causal
                mag = jnp.where(allowed, square * inverse, NEG)
                mag_buf[h, ks, :] = mag
                sign_buf[h, ks, :] = s * inverse
                best = jnp.max(mag, 0, keepdims=True)
                top = best if top is None else jnp.maximum(top, best)
            weight_sum = jnp.zeros((1, TILE), F32)
            mixture = jnp.zeros((HEAD, TILE), F32)
            for i in range(j + 1):
                ks = slice(i * TILE, (i + 1) * TILE)
                raised = jnp.exp(mag_buf[h, ks, :] - top)
                weight_sum = weight_sum + total(raised)
                mixture = mixture + nn(
                    values[h * HEAD : (h + 1) * HEAD, ks], (sign_buf[h, ks, :] * raised).astype(BF)
                )
            heads.append(mixture * (1.0 / weight_sum))
            lse_ref[0, h : h + 1, qs] = top + jnp.log(weight_sum)
        o_ref[qs, :] = jnp.transpose(jnp.concatenate(heads, 0)).astype(BF)
    rows = keep_ref.shape[0]
    keep_ref[...] = o_ref[pl.ds(pl.multiple_of(place_ref[0] * rows, rows), rows), :]
    send_ref[...] = o_ref[pl.ds(pl.multiple_of((1 - place_ref[0]) * rows, rows), rows), :]


def attend(place, qkv, firsts, start=0, stop=None):
    length, columns = qkv.shape
    pairs = columns // 3 // PAIR
    count = (pairs if stop is None else stop) - start
    block = lambda part: pl.BlockSpec((length, PAIR), lambda p, s: (0, part * pairs + start + p))
    half = pl.BlockSpec((length // 2, PAIR), lambda p, s: (0, p))
    return pl.pallas_call(
        forward_kernel,
        grid_spec=pltpu.PrefetchScalarGridSpec(
            num_scalar_prefetch=1,
            grid=(count,),
            in_specs=[block(0), block(1), block(2), pl.BlockSpec((1, length), lambda p, s: (0, 0))],
            out_specs=[half, half, pl.BlockSpec((1, 2, length), lambda p, s: (p, 0, 0))],
            scratch_shapes=[pltpu.VMEM((2, length, TILE), F32)] * 2 + [pltpu.VMEM((length, PAIR), BF)],
        ),
        out_shape=[
            jax.ShapeDtypeStruct((length // 2, count * PAIR), BF),
            jax.ShapeDtypeStruct((length // 2, count * PAIR), BF),
            jax.ShapeDtypeStruct((count, 2, length), F32),
        ],
        compiler_params=pltpu.CompilerParams(vmem_limit_bytes=60 * MIB),
        cost_estimate=LIGHT,
        name="attention_forward",
    )(place, qkv, qkv, qkv, firsts)


def backward_kernel(
    place_ref, q_ref, k_ref, v_ref, own_ref, got_ref, lse_ref, first_ref,
    dq_ref, dk_ref, dv_ref, dk_sum, dv_sum, part_buf, weight_buf, do_ref,
):
    rows = own_ref.shape[0]
    do_ref[pl.ds(pl.multiple_of(place_ref[0] * rows, rows), rows), :] = own_ref[...]
    do_ref[pl.ds(pl.multiple_of((1 - place_ref[0]) * rows, rows), rows), :] = got_ref[...]
    count = q_ref.shape[0] // TILE
    lane = lax.broadcasted_iota(jnp.int32, (1, PAIR), 1)
    keys = jnp.transpose(k_ref[...].astype(F32)).astype(BF)
    key_at = lax.broadcasted_iota(jnp.int32, (TILE, TILE), 0)
    causal = key_at <= lax.broadcasted_iota(jnp.int32, (TILE, TILE), 1)
    for j in range(count):
        qs = slice(j * TILE, (j + 1) * TILE)
        q = q_ref[qs, :] * BF(HEAD**-0.5)
        do = do_ref[qs, :]
        first = first_ref[:, qs]
        heads = []
        for h in range(2):
            chosen = (lane >= HEAD) == (h == 1)
            qh = jnp.where(chosen, q, BF(0))
            doh = jnp.where(chosen, do, BF(0))
            lse = lse_ref[0, h : h + 1, qs]
            centre = jnp.zeros((1, TILE), F32)
            for i in range(j + 1):
                ks = slice(i * TILE, (i + 1) * TILE)
                s = nt(k_ref[ks, :], qh)
                dw = nt(v_ref[ks, :], doh)
                square = s * s + 1.0
                inverse = lax.rsqrt(square)
                allowed = key_at + i * TILE >= first
                if i == j:
                    allowed = allowed & causal
                p = jnp.exp(jnp.where(allowed, square * inverse - lse, NEG))
                w = s * inverse * p
                centre = centre + total(w * dw)
                part_buf[h, ks, :] = p * dw * (1.0 + inverse * inverse * (inverse - 1.0))
                weight_buf[h, ks, :] = w
                dv = nn(w.astype(BF), doh)
                if i == j and h == 0:
                    dv_sum[ks, :] = dv
                else:
                    dv_sum[ks, :] += dv
            dq = jnp.zeros((HEAD, TILE), F32)
            for i in range(j + 1):
                ks = slice(i * TILE, (i + 1) * TILE)
                ds = (part_buf[h, ks, :] - weight_buf[h, ks, :] * centre).astype(BF)
                dk = nn(ds, qh)
                if i == j and h == 0:
                    dk_sum[ks, :] = dk
                else:
                    dk_sum[ks, :] += dk
                dq = dq + nn(keys[h * HEAD : (h + 1) * HEAD, ks], ds)
            heads.append(dq)
        dq_ref[qs, :] = (jnp.transpose(jnp.concatenate(heads, 0)) * HEAD**-0.5).astype(BF)
    dk_ref[...] = dk_sum[...].astype(BF)
    dv_ref[...] = dv_sum[...].astype(BF)


def attend_back(place, qkv, own, got, lse, firsts):
    length, columns = qkv.shape
    pairs = columns // 3 // PAIR
    block = lambda part: pl.BlockSpec((length, PAIR), lambda p, s: (0, part * pairs + p))
    half = pl.BlockSpec((length // 2, PAIR), lambda p, s: (0, p))
    shape = jax.ShapeDtypeStruct((length, columns // 3), BF)
    return pl.pallas_call(
        backward_kernel,
        grid_spec=pltpu.PrefetchScalarGridSpec(
            num_scalar_prefetch=1,
            grid=(pairs,),
            in_specs=[
                block(0),
                block(1),
                block(2),
                half,
                half,
                pl.BlockSpec((1, 2, length), lambda p, s: (p, 0, 0)),
                pl.BlockSpec((1, length), lambda p, s: (0, 0)),
            ],
            out_specs=[block(0)] * 3,
            scratch_shapes=[pltpu.VMEM((length, PAIR), F32)] * 2
            + [pltpu.VMEM((2, length, TILE), F32)] * 2
            + [pltpu.VMEM((length, PAIR), BF)],
        ),
        out_shape=[shape] * 3,
        compiler_params=pltpu.CompilerParams(vmem_limit_bytes=60 * MIB),
        cost_estimate=LIGHT,
        name="attention_backward",
    )(place, qkv, qkv, qkv, own, got, lse, firsts)


def half_backward_kernel(phase, place_ref, q_ref, k_ref, v_ref, do_ref, lse_ref, first_ref, *refs):
    sums_in, refs = (refs[:2], refs[2:]) if phase else ((), refs)
    dq_ref, dk_ref, dv_ref, dk_sum, dv_sum, part_buf, weight_buf = refs
    lane = lax.broadcasted_iota(jnp.int32, (1, PAIR), 1)
    keys = jnp.transpose(k_ref[...].astype(F32)).astype(BF)
    key_at = lax.broadcasted_iota(jnp.int32, (TILE, TILE), 0)
    causal = key_at <= lax.broadcasted_iota(jnp.int32, (TILE, TILE), 1)
    if phase:
        dk_sum[...] = sums_in[0][...]
        dv_sum[...] = sums_in[1][...]
    else:
        dk_sum[...] = jnp.zeros_like(dk_sum)
        dv_sum[...] = jnp.zeros_like(dv_sum)

    def rows(j, at):
        qs = slice(j * TILE, (j + 1) * TILE)
        own = slice(at * TILE, (at + 1) * TILE)
        q = q_ref[qs, :] * BF(HEAD**-0.5)
        do = do_ref[own, :]
        first = first_ref[:, qs]
        heads = []
        for h in range(2):
            chosen = (lane >= HEAD) == (h == 1)
            qh = jnp.where(chosen, q, BF(0))
            doh = jnp.where(chosen, do, BF(0))
            lse = lse_ref[0, h : h + 1, qs]
            centre = jnp.zeros((1, TILE), F32)
            for i in range(j + 1):
                ks = slice(i * TILE, (i + 1) * TILE)
                s = nt(k_ref[ks, :], qh)
                dw = nt(v_ref[ks, :], doh)
                square = s * s + 1.0
                inverse = lax.rsqrt(square)
                allowed = key_at + i * TILE >= first
                if i == j:
                    allowed = allowed & causal
                p = jnp.exp(jnp.where(allowed, square * inverse - lse, NEG))
                w = s * inverse * p
                centre = centre + total(w * dw)
                part_buf[h, ks, :] = p * dw * (1.0 + inverse * inverse * (inverse - 1.0))
                weight_buf[h, ks, :] = w
                dv_sum[ks, :] += nn(w.astype(BF), doh)
            dq = jnp.zeros((HEAD, TILE), F32)
            for i in range(j + 1):
                ks = slice(i * TILE, (i + 1) * TILE)
                ds = (part_buf[h, ks, :] - weight_buf[h, ks, :] * centre).astype(BF)
                dk_sum[ks, :] += nn(ds, qh)
                dq = dq + nn(keys[h * HEAD : (h + 1) * HEAD, ks], ds)
            heads.append(dq)
        dq_ref[own, :] = (jnp.transpose(jnp.concatenate(heads, 0)) * HEAD**-0.5).astype(BF)

    later = place_ref[0] == (0 if phase else 1)

    @pl.when(jnp.logical_not(later))
    def _():
        rows(0, 0)
        rows(1, 1)

    @pl.when(later)
    def _():
        rows(2, 0)
        rows(3, 1)

    dk_ref[...] = dk_sum[...].astype(dk_ref.dtype)
    dv_ref[...] = dv_sum[...].astype(dv_ref.dtype)


def attend_back_half(place, phase, qkv, do, lse, firsts, sums=()):
    length, columns = qkv.shape
    pairs = columns // 3 // PAIR
    block = lambda part: pl.BlockSpec((length, PAIR), lambda p, s: (0, part * pairs + p))
    half = pl.BlockSpec((length // 2, PAIR), lambda p, s: (0, p))
    shape = jax.ShapeDtypeStruct
    full = shape((length, columns // 3), BF if phase else F32)
    return pl.pallas_call(
        functools.partial(half_backward_kernel, phase),
        grid_spec=pltpu.PrefetchScalarGridSpec(
            num_scalar_prefetch=1,
            grid=(pairs,),
            in_specs=[
                block(0), block(1), block(2), half,
                pl.BlockSpec((1, 2, length), lambda p, s: (p, 0, 0)),
                pl.BlockSpec((1, length), lambda p, s: (0, 0)),
            ] + [block(0)] * len(sums),
            out_specs=[half, block(0), block(0)],
            scratch_shapes=[pltpu.VMEM((length, PAIR), F32)] * 2 + [pltpu.VMEM((2, length, TILE), F32)] * 2,
        ),
        out_shape=[shape((length // 2, columns // 3), BF), full, full],
        compiler_params=pltpu.CompilerParams(vmem_limit_bytes=60 * MIB),
        cost_estimate=LIGHT,
        name=f"attention_backward_{phase}",
    )(place, qkv, qkv, qkv, do, lse, firsts, *sums)


FF_STEP = 768
OUT_BIAS, GAIN, SHIFT, LAST_BIAS = range(4)
D_OUT_BIAS, D_GAIN, D_SHIFT, D_LAST_BIAS = range(4)


def middle_kernel(
    tok_ref, o_ref, g_ref, wo_ref, w1_ref, w2_ref, b1_ref, vec_ref,
    out_ref, dx_ref, do_ref, gone_ref, gtwo_ref, db1_ref, sums_ref,
    x_buf, h_buf, y_sum, dh_sum,
):
    step = pl.program_id(0)
    last = pl.num_programs(0) - 1

    @pl.when(step == 0)
    def _():
        x = tok_ref[...].astype(F32) + nn(o_ref[...], wo_ref[...]) + vec_ref[OUT_BIAS : OUT_BIAS + 1, :]
        x_buf[...] = x
        hat, _ = normalise(x)
        h_buf[...] = (hat * vec_ref[GAIN : GAIN + 1, :] + vec_ref[SHIFT : SHIFT + 1, :]).astype(BF)
        y_sum[...] = jnp.zeros_like(y_sum)
        dh_sum[...] = jnp.zeros_like(dh_sum)

    @pl.when(step < last)
    def _():
        h = h_buf[...]
        g = g_ref[...]
        u = nn(h, w1_ref[...]) + b1_ref[...]
        root = 0.7978845608028654
        u2 = u * u
        bent = jnp.tanh(root * u * (1.0 + 0.044715 * u2))
        a = (0.5 * u * (1.0 + bent)).astype(BF)
        slope = 0.5 * (1.0 + bent) + 0.5 * u * (1.0 - bent * bent) * (root * (1.0 + 0.134145 * u2))
        y_sum[...] += nn(a, w2_ref[...])
        du = (nt(g, w2_ref[...]) * slope).astype(BF)
        db1_ref[...] = total(du.astype(F32))
        dh_sum[...] += nt(du, w1_ref[...])
        gone_ref[...] = tn(h, du).astype(BF)
        gtwo_ref[...] = tn(a, g).astype(BF)

    @pl.when(step == last)
    def _():
        x = x_buf[...]
        g = g_ref[...].astype(F32)
        out_ref[...] = (x + y_sum[...] + vec_ref[LAST_BIAS : LAST_BIAS + 1, :]).astype(BF)
        hat, inverse = normalise(x)
        dh = dh_sum[...]
        dx = g + norm_grad(dh, hat, inverse, vec_ref[GAIN : GAIN + 1, :])
        dx_ref[...] = dx
        dxr = dx.astype(BF)
        do_ref[...] = nt(dxr, wo_ref[...]).astype(BF)
        gone_ref[...] = tn(o_ref[...], dxr).astype(BF)
        sums_ref[...] = jnp.zeros_like(sums_ref)
        sums_ref[D_OUT_BIAS : D_OUT_BIAS + 1, :] = total(dx)
        sums_ref[D_GAIN : D_GAIN + 1, :] = total(dh * hat)
        sums_ref[D_SHIFT : D_SHIFT + 1, :] = total(dh)
        sums_ref[D_LAST_BIAS : D_LAST_BIAS + 1, :] = total(g)


def middle(tokens, mixture, grad, wo, w1, w2, b1, vectors):
    rows, width = tokens.shape
    hidden = w1.shape[1]
    steps = hidden // FF_STEP
    fixed = lambda r, c: pl.BlockSpec((r, c), lambda i: (0, 0))
    across = lambda r: pl.BlockSpec((r, FF_STEP), lambda i: (0, jnp.minimum(i, steps - 1)))
    down = pl.BlockSpec((FF_STEP, width), lambda i: (jnp.minimum(i, steps - 1), 0))
    return pl.pallas_call(
        middle_kernel,
        grid=(steps + 1,),
        in_specs=[
            fixed(rows, width), fixed(rows, width), fixed(rows, width), fixed(width, width),
            across(width), down, across(1), fixed(*vectors.shape),
        ],
        out_specs=[
            fixed(rows, width), fixed(rows, width), fixed(rows, width),
            pl.BlockSpec((width, FF_STEP), lambda i: (0, i)), down, across(1), fixed(8, width),
        ],
        out_shape=[
            jax.ShapeDtypeStruct((rows, width), BF),
            jax.ShapeDtypeStruct((rows, width), F32),
            jax.ShapeDtypeStruct((rows, width), BF),
            jax.ShapeDtypeStruct((width, hidden + FF_STEP), BF),
            jax.ShapeDtypeStruct((hidden, width), BF),
            jax.ShapeDtypeStruct((1, hidden), F32),
            jax.ShapeDtypeStruct((8, width), F32),
        ],
        scratch_shapes=[
            pltpu.VMEM((rows, width), F32),
            pltpu.VMEM((rows, width), BF),
            pltpu.VMEM((rows, width), F32),
            pltpu.VMEM((rows, width), F32),
        ],
        compiler_params=pltpu.CompilerParams(vmem_limit_bytes=60 * MIB),
        cost_estimate=LIGHT,
        name="feed_forward_both_ways",
    )(tokens, mixture, grad, wo, w1, w2, b1, vectors)


def unproject_kernel(
    place_ref, own_ref, other_ref, dq_ref, dk_ref, dv_ref, weight_ref, keep_ref, send_ref, sums_ref, bias_ref
):
    step = pl.program_id(0)
    mine = (step // 2) == place_ref[0]
    rows = jnp.where(mine, own_ref[...].astype(F32), other_ref[...].astype(F32))
    hat, _ = normalise(rows)
    third = dq_ref.shape[1]
    grad = nt(dq_ref[...], weight_ref[:, :third])
    grad = grad + nt(dk_ref[...], weight_ref[:, third : 2 * third])
    grad = grad + nt(dv_ref[...], weight_ref[:, 2 * third :])

    @pl.when(step == 0)
    def _():
        sums_ref[...] = jnp.zeros_like(sums_ref)
        bias_ref[...] = jnp.zeros_like(bias_ref)

    sums_ref[0:1, :] += total(grad * hat)
    sums_ref[1:2, :] += total(grad)
    bias_ref[0:1, :] += total(dq_ref[...].astype(F32))
    bias_ref[1:2, :] += total(dk_ref[...].astype(F32))
    bias_ref[2:3, :] += total(dv_ref[...].astype(F32))

    @pl.when(mine)
    def _():
        keep_ref[...] = grad

    @pl.when(jnp.logical_not(mine))
    def _():
        send_ref[...] = grad.astype(BF)


def unproject(place, own, other, dq, dk, dv, weight):
    rows, width = own.shape
    third = dq.shape[1]
    step = rows // 2
    half = pl.BlockSpec((step, width), lambda i, s: (i % 2, 0))
    part = pl.BlockSpec((step, third), lambda i, s: (i, 0))
    fixed = lambda r, c: pl.BlockSpec((r, c), lambda i, s: (0, 0))
    return pl.pallas_call(
        unproject_kernel,
        grid_spec=pltpu.PrefetchScalarGridSpec(
            num_scalar_prefetch=1,
            grid=(4,),
            in_specs=[half, half, part, part, part, fixed(*weight.shape)],
            out_specs=[
                pl.BlockSpec((step, width), lambda i, s: (jnp.clip(i - 2 * s[0], 0, 1), 0)),
                pl.BlockSpec((step, width), lambda i, s: (jnp.clip(i - 2 * (1 - s[0]), 0, 1), 0)),
                fixed(8, width),
                fixed(8, third),
            ],
        ),
        out_shape=[
            jax.ShapeDtypeStruct((rows, width), F32),
            jax.ShapeDtypeStruct((rows, width), BF),
            jax.ShapeDtypeStruct((8, width), F32),
            jax.ShapeDtypeStruct((8, third), F32),
        ],
        compiler_params=pltpu.CompilerParams(vmem_limit_bytes=60 * MIB),
        cost_estimate=LIGHT,
        name="grad_at_first_norm",
    )(place, own, other, dq, dk, dv, weight)


def tie(*blocks):
    return lax.optimization_barrier(blocks)


def swap(block, axis):
    return lax.ppermute(block, axis, [(0, 1), (1, 0)])


def general_plan(
    tokens, segment_ids, ln1_gain, ln1_bias, qkv_weight, qkv_bias, out_weight, out_bias,
    ln2_gain, ln2_bias, fc1_weight, fc1_bias, fc2_weight, fc2_bias, output_grad,
):
    outer, inner = lax.axis_size("outer"), lax.axis_size("inner")
    core, side = lax.axis_index("core"), lax.axis_index("side")
    everyone = ("outer", "core", "inner", "side")
    chips = ("outer", "inner", "side")
    rows = tokens.shape[0]
    share = qkv_weight.shape[0]
    place = side.astype(jnp.int32).reshape(1)

    other = swap(tokens, "side")
    other_marks = swap(segment_ids, "side")
    marks = jnp.where(
        side == 0,
        jnp.concatenate([segment_ids, other_marks]),
        jnp.concatenate([other_marks, segment_ids]),
    )
    firsts = sum(jnp.where(marks > v, jnp.sum(marks == v), 0) for v in range(3))
    firsts = firsts.astype(jnp.int32)[None, :]

    parts = qkv_weight.reshape(share, 3, 2, D // 2).transpose(2, 0, 1, 3).reshape(2, share, 3 * D // 2)
    vectors = jnp.concatenate(
        [
            v.reshape(share, -1)
            for v in (ln1_gain, ln1_bias, qkv_bias, out_bias, ln2_gain, ln2_bias, fc1_bias, fc2_bias)
        ],
        1,
    )
    vectors = jnp.pad(vectors, ((0, 0), (0, 128 - vectors.shape[1])))
    parts = jnp.concatenate([parts, jnp.broadcast_to(vectors, (2, share, 128))], 2)
    parts = parts.reshape(2, share, 2, 5 * 128).transpose(2, 0, 1, 3)
    parts = jnp.broadcast_to(parts[None, :, None], (outer, 2, inner, 2, share, 5 * 128))
    got = lax.all_to_all(
        parts.reshape(outer * inner * 4, share, 5 * 128), everyone, split_axis=0, concat_axis=0, tiled=True
    ).reshape(D, 5 * 128)
    twin = swap(got, "core")
    packed = jnp.where(core == 0, jnp.concatenate([got, twin], 1), jnp.concatenate([twin, got], 1))
    w_qkv = packed[:, : 9 * 128]
    table = packed[:, 9 * 128 :].astype(F32)
    column = lambda i: table[:, i][None, :]
    qkv_bias_all = table[:, 2:5].reshape(3, 2, D // 2)
    qkv_bias_mine = lax.dynamic_index_in_dim(qkv_bias_all, side, 1, keepdims=False).reshape(1, -1)
    b1 = table[:, 8:12].reshape(1, -1)
    mid_vectors = jnp.concatenate([column(5), column(6), column(7), column(12)], 0)

    wide = lax.all_gather(jnp.concatenate([fc1_weight, out_weight], 1), everyone, axis=0, tiled=True)
    w2 = lax.all_gather(fc2_weight, everyone, axis=0, tiled=True)
    w1, wo = wide[:, : fc1_weight.shape[1]], wide[:, fc1_weight.shape[1] :]

    normed, qkv = project(place, tokens, other, column(0), column(1), w_qkv, qkv_bias_mine)
    mine, theirs, lse = attend(place, qkv, firsts)
    theirs = swap(theirs, "side")
    mixture = jnp.where(side == 0, jnp.concatenate([mine, theirs], 1), jnp.concatenate([theirs, mine], 1))

    output, dx1, do, grad_wide, grad_two, db1, sums = middle(
        tokens, mixture, output_grad, wo, w1, w2, b1, mid_vectors
    )

    half = D // 2
    do_mine = lax.dynamic_slice_in_dim(do, side * half, half, 1)
    do_theirs = swap(lax.dynamic_slice_in_dim(do, (1 - side) * half, half, 1), "side")

    def reduce_rows(grad):
        width = grad.shape[1]
        pieces = grad.reshape(outer, 2, inner * 2, grad.shape[0] // (4 * outer * inner), width)
        keep = lax.dynamic_index_in_dim(pieces, core, 1, keepdims=False)
        send = lax.dynamic_index_in_dim(pieces, 1 - core, 1, keepdims=False)
        both = (keep.astype(F32) + swap(send, "core").astype(F32)).astype(BF)
        both = both.reshape((outer * inner * 2,) + both.shape[2:])
        return lax.all_to_all(both, chips, split_axis=0, concat_axis=0, tiled=True)

    wide_total = jnp.sum(reduce_rows(grad_wide).astype(F32), 0)
    two_total = jnp.sum(reduce_rows(grad_two).astype(F32), 0)

    dq, dk, dv = attend_back(place, qkv, do_mine, do_theirs, lse, firsts)
    kept, sent, first_sums, bias_sums = unproject(place, tokens, other, dq, dk, dv, w_qkv)
    back = swap(sent, "side")
    grad_qkv = jnp.concatenate([tn(normed, d).astype(BF) for d in (dq, dk, dv)], 1)
    bias_mine = jnp.zeros((3, 2, half), F32)
    bias_mine = lax.dynamic_update_slice(bias_mine, bias_sums[:3][:, None], (0, side, 0)).reshape(-1)
    small = jnp.concatenate(
        [
            v.reshape(D, -1)
            for v in (
                first_sums[0], first_sums[1], bias_mine, sums[D_OUT_BIAS], sums[D_GAIN],
                sums[D_SHIFT], db1, sums[D_LAST_BIAS],
            )
        ],
        1,
    )
    small = jnp.pad(small, ((0, 0), (0, 128 - small.shape[1]))).astype(BF)
    tail = reduce_rows(jnp.concatenate([grad_qkv, small], 1)).astype(F32)
    tail = tail.reshape(outer * inner, 2, share, 10 * 128)
    qkv_total = jnp.sum(tail[..., : 9 * 128], 0).reshape(2, share, 3, half)
    qkv_total = qkv_total.transpose(1, 2, 0, 3).reshape(share, 3 * D)
    small_total = jnp.sum(tail[..., 9 * 128 :], (0, 1))
    pick = lambda i, n=1: small_total[:, i : i + n].reshape(-1)

    hat, inverse = normalise(tokens.astype(F32))
    input_grad = dx1 + norm_grad(kept + back.astype(F32), hat, inverse, column(0))
    hidden = fc1_weight.shape[1]
    return (
        output,
        input_grad,
        pick(0),
        pick(1),
        qkv_total,
        pick(2, 3),
        wide_total[:, hidden:],
        pick(5),
        pick(6),
        pick(7),
        wide_total[:, :hidden],
        pick(8, 4),
        two_total,
        pick(12),
    )


SHARE = 24
FF_SHARE = 96
FF_HALF = 8 * FF_SHARE


def pack_kernel(weight_ref, *refs):
    *vector_refs, out_ref, buf = refs
    half = D // 2
    buf[...] = jnp.zeros_like(buf)
    for i, ref in enumerate(vector_refs):
        buf[i : i + 1, : ref.shape[1]] = ref[...].astype(F32)
    vectors = buf[...].astype(BF)
    for x in range(2):
        q, k, v = (weight_ref[:, part * D + x * half : part * D + (x + 1) * half] for part in range(3))
        low = jnp.concatenate([q, k[:, :256]], 1)
        high = jnp.concatenate([k[:, 256:], v, vectors], 1)
        for y in range(2):
            for z in range(4):
                out_ref[((2 * y) * 4 + z) * 2 + x] = low
                out_ref[((2 * y + 1) * 4 + z) * 2 + x] = high


def pack(weight, vectors):
    share = weight.shape[0]
    return pl.pallas_call(
        pack_kernel,
        out_shape=jax.ShapeDtypeStruct((32, share, 640), BF),
        scratch_shapes=[pltpu.VMEM((share, 128), F32)],
        compiler_params=pltpu.CompilerParams(vmem_limit_bytes=60 * MIB),
        name="pack_qkv_weights",
    )(weight, *(v.reshape(1, -1) for v in vectors))


ALL_VECTORS = 8
GAIN_ONE, SHIFT_ONE, QKV_BIAS = 0, 1, 2


def spread(rows, where, count):
    lanes = lax.broadcasted_iota(jnp.int32, (128, where.shape[1]), 0)
    chosen = jnp.where(lanes == where[1:2, :], 1.0, 0.0).astype(BF)
    found = nn(rows.astype(BF), chosen)
    devices = rows.shape[0] // count
    owners = lax.broadcasted_iota(jnp.int32, (devices, where.shape[1]), 0) == where[0:1, :]
    return jnp.concatenate(
        [total(jnp.where(owners, found[i * devices : (i + 1) * devices], 0.0)) for i in range(count)], 0
    )


def places(each, numbers):
    numbers = np.asarray(numbers)
    return np.stack([numbers // each, numbers % each]).astype(np.int32)


def plane_project_kernel(
    ids_ref, own_ref, other_ref, got_ref, twin_ref, at_d_ref, at_qkv_ref,
    normed_ref, qkv_ref, weight_ref, vec_ref, table, bias,
):
    @pl.when(pl.program_id(0) == 0)
    def _():
        first = ids_ref[1] == 0
        got, twin = got_ref[...], twin_ref[...]
        weight_ref[:, :640] = jnp.where(first, got, twin)
        high = jnp.where(first, twin, got)
        weight_ref[:, 640:] = high[:, :512]
        table[...] = high[:, 512:].astype(F32)
        rows = lambda i: table[pl.ds(i, 32, stride=SHARE), :]
        bias[...] = spread(rows(QKV_BIAS), at_qkv_ref[0], 1)
        vec_ref[...] = spread(jnp.concatenate([rows(GAIN_ONE), rows(SHIFT_ONE)], 0), at_d_ref[...], 2)

    mine = (pl.program_id(0) // 2) == ids_ref[3]
    rows = jnp.where(mine, own_ref[...], other_ref[...]).astype(F32)
    hat, _ = normalise(rows)
    normed = (hat * vec_ref[0:1, :] + vec_ref[1:2, :]).astype(BF)
    normed_ref[...] = normed
    qkv_ref[...] = (nn(normed, weight_ref[...]) + bias[...]).astype(BF)


def plane_project(ids, own, other, got, twin):
    rows, width = own.shape
    columns = 3 * width // 2
    step = rows // 2
    at_d = places(SHARE, range(width))
    at_qkv = [
        places(3 * SHARE, [part * width + x * width // 2 + m for part in range(3) for m in range(width // 2)])
        for x in range(2)
    ]
    at_qkv = jnp.stack([jnp.asarray(a) for a in at_qkv])
    half = pl.BlockSpec((step, width), lambda i, s: (i % 2, 0))
    fixed = lambda r, c: pl.BlockSpec((r, c), lambda i, s: (0, 0))
    return pl.pallas_call(
        plane_project_kernel,
        grid_spec=pltpu.PrefetchScalarGridSpec(
            num_scalar_prefetch=1,
            grid=(4,),
            in_specs=[
                half, half, fixed(*got.shape), fixed(*got.shape), fixed(2, width),
                pl.BlockSpec((1, 2, columns), lambda i, s: (s[3], 0, 0)),
            ],
            out_specs=[
                pl.BlockSpec((step, width), lambda i, s: (i, 0)),
                pl.BlockSpec((step, columns), lambda i, s: (i, 0)),
                fixed(width, columns),
                fixed(2, width),
            ],
            scratch_shapes=[pltpu.VMEM((width, 128), F32), pltpu.VMEM((1, columns), F32)],
        ),
        out_shape=[
            jax.ShapeDtypeStruct((2 * rows, width), BF),
            jax.ShapeDtypeStruct((2 * rows, columns), BF),
            jax.ShapeDtypeStruct((width, columns), BF),
            jax.ShapeDtypeStruct((2, width), F32),
        ],
        compiler_params=pltpu.CompilerParams(vmem_limit_bytes=60 * MIB),
        cost_estimate=LIGHT,
        name="norm_and_qkv",
    )(ids, own, other, got, twin, jnp.asarray(at_d), at_qkv)


def middle_vectors_kernel(ids_ref, got_ref, twin_ref, at_d_ref, at_ff_ref, vec_ref, b1_ref, table):
    table[...] = jnp.where(ids_ref[1] == 0, twin_ref[...], got_ref[...]).astype(F32)
    rows = lambda i: table[pl.ds(i, 32, stride=SHARE), :]
    vec_ref[...] = spread(jnp.concatenate([rows(i) for i in (3, 4, 5, 7)], 0), at_d_ref[...], 4)
    b1_ref[...] = spread(rows(6), at_ff_ref[...], 1)


def middle_vectors(ids, got, twin):
    width, hidden = got.shape[0], 4 * got.shape[0]
    at_d, at_ff = jnp.asarray(places(SHARE, range(width))), jnp.asarray(places(FF_SHARE, range(hidden)))
    last = pl.BlockSpec((width, 128), lambda i, s: (0, 4))
    fixed = lambda r, c: pl.BlockSpec((r, c), lambda i, s: (0, 0))
    return pl.pallas_call(
        middle_vectors_kernel,
        grid_spec=pltpu.PrefetchScalarGridSpec(
            num_scalar_prefetch=1,
            grid=(1,),
            in_specs=[last, last, fixed(2, width), fixed(2, hidden)],
            out_specs=[fixed(4, width), fixed(1, hidden)],
            scratch_shapes=[pltpu.VMEM((width, 128), F32)],
        ),
        out_shape=[jax.ShapeDtypeStruct((4, width), F32), jax.ShapeDtypeStruct((1, hidden), F32)],
        compiler_params=pltpu.CompilerParams(vmem_limit_bytes=60 * MIB),
        cost_estimate=LIGHT,
        name="middle_vectors",
    )(ids, got, twin, at_d, at_ff)


def out_project_kernel(ids_ref, tok_ref, own_ref, got_ref, wo_own_ref, wo_got_ref, vec_ref, x_ref, h_ref):
    x = tok_ref[...].astype(F32) + nn(own_ref[...], wo_own_ref[...]) + nn(got_ref[...], wo_got_ref[...])
    x = x + vec_ref[OUT_BIAS : OUT_BIAS + 1, :]
    x_ref[...] = x
    hat, _ = normalise(x)
    h_ref[...] = (hat * vec_ref[GAIN : GAIN + 1, :] + vec_ref[SHIFT : SHIFT + 1, :]).astype(BF)


def out_project(ids, tokens, own, got, wide, vectors):
    rows, width = tokens.shape
    half = width // 2
    step = rows // 2
    tile = lambda c: pl.BlockSpec((step, c), lambda i, s: (i, 0))
    return pl.pallas_call(
        out_project_kernel,
        grid_spec=pltpu.PrefetchScalarGridSpec(
            num_scalar_prefetch=1,
            grid=(2,),
            in_specs=[
                tile(width), tile(half), tile(half),
                pl.BlockSpec((half, width), lambda i, s: (s[3], wide.shape[1] // width - 1)),
                pl.BlockSpec((half, width), lambda i, s: (1 - s[3], wide.shape[1] // width - 1)),
                pl.BlockSpec(vectors.shape, lambda i, s: (0, 0)),
            ],
            out_specs=[tile(width), tile(width)],
        ),
        out_shape=[jax.ShapeDtypeStruct((rows, width), F32), jax.ShapeDtypeStruct((rows, width), BF)],
        compiler_params=pltpu.CompilerParams(vmem_limit_bytes=60 * MIB),
        cost_estimate=LIGHT,
        name="out_projection_and_second_norm",
    )(ids, tokens, own, got, wide, wide, vectors)


def gelu_both(u):
    root = 0.7978845608028654
    u2 = u * u
    bent = jnp.tanh(u * (root + (root * 0.044715) * u2))
    c = 0.5 * bent + 0.5
    a = u * c
    slope = c + a * (1.0 - bent) * (root + (root * 0.134145) * u2)
    return a.astype(BF), slope


FF_ROWS = 512


def feed_forward_kernel(plane, ids_ref, *refs):
    h_own_hbm, h_sib_hbm, g_own_hbm, g_sib_hbm, wide_hbm, own_hbm, far_hbm, b1_ref, *refs = refs
    earlier, refs = (refs[:2], refs[2:]) if plane else ((), refs)
    outs, db1_ref, refs = refs[:9], refs[9], refs[10:]
    h, g, w1, own, far, w2, y_all, dh_all, one, a_all, du_all, y_sib, dh_sib, *refs = refs
    q00, q10, q01, q11, two, *refs = refs
    y_old, dh_old, in_sems, out_sems = refs if plane else (None, None, *refs)
    my_y, my_c, my_z, my_x = (ids_ref[i] for i in range(4))
    unit = FF_SHARE
    rows = h_own_hbm.shape[0]

    column = pl.multiple_of(((my_y ^ plane) * 2 + my_c) * FF_HALF, FF_HALF)
    sources = [
        (wide_hbm.at[:, pl.ds(column, FF_HALF)], w1), (own_hbm, own), (far_hbm, far), (h_own_hbm, h.at[:rows]),
        (g_own_hbm, g.at[:rows]), (h_sib_hbm, h.at[rows:]), (g_sib_hbm, g.at[rows:]),
    ]
    if plane:
        sources += [(earlier[0], y_old), (earlier[1], dh_old)]
    loads = [pltpu.make_async_copy(src, dst, in_sems.at[i]) for i, (src, dst) in enumerate(sources)]
    for load in loads:
        load.start()
    for load in loads[:3]:
        load.wait()
    for z in range(4):
        near, distant = own[z ^ my_z], far[z ^ my_z]
        w2[2 * z * unit : (2 * z + 1) * unit, :] = jnp.where(my_x == 0, near, distant)
        w2[(2 * z + 1) * unit : (2 * z + 2) * unit, :] = jnp.where(my_x == 0, distant, near)
    for load in loads[3:5]:
        load.wait()

    def one_pass(i, carry):
        if FF_ROWS == rows:
            sib_next = i == 1
        else:
            sib_next = i * FF_ROWS == rows

        @pl.when(sib_next)
        def _():
            for load in loads[5:7]:
                load.wait()

        at = pl.ds(pl.multiple_of(i * FF_ROWS, FF_ROWS), FF_ROWS)
        hr, gr = h[at, :], g[at, :]
        a, slope = gelu_both(nn(hr, w1[...]) + b1_ref[...])
        du = (nt(gr, w2[...]) * slope).astype(BF)
        a_all[at, :] = a
        du_all[at, :] = du
        dh_all[at, :] = nt(du, w1[...])
        y_all[at, :] = nn(a, w2[...])
        return carry + total(du.astype(F32))

    db1_ref[...] = lax.fori_loop(0, 2 * rows // FF_ROWS, one_pass, jnp.zeros(db1_ref.shape, F32))

    stores = []

    def store(src, at):
        copy = pltpu.make_async_copy(src, outs[at], out_sems.at[at])
        copy.start()
        stores.append(copy)

    dh_sib[...] = dh_all[rows:, :].astype(BF)
    store(dh_sib, 3)
    if plane:
        for load in loads[7:]:
            load.wait()
        dh_all[:rows, :] += dh_old[...]
        y_all[:rows, :] += y_old[...]
    store(dh_all.at[:rows], 2)
    store(y_all.at[:rows], 0)
    y_sib[...] = y_all[rows:, :].astype(BF)
    store(y_sib, 1)

    one[...] = tn(h[...], du_all[...])
    two[...] = tn(a_all[...], g[...]).astype(BF)
    store(two, 8)
    for xr, yr, ref, at in ((1, 0, q10, 5), (1, 1, q11, 7), (0, 1, q01, 6), (0, 0, q00, 4)):
        half, share_at = my_y ^ yr, my_x ^ xr
        for z in range(4):
            parts = []
            for c in range(2):
                start = half * (16 * SHARE) + share_at * SHARE + (c * 4 + z) * 2 * SHARE
                parts.append(one[pl.ds(pl.multiple_of(start, 8), SHARE), :])
            ref[2 * z * SHARE : 2 * (z + 1) * SHARE, :] = jnp.concatenate(parts, 0).astype(BF)
        store(ref, at)
    for copy in stores:
        copy.wait()


def feed_forward(ids, plane, h_own, h_sib, g_own, g_sib, wide, own, far, b1, earlier=()):
    rows, width = h_own.shape
    anywhere = pl.BlockSpec(memory_space=pl.ANY)
    shape = jax.ShapeDtypeStruct
    f32, bf = shape((rows, width), F32), shape((rows, width), BF)
    pieces = [shape((8 * SHARE, width), BF)] * 4
    pieces += [shape((FF_HALF, width), BF)]
    held = lambda s: pltpu.VMEM(s.shape, s.dtype)
    scratch = [pltpu.VMEM((2 * rows, width), BF)] * 2
    scratch += [pltpu.VMEM((width, FF_HALF), BF), held(own), held(far), pltpu.VMEM((FF_HALF, width), BF)]
    scratch += [pltpu.VMEM((2 * rows, width), F32)] * 2 + [pltpu.VMEM((width, FF_HALF), F32)]
    scratch += [pltpu.VMEM((2 * rows, FF_HALF), BF)] * 2
    scratch += [held(bf)] * 2 + [held(s) for s in pieces]
    scratch += [held(f32)] * 2 if plane else []
    scratch += [pltpu.SemaphoreType.DMA((9,)), pltpu.SemaphoreType.DMA((9,))]
    return pl.pallas_call(
        functools.partial(feed_forward_kernel, plane),
        grid_spec=pltpu.PrefetchScalarGridSpec(
            num_scalar_prefetch=1,
            grid=(1,),
            in_specs=[anywhere] * 7
            + [pl.BlockSpec((1, FF_HALF), lambda i, s: (0, (s[0] ^ plane) * 2 + s[1]))]
            + [anywhere] * len(earlier),
            out_specs=[anywhere] * 9 + [pl.BlockSpec((1, FF_HALF), lambda i, s: (0, 0))],
            scratch_shapes=scratch,
        ),
        out_shape=[f32, bf, f32, bf] + pieces + [shape((1, FF_HALF), F32)],
        compiler_params=pltpu.CompilerParams(vmem_limit_bytes=60 * MIB),
        cost_estimate=LIGHT,
        name=f"feed_forward_both_ways_{plane}",
    )(ids, h_own, h_sib, g_own, g_sib, wide, own, far, b1, *earlier)


def second_norm_kernel(
    ids_ref, x_ref, dh_ref, dh0_ref, dh1_ref, g_ref, wo_ref, vec_ref, dx_ref, dxr_ref, do_own_ref, do_send_ref, sums
):
    x = x_ref[...]
    g = g_ref[...].astype(F32)
    hat, inverse = normalise(x)
    dh = dh_ref[...] + dh0_ref[...].astype(F32) + dh1_ref[...].astype(F32)
    dx = g + norm_grad(dh, hat, inverse, vec_ref[GAIN : GAIN + 1, :])
    dx_ref[...] = dx
    dxr = dx.astype(BF)
    dxr_ref[...] = dxr
    half = wo_ref.shape[0] // 2
    mine = pl.ds(pl.multiple_of(ids_ref[3] * half, half), half)
    theirs = pl.ds(pl.multiple_of((1 - ids_ref[3]) * half, half), half)
    do_send_ref[...] = nt(dxr, wo_ref[theirs, :]).astype(BF)
    do_own_ref[...] = nt(dxr, wo_ref[mine, :]).astype(BF)

    @pl.when(pl.program_id(0) == 0)
    def _():
        sums[...] = jnp.zeros_like(sums)

    sums[D_OUT_BIAS : D_OUT_BIAS + 1, :] += total(dx)
    sums[D_GAIN : D_GAIN + 1, :] += total(dh * hat)
    sums[D_SHIFT : D_SHIFT + 1, :] += total(dh)
    sums[D_LAST_BIAS : D_LAST_BIAS + 1, :] += total(g)


def second_norm_back(ids, x, dh, dh0, dh1, g, wide, vectors):
    rows, width = x.shape
    step = rows // 2
    tile = lambda c: pl.BlockSpec((step, c), lambda i, s: (i, 0))
    shape = jax.ShapeDtypeStruct
    half = width // 2
    return pl.pallas_call(
        second_norm_kernel,
        grid_spec=pltpu.PrefetchScalarGridSpec(
            num_scalar_prefetch=1,
            grid=(2,),
            in_specs=[tile(width)] * 5
            + [
                pl.BlockSpec((width, width), lambda i, s: (0, wide.shape[1] // width - 1)),
                pl.BlockSpec(vectors.shape, lambda i, s: (0, 0)),
            ],
            out_specs=[tile(width), tile(width), tile(half), tile(half), pl.BlockSpec((8, width), lambda i, s: (0, 0))],
        ),
        out_shape=[
            shape((rows, width), F32), shape((rows, width), BF), shape((rows, half), BF),
            shape((rows, half), BF), shape((8, width), F32),
        ],
        compiler_params=pltpu.CompilerParams(vmem_limit_bytes=60 * MIB),
        cost_estimate=LIGHT,
        name="second_norm_back",
    )(ids, x, dh, dh0, dh1, g, wide, vectors)


def out_weight_kernel(
    ids_ref, dxr_ref, o_own_ref, o_got_ref, sums_ref, near_ref, far_ref, keep_ref, send_ref, gwo
):
    width = dxr_ref.shape[1]
    half = width // 2
    mine = pl.ds(pl.multiple_of(ids_ref[3] * half, half), half)
    theirs = pl.ds(pl.multiple_of((1 - ids_ref[3]) * half, half), half)
    gwo[mine, :] = tn(o_own_ref[...], dxr_ref[...]).astype(BF)
    gwo[theirs, :] = tn(o_got_ref[...], dxr_ref[...]).astype(BF)
    lane = lax.broadcasted_iota(jnp.int32, (width, 128), 1)
    columns = jnp.transpose(sums_ref[...])
    table = jnp.zeros((width, 128), F32)
    for i in range(4):
        table = table + jnp.where(lane == i, columns[:, i : i + 1], 0.0)
    block = width // 4
    first, low = ids_ref[1] == 0, ids_ref[0] == 0
    near = jnp.transpose(jnp.broadcast_to(near_ref[...], (8, width)))[:, :1]
    far = jnp.transpose(jnp.broadcast_to(far_ref[...], (8, width)))[:, :1]
    halves = (jnp.where(low, near, far), jnp.where(low, far, near))
    for j in range(4):
        cut = lambda h: jnp.concatenate([h[k * FF_SHARE + j * SHARE :][:SHARE] for k in range(width // FF_SHARE)], 0)
        zero = jnp.zeros((block, 1), F32)
        column = []
        for h in halves:
            column += [jnp.where(first, cut(h), zero), jnp.where(first, zero, cut(h))]
        table = table + jnp.where(lane == 4 + j, jnp.concatenate(column, 0), 0.0)
    table = table.astype(BF)
    size = 2 * SHARE
    for y in range(2):
        for z in range(4):
            to = slice((z * 2 + y) * size, (z * 2 + y + 1) * size)
            for ref, here in ((keep_ref, ids_ref[1]), (send_ref, 1 - ids_ref[1])):
                start = pl.multiple_of(here * 4 * size + (y * 8 + z) * size, 16)
                ref[to, :width] = gwo[pl.ds(start, size), :]
            cut = lambda c: table[((y * 2 + c) * 4 + z) * size :][:size]
            keep_ref[to, width:] = jnp.where(first, cut(0), cut(1))
            send_ref[to, width:] = jnp.where(first, cut(1), cut(0))


def out_weight_grad(ids, dxr, o_own, o_got, sums, near, far):
    width = dxr.shape[1]
    whole = lambda a: pl.BlockSpec(a.shape, lambda i, s: (0, 0))
    out = jax.ShapeDtypeStruct((width // 2, width + 128), BF)
    args = (dxr, o_own, o_got, sums, near, far)
    return pl.pallas_call(
        out_weight_kernel,
        grid_spec=pltpu.PrefetchScalarGridSpec(
            num_scalar_prefetch=1, grid=(1,), in_specs=[whole(a) for a in args], out_specs=[whole(out)] * 2,
            scratch_shapes=[pltpu.VMEM((width, width), BF)],
        ),
        out_shape=[out, out],
        compiler_params=pltpu.CompilerParams(vmem_limit_bytes=60 * MIB),
        cost_estimate=LIGHT,
        name="out_weight_grad",
    )(ids, *args)


def qkv_back_kernel(
    ids_ref, h_ref, own_ref, other_ref, dk_ref, dv_ref, weight_ref, vec_ref,
    keep_ref, send_ref, dh_keep_ref, dh_send_ref, full,
):
    first = ids_ref[1] == 0
    width = h_ref.shape[1]
    block = width // 4
    third = dk_ref.shape[1]
    lower = ids_ref[3] == 0
    own, other = own_ref[...], other_ref[...]
    dq = jnp.concatenate([jnp.where(lower, own, other), jnp.where(lower, other, own)], 0)
    grads = jnp.concatenate([dq, dk_ref[...], dv_ref[...]], 1)
    weight = weight_ref[...]
    full[...] = tn(h_ref[...], grads)

    vectors = jnp.transpose(jnp.concatenate([vec_ref[...]] * 4, 0))
    gain, shift = vectors[:, 0:1], vectors[:, 1:2]
    sums = total(grads.astype(F32))
    by_shift = nt(weight, jnp.broadcast_to(sums, (8, 3 * third)).astype(BF))[:, :1]
    by_gain = (jnp.sum(weight.astype(F32) * full[...], 1, keepdims=True) - shift * by_shift) / gain
    place = lax.broadcasted_iota(jnp.int32, (width, third), 1) - 3 * lax.broadcasted_iota(jnp.int32, (width, third), 0)
    chosen = []
    for part in range(3):
        low = -(part * width + ids_ref[3] * third)
        here = (place >= low) & (place < low + 3)
        chosen.append(jnp.where(here, sums[:, part * third : (part + 1) * third], 0.0).astype(BF))
    row = lax.broadcasted_iota(jnp.int32, (3 * third, 128), 0)
    spots = jnp.where(lax.rem(row, 3) + 2 == lax.broadcasted_iota(jnp.int32, (3 * third, 128), 1), 1.0, 0.0).astype(BF)
    table = nn(jnp.concatenate(chosen, 1), spots)
    lane = lax.broadcasted_iota(jnp.int32, (width, 128), 1)
    table = table + jnp.where(lane == 0, by_gain, 0.0) + jnp.where(lane == 1, by_shift, 0.0)

    table = table.astype(BF)
    for y in range(2):
        at = slice(y * block, (y + 1) * block)
        low, high = table[2 * y * block :][:block], table[(2 * y + 1) * block :][:block]
        keep_ref[at, 3 * third :] = jnp.where(first, low, high)
        send_ref[at, 3 * third :] = jnp.where(first, high, low)
        for ref, here in ((keep_ref, ids_ref[1]), (send_ref, 1 - ids_ref[1])):
            start = pl.multiple_of(here * block + 2 * y * block, 16)
            ref[at, : 3 * third] = full[pl.ds(start, block), :].astype(BF)

    dh = nt(grads, weight)
    rows = dh_keep_ref.shape[0]
    mine = ids_ref[3] == 0
    dh_keep_ref[...] = jnp.where(mine, dh[:rows], dh[rows:])
    dh_send_ref[...] = jnp.where(mine, dh[rows:], dh[:rows]).astype(BF)


def qkv_back(ids, normed, dq_own, dq_other, dk, dv, weight, vectors):
    rows, width = normed.shape
    third = dk.shape[1]
    shape = jax.ShapeDtypeStruct
    whole = lambda a: pl.BlockSpec(a.shape, lambda i, s: (0, 0))
    part = shape((width // 2, 3 * third + 128), BF)
    outs = [part, part, shape((rows // 2, width), F32), shape((rows // 2, width), BF)]
    args = (normed, dq_own, dq_other, dk, dv, weight, vectors)
    return pl.pallas_call(
        qkv_back_kernel,
        grid_spec=pltpu.PrefetchScalarGridSpec(
            num_scalar_prefetch=1, grid=(1,), in_specs=[whole(a) for a in args], out_specs=[whole(o) for o in outs],
            scratch_shapes=[pltpu.VMEM((width, 3 * third), F32)],
        ),
        out_shape=outs,
        compiler_params=pltpu.CompilerParams(vmem_limit_bytes=60 * MIB),
        cost_estimate=LIGHT,
        name="qkv_back",
    )(ids, *args)


def tail_kernel(tail_ref, qkv_ref, small_ref):
    half = D // 2
    small = jnp.zeros((SHARE, 128), F32)
    for x in range(2):
        sums = jnp.zeros((SHARE, 3 * half + 128), F32)
        for i in range(4):
            sums = sums + tail_ref[2 * i + x].astype(F32)
        for part in range(3):
            qkv_ref[:, part * D + x * half : part * D + (x + 1) * half] = sums[:, part * half : (part + 1) * half]
        small = small + sums[:, 3 * half :]
    small_ref[...] = small


def sum_tail(tail):
    shape = jax.ShapeDtypeStruct
    return pl.pallas_call(
        tail_kernel,
        out_shape=[shape((SHARE, 3 * D), F32), shape((SHARE, 128), F32)],
        compiler_params=pltpu.CompilerParams(vmem_limit_bytes=60 * MIB),
        cost_estimate=HEAVY,
        name="sum_of_qkv_gradients",
    )(tail)


def plane_plan(
    tokens, segment_ids, ln1_gain, ln1_bias, qkv_weight, qkv_bias, out_weight, out_bias,
    ln2_gain, ln2_bias, fc1_weight, fc1_bias, fc2_weight, fc2_bias, output_grad,
):
    outer, inner = lax.axis_size("outer"), lax.axis_size("inner")
    core, side = lax.axis_index("core"), lax.axis_index("side")
    deep, line = lax.axis_index("outer"), lax.axis_index("inner")
    everyone = ("outer", "core", "inner", "side")
    chips = ("outer", "inner", "side")
    share = qkv_weight.shape[0]
    half = D // 2
    ids = jnp.stack([deep, core, line, side]).astype(jnp.int32)
    place = side.astype(jnp.int32).reshape(1)
    along = lambda block, d: lax.ppermute(block, "inner", [(i, i ^ d) for i in range(inner)])
    across = lambda block, d: lax.ppermute(block, ("outer", "side"), [(i, i ^ d) for i in range(4)])

    wide = lax.all_gather(jnp.concatenate([fc1_weight, out_weight], 1), everyone, axis=0, tiled=True)

    other_marks = swap(segment_ids, "side")
    marks = jnp.where(
        side == 0,
        jnp.concatenate([segment_ids, other_marks]),
        jnp.concatenate([other_marks, segment_ids]),
    )
    firsts = sum(jnp.where(marks > v, jnp.sum(marks == v), 0) for v in range(3))
    firsts = firsts.astype(jnp.int32)[None, :]
    late_tokens, _, ids = tie(tokens, other_marks, ids)
    other = swap(late_tokens, "side")

    named = (ln1_gain, ln1_bias, qkv_bias, out_bias, ln2_gain, ln2_bias, fc1_bias, fc2_bias)
    parts = pack(qkv_weight, named)
    got = lax.all_to_all(parts, everyone, split_axis=0, concat_axis=0, tiled=True).reshape(D, 640)
    got, other, firsts = tie(got, other, firsts)
    twin = swap(got, "core")

    _, down = tie(got, fc2_weight)
    lined = [along(down, d) for d in range(1, inner)]

    normed, qkv, w_qkv, first_vectors = plane_project(ids, tokens, other, got, twin)
    gain_one = first_vectors[:1]
    o_own, o_send, lse = attend(place, qkv, firsts, 0, 2)
    o_own, qkv, *lined = tie(o_own, qkv, *lined)
    stacked = jnp.stack([down, *lined])
    o_own_last, o_send_last, lse_last = attend(place, qkv, firsts, 2, 3)
    o_own = jnp.concatenate([o_own, o_own_last], 1)
    lse = jnp.concatenate([lse, lse_last], 0)
    o_got = swap(jnp.concatenate([o_send, o_send_last], 1), "side")
    o_got, far_x, far_y = tie(o_got, across(stacked, 1), across(stacked, 2))
    far_xy = across(far_x, 2)
    g_sib = swap(output_grad, "core")
    mid_vectors, b1 = middle_vectors(ids, *tie(got, twin, o_own)[:2])
    x1, h_own = out_project(ids, tokens, o_own, o_got, wide, mid_vectors)
    h_sib = swap(h_own, "core")

    acts = (h_own, h_sib, output_grad, g_sib, wide)
    y0, y0_sib, dh0, dh0_sib, a00, a10, a01, a11, two_near, db1_near = feed_forward(
        ids, 0, *acts, stacked, far_x, b1
    )
    line = lambda block: lax.psum_scatter(block, "inner", scatter_dimension=0, tiled=True)
    dh0_got, y0_got = swap(dh0_sib, "core"), swap(y0_sib, "core")
    got_a10, got_a01, got_a11 = across(a10, 1), across(a01, 2), across(a11, 3)
    far_y, far_xy, dh0, two_near = tie(far_y, far_xy, dh0, two_near)
    two_near = line(two_near)
    y, y_send, dh, dh_send, b00, b10, b01, b11, two_far, db1_far = feed_forward(
        ids, 1, *acts, far_y, far_xy, b1, (y0, dh0)
    )
    dh_send, got_a10, got_a01, got_a11 = tie(dh_send, got_a10, got_a01, got_a11)
    dh_got, y_got = swap(dh_send, "core"), swap(y_send, "core")
    dh_got, dh0_got, y0_got, two_far = tie(dh_got, dh0_got, y0_got, two_far)
    two_far = line(two_far)
    dx1, dxr, do_own, do_send, sums = second_norm_back(
        ids, x1, dh, dh0_got, dh_got, output_grad, wide, mid_vectors
    )
    do_got = swap(do_send, "side")
    parts = (x1, y, y0_got.astype(F32), y_got.astype(F32), mid_vectors[LAST_BIAS : LAST_BIAS + 1])
    output = sum(parts).astype(BF)
    out_keep, out_send = out_weight_grad(ids, dxr, o_own, o_got, sums, db1_near, db1_far)

    out_got = swap(out_send, "core")
    out_got, b10, b01, b11 = tie(out_got, b10, b01, b11)
    out_both = (out_keep.astype(F32) + out_got.astype(F32)).astype(BF).reshape(inner, 4 * share, -1)
    got_b10, got_b01, got_b11 = across(b10, 1), across(b01, 2), across(b11, 3)

    dq_own, *dkv = attend_back_half(place, 0, qkv, do_own, lse, firsts)
    dq_other, dk, dv = attend_back_half(place, 1, qkv, do_got, lse, firsts, dkv)
    dq_other, got_b10, got_b01, got_b11 = tie(dq_other, got_b10, got_b01, got_b11)
    qkv_keep, qkv_send, kept, sent = qkv_back(ids, normed, dq_own, dq_other, dk, dv, w_qkv, first_vectors)
    qkv_send, two_near, two_far = tie(qkv_send, two_near, two_far)
    both = (qkv_keep.astype(F32) + swap(qkv_send, "core").astype(F32)).astype(BF)
    both = both.reshape(outer, D // 4, -1)
    mine, theirs = (lax.dynamic_index_in_dim(both, at, 0, keepdims=False) for at in (deep, 1 - deep))
    both = (mine.astype(F32) + across(theirs, 2).astype(F32)).astype(BF)
    tail = lax.all_to_all(
        both.reshape(inner * 2, share, -1), ("inner", "side"), split_axis=0, concat_axis=0, tiled=True
    )
    back = swap(sent, "side")

    add = lambda *parts: sum(p.astype(F32) for p in parts).astype(BF).reshape(inner, -1, D)
    plane_sum = jnp.concatenate([add(a00, got_a10, got_b01, got_b11), add(b00, got_b10, got_a01, got_a11)], 1)
    joined = jnp.concatenate([jnp.pad(plane_sum, ((0, 0), (0, 0), (0, 128))), out_both], 1)
    joined = line(joined.reshape(8 * inner * share, D + 128))
    one_sum, out_line = joined[: 4 * share, :D].astype(F32), joined[4 * share :]
    tail, back, one_sum = tie(tail, back, one_sum)
    near, far = one_sum[: 2 * share], one_sum[2 * share :]
    one_parts = jnp.where(deep == 0, jnp.stack([near, far]), jnp.stack([far, near])).reshape(2, 2, share, D)
    one_keep = lax.dynamic_index_in_dim(one_parts, core, 1, keepdims=False)
    one_got = swap(lax.dynamic_index_in_dim(one_parts, 1 - core, 1, keepdims=False), "core")
    one_total = jnp.where(
        core == 0, jnp.stack([one_keep, one_got], 1), jnp.stack([one_got, one_keep], 1)
    )
    one_total = one_total.transpose(2, 0, 1, 3).reshape(share, 4 * D)

    two = (two_near.reshape(2, FF_SHARE, D), two_far.reshape(2, FF_SHARE, D))
    side_of = lambda half, x: lax.dynamic_index_in_dim(two[half], x, 0, keepdims=False)
    two_parts = (
        side_of(0, side), across(side_of(0, 1 - side), 1),
        across(side_of(1, side), 2), across(side_of(1, 1 - side), 3),
    )
    two_total = sum(p.astype(F32) for p in two_parts)
    out_line = out_line.reshape(outer, 2, share, -1)
    part = lambda d: lax.dynamic_slice(
        out_line, (deep ^ (d >> 1), side ^ (d & 1), 0, 0), (1, 1) + out_line.shape[2:]
    )[0, 0]
    out_total = sum(p.astype(F32) for p in [part(0)] + [across(part(d), d) for d in range(1, 4)])
    known_total = out_total[:, D:]
    out_total = out_total[:, :D]

    qkv_total, small_total = sum_tail(tail)
    pick = lambda i, n=1: small_total[:, i : i + n].reshape(-1)
    pick_known = lambda i, n=1: known_total[:, i : i + n].reshape(-1)

    hat, inverse = normalise(tokens.astype(F32))
    input_grad = dx1 + norm_grad(kept + back.astype(F32), hat, inverse, gain_one)
    return (
        output, input_grad, pick(0), pick(1), qkv_total, pick(2, 3), out_total, pick_known(0),
        pick_known(1), pick_known(2), one_total, known_total[:, 4:8].T.reshape(-1), two_total, pick_known(3),
    )


def solution(mesh):
    dp, fsdp = mesh.devices.shape
    finer = Mesh(
        mesh.devices.reshape(dp // 2, 2, fsdp // 2, 2), ("outer", "core", "inner", "side")
    )
    every = ("outer", "core", "inner", "side")
    vec, mat = P(every), P(every, None)
    plan = plane_plan if finer.devices.shape == (2, 2, 4, 2) else general_plan
    return jax.shard_map(
        plan,
        mesh=finer,
        in_specs=(mat, vec, vec, vec, mat, vec, mat, vec, vec, vec, mat, vec, mat, vec, mat),
        out_specs=(mat, mat, vec, vec, mat, vec, mat, vec, vec, vec, mat, vec, mat, vec),
        check_vma=False,
    )
```

```python
import functools

import jax
import jax.numpy as jnp
import numpy as np
from jax import lax
from jax.experimental import pallas as pl
from jax.experimental.pallas import tpu as pltpu
from jax.sharding import Mesh, PartitionSpec as P

D = 768
HEAD = 64
PAIR = 2 * HEAD
EPSILON = 1e-05
NEG = -1e30
TILE = 256
BF = jnp.bfloat16
F32 = jnp.float32
MIB = 1 << 20
LIGHT = pl.CostEstimate(flops=1 << 20, bytes_accessed=1 << 20, transcendentals=0)
HEAVY = pl.CostEstimate(flops=1 << 36, bytes_accessed=1 << 20, transcendentals=0)


def nn(a, b):
    return jnp.dot(a, b, preferred_element_type=F32)


def nt(a, b):
    return lax.dot_general(a, b, (((1,), (1,)), ((), ())), preferred_element_type=F32)


def tn(a, b):
    return lax.dot_general(a, b, (((0,), (0,)), ((), ())), preferred_element_type=F32)


def normalise(rows):
    average = jnp.mean(rows, -1, keepdims=True)
    centred = rows - average
    inverse = lax.rsqrt(jnp.mean(centred * centred, -1, keepdims=True) + EPSILON)
    return centred * inverse, inverse


def norm_grad(grad, hat, inverse, gain):
    scaled = grad * gain
    return inverse * (
        scaled
        - jnp.mean(scaled, -1, keepdims=True)
        - hat * jnp.mean(scaled * hat, -1, keepdims=True)
    )


def total(rows):
    return jnp.sum(rows, 0, keepdims=True)


def project_kernel(place_ref, own_ref, other_ref, gain_ref, shift_ref, weight_ref, bias_ref, normed_ref, qkv_ref):
    mine = (pl.program_id(0) // 2) == place_ref[0]
    rows = jnp.where(mine, own_ref[...].astype(F32), other_ref[...].astype(F32))
    hat, _ = normalise(rows)
    normed = (hat * gain_ref[...] + shift_ref[...]).astype(BF)
    normed_ref[...] = normed
    qkv_ref[...] = (nn(normed, weight_ref[...]) + bias_ref[...]).astype(BF)


def project(place, own, other, gain, shift, weight, bias):
    rows, width = own.shape
    columns = weight.shape[1]
    step = rows // 2
    half = pl.BlockSpec((step, width), lambda i, s: (i % 2, 0))
    fixed = lambda r, c: pl.BlockSpec((r, c), lambda i, s: (0, 0))
    return pl.pallas_call(
        project_kernel,
        grid_spec=pltpu.PrefetchScalarGridSpec(
            num_scalar_prefetch=1,
            grid=(4,),
            in_specs=[half, half, fixed(1, width), fixed(1, width), fixed(width, columns), fixed(1, columns)],
            out_specs=[
                pl.BlockSpec((step, width), lambda i, s: (i, 0)),
                pl.BlockSpec((step, columns), lambda i, s: (i, 0)),
            ],
        ),
        out_shape=[
            jax.ShapeDtypeStruct((2 * rows, width), BF),
            jax.ShapeDtypeStruct((2 * rows, columns), BF),
        ],
        compiler_params=pltpu.CompilerParams(vmem_limit_bytes=60 * MIB),
        cost_estimate=LIGHT,
        name="norm_and_qkv",
    )(place, own, other, gain, shift, weight, bias)


def forward_kernel(
    place_ref, q_ref, k_ref, v_ref, first_ref, keep_ref, send_ref, lse_ref, mag_buf, sign_buf, o_ref
):
    count = q_ref.shape[0] // TILE
    lane = lax.broadcasted_iota(jnp.int32, (1, PAIR), 1)
    values = jnp.transpose(v_ref[...].astype(F32)).astype(BF)
    key_at = lax.broadcasted_iota(jnp.int32, (TILE, TILE), 0)
    causal = key_at <= lax.broadcasted_iota(jnp.int32, (TILE, TILE), 1)
    for j in range(count):
        qs = slice(j * TILE, (j + 1) * TILE)
        q = q_ref[qs, :] * BF(HEAD**-0.5)
        first = first_ref[:, qs]
        heads = []
        for h in range(2):
            qh = jnp.where((lane >= HEAD) == (h == 1), q, BF(0))
            top = None
            for i in range(j + 1):
                ks = slice(i * TILE, (i + 1) * TILE)
                s = nt(k_ref[ks, :], qh)
                square = s * s + 1.0
                inverse = lax.rsqrt(square)
                allowed = key_at + i * TILE >= first
                if i == j:
                    allowed = allowed & causal
                mag = jnp.where(allowed, square * inverse, NEG)
                mag_buf[h, ks, :] = mag
                sign_buf[h, ks, :] = s * inverse
                best = jnp.max(mag, 0, keepdims=True)
                top = best if top is None else jnp.maximum(top, best)
            weight_sum = jnp.zeros((1, TILE), F32)
            mixture = jnp.zeros((HEAD, TILE), F32)
            for i in range(j + 1):
                ks = slice(i * TILE, (i + 1) * TILE)
                raised = jnp.exp(mag_buf[h, ks, :] - top)
                weight_sum = weight_sum + total(raised)
                mixture = mixture + nn(
                    values[h * HEAD : (h + 1) * HEAD, ks], (sign_buf[h, ks, :] * raised).astype(BF)
                )
            heads.append(mixture * (1.0 / weight_sum))
            lse_ref[0, h : h + 1, qs] = top + jnp.log(weight_sum)
        o_ref[qs, :] = jnp.transpose(jnp.concatenate(heads, 0)).astype(BF)
    rows = keep_ref.shape[0]
    keep_ref[...] = o_ref[pl.ds(pl.multiple_of(place_ref[0] * rows, rows), rows), :]
    send_ref[...] = o_ref[pl.ds(pl.multiple_of((1 - place_ref[0]) * rows, rows), rows), :]


def attend(place, qkv, firsts, start=0, stop=None):
    length, columns = qkv.shape
    pairs = columns // 3 // PAIR
    count = (pairs if stop is None else stop) - start
    block = lambda part: pl.BlockSpec((length, PAIR), lambda p, s: (0, part * pairs + start + p))
    half = pl.BlockSpec((length // 2, PAIR), lambda p, s: (0, p))
    return pl.pallas_call(
        forward_kernel,
        grid_spec=pltpu.PrefetchScalarGridSpec(
            num_scalar_prefetch=1,
            grid=(count,),
            in_specs=[block(0), block(1), block(2), pl.BlockSpec((1, length), lambda p, s: (0, 0))],
            out_specs=[half, half, pl.BlockSpec((1, 2, length), lambda p, s: (p, 0, 0))],
            scratch_shapes=[pltpu.VMEM((2, length, TILE), F32)] * 2 + [pltpu.VMEM((length, PAIR), BF)],
        ),
        out_shape=[
            jax.ShapeDtypeStruct((length // 2, count * PAIR), BF),
            jax.ShapeDtypeStruct((length // 2, count * PAIR), BF),
            jax.ShapeDtypeStruct((count, 2, length), F32),
        ],
        compiler_params=pltpu.CompilerParams(vmem_limit_bytes=60 * MIB),
        cost_estimate=LIGHT,
        name="attention_forward",
    )(place, qkv, qkv, qkv, firsts)


def backward_kernel(
    place_ref, q_ref, k_ref, v_ref, own_ref, got_ref, lse_ref, first_ref,
    dq_ref, dk_ref, dv_ref, dk_sum, dv_sum, part_buf, weight_buf, do_ref,
):
    rows = own_ref.shape[0]
    do_ref[pl.ds(pl.multiple_of(place_ref[0] * rows, rows), rows), :] = own_ref[...]
    do_ref[pl.ds(pl.multiple_of((1 - place_ref[0]) * rows, rows), rows), :] = got_ref[...]
    count = q_ref.shape[0] // TILE
    lane = lax.broadcasted_iota(jnp.int32, (1, PAIR), 1)
    keys = jnp.transpose(k_ref[...].astype(F32)).astype(BF)
    key_at = lax.broadcasted_iota(jnp.int32, (TILE, TILE), 0)
    causal = key_at <= lax.broadcasted_iota(jnp.int32, (TILE, TILE), 1)
    for j in range(count):
        qs = slice(j * TILE, (j + 1) * TILE)
        q = q_ref[qs, :] * BF(HEAD**-0.5)
        do = do_ref[qs, :]
        first = first_ref[:, qs]
        heads = []
        for h in range(2):
            chosen = (lane >= HEAD) == (h == 1)
            qh = jnp.where(chosen, q, BF(0))
            doh = jnp.where(chosen, do, BF(0))
            lse = lse_ref[0, h : h + 1, qs]
            centre = jnp.zeros((1, TILE), F32)
            for i in range(j + 1):
                ks = slice(i * TILE, (i + 1) * TILE)
                s = nt(k_ref[ks, :], qh)
                dw = nt(v_ref[ks, :], doh)
                square = s * s + 1.0
                inverse = lax.rsqrt(square)
                allowed = key_at + i * TILE >= first
                if i == j:
                    allowed = allowed & causal
                p = jnp.exp(jnp.where(allowed, square * inverse - lse, NEG))
                w = s * inverse * p
                centre = centre + total(w * dw)
                part_buf[h, ks, :] = p * dw * (1.0 + inverse * inverse * (inverse - 1.0))
                weight_buf[h, ks, :] = w
                dv = nn(w.astype(BF), doh)
                if i == j and h == 0:
                    dv_sum[ks, :] = dv
                else:
                    dv_sum[ks, :] += dv
            dq = jnp.zeros((HEAD, TILE), F32)
            for i in range(j + 1):
                ks = slice(i * TILE, (i + 1) * TILE)
                ds = (part_buf[h, ks, :] - weight_buf[h, ks, :] * centre).astype(BF)
                dk = nn(ds, qh)
                if i == j and h == 0:
                    dk_sum[ks, :] = dk
                else:
                    dk_sum[ks, :] += dk
                dq = dq + nn(keys[h * HEAD : (h + 1) * HEAD, ks], ds)
            heads.append(dq)
        dq_ref[qs, :] = (jnp.transpose(jnp.concatenate(heads, 0)) * HEAD**-0.5).astype(BF)
    dk_ref[...] = dk_sum[...].astype(BF)
    dv_ref[...] = dv_sum[...].astype(BF)


def attend_back(place, qkv, own, got, lse, firsts):
    length, columns = qkv.shape
    pairs = columns // 3 // PAIR
    block = lambda part: pl.BlockSpec((length, PAIR), lambda p, s: (0, part * pairs + p))
    half = pl.BlockSpec((length // 2, PAIR), lambda p, s: (0, p))
    shape = jax.ShapeDtypeStruct((length, columns // 3), BF)
    return pl.pallas_call(
        backward_kernel,
        grid_spec=pltpu.PrefetchScalarGridSpec(
            num_scalar_prefetch=1,
            grid=(pairs,),
            in_specs=[
                block(0),
                block(1),
                block(2),
                half,
                half,
                pl.BlockSpec((1, 2, length), lambda p, s: (p, 0, 0)),
                pl.BlockSpec((1, length), lambda p, s: (0, 0)),
            ],
            out_specs=[block(0)] * 3,
            scratch_shapes=[pltpu.VMEM((length, PAIR), F32)] * 2
            + [pltpu.VMEM((2, length, TILE), F32)] * 2
            + [pltpu.VMEM((length, PAIR), BF)],
        ),
        out_shape=[shape] * 3,
        compiler_params=pltpu.CompilerParams(vmem_limit_bytes=60 * MIB),
        cost_estimate=LIGHT,
        name="attention_backward",
    )(place, qkv, qkv, qkv, own, got, lse, firsts)


def half_backward_kernel(phase, place_ref, q_ref, k_ref, v_ref, do_ref, lse_ref, first_ref, *refs):
    sums_in, refs = (refs[:2], refs[2:]) if phase else ((), refs)
    dq_ref, dk_ref, dv_ref, dk_sum, dv_sum, part_buf, weight_buf = refs
    lane = lax.broadcasted_iota(jnp.int32, (1, PAIR), 1)
    keys = jnp.transpose(k_ref[...].astype(F32)).astype(BF)
    key_at = lax.broadcasted_iota(jnp.int32, (TILE, TILE), 0)
    causal = key_at <= lax.broadcasted_iota(jnp.int32, (TILE, TILE), 1)
    if phase:
        dk_sum[...] = sums_in[0][...].astype(F32)
        dv_sum[...] = sums_in[1][...].astype(F32)
    else:
        dk_sum[...] = jnp.zeros_like(dk_sum)
        dv_sum[...] = jnp.zeros_like(dv_sum)

    def rows(j, at):
        qs = slice(j * TILE, (j + 1) * TILE)
        own = slice(at * TILE, (at + 1) * TILE)
        q = q_ref[qs, :] * BF(HEAD**-0.5)
        do = do_ref[own, :]
        first = first_ref[:, qs]
        heads = []
        for h in range(2):
            chosen = (lane >= HEAD) == (h == 1)
            qh = jnp.where(chosen, q, BF(0))
            doh = jnp.where(chosen, do, BF(0))
            lse = lse_ref[0, h : h + 1, qs]
            centre = jnp.zeros((1, TILE), F32)
            for i in range(j + 1):
                ks = slice(i * TILE, (i + 1) * TILE)
                s = nt(k_ref[ks, :], qh)
                dw = nt(v_ref[ks, :], doh)
                square = s * s + 1.0
                inverse = lax.rsqrt(square)
                allowed = key_at + i * TILE >= first
                if i == j:
                    allowed = allowed & causal
                p = jnp.exp(jnp.where(allowed, square * inverse - lse, NEG))
                w = s * inverse * p
                centre = centre + total(w * dw)
                part_buf[h, ks, :] = p * dw * (1.0 + inverse * inverse * (inverse - 1.0))
                weight_buf[h, ks, :] = w
                dv_sum[ks, :] += nn(w.astype(BF), doh)
            dq = jnp.zeros((HEAD, TILE), F32)
            for i in range(j + 1):
                ks = slice(i * TILE, (i + 1) * TILE)
                ds = (part_buf[h, ks, :] - weight_buf[h, ks, :] * centre).astype(BF)
                dk_sum[ks, :] += nn(ds, qh)
                dq = dq + nn(keys[h * HEAD : (h + 1) * HEAD, ks], ds)
            heads.append(dq)
        dq_ref[own, :] = (jnp.transpose(jnp.concatenate(heads, 0)) * HEAD**-0.5).astype(BF)

    later = place_ref[0] == (0 if phase else 1)

    @pl.when(jnp.logical_not(later))
    def _():
        rows(0, 0)
        rows(1, 1)

    @pl.when(later)
    def _():
        rows(2, 0)
        rows(3, 1)

    dk_ref[...] = dk_sum[...].astype(dk_ref.dtype)
    dv_ref[...] = dv_sum[...].astype(dv_ref.dtype)


def attend_back_half(place, phase, qkv, do, lse, firsts, sums=()):
    length, columns = qkv.shape
    pairs = columns // 3 // PAIR
    block = lambda part: pl.BlockSpec((length, PAIR), lambda p, s: (0, part * pairs + p))
    half = pl.BlockSpec((length // 2, PAIR), lambda p, s: (0, p))
    shape = jax.ShapeDtypeStruct
    full = shape((length, columns // 3), BF)
    return pl.pallas_call(
        functools.partial(half_backward_kernel, phase),
        grid_spec=pltpu.PrefetchScalarGridSpec(
            num_scalar_prefetch=1,
            grid=(pairs,),
            in_specs=[
                block(0), block(1), block(2), half,
                pl.BlockSpec((1, 2, length), lambda p, s: (p, 0, 0)),
                pl.BlockSpec((1, length), lambda p, s: (0, 0)),
            ] + [block(0)] * len(sums),
            out_specs=[half, block(0), block(0)],
            scratch_shapes=[pltpu.VMEM((length, PAIR), F32)] * 2 + [pltpu.VMEM((2, length, TILE), F32)] * 2,
        ),
        out_shape=[shape((length // 2, columns // 3), BF), full, full],
        compiler_params=pltpu.CompilerParams(vmem_limit_bytes=60 * MIB),
        cost_estimate=LIGHT,
        name=f"attention_backward_{phase}",
    )(place, qkv, qkv, qkv, do, lse, firsts, *sums)


FF_STEP = 768
OUT_BIAS, GAIN, SHIFT, LAST_BIAS = range(4)
D_OUT_BIAS, D_GAIN, D_SHIFT, D_LAST_BIAS = range(4)


def middle_kernel(
    tok_ref, o_ref, g_ref, wo_ref, w1_ref, w2_ref, b1_ref, vec_ref,
    out_ref, dx_ref, do_ref, gone_ref, gtwo_ref, db1_ref, sums_ref,
    x_buf, h_buf, y_sum, dh_sum,
):
    step = pl.program_id(0)
    last = pl.num_programs(0) - 1

    @pl.when(step == 0)
    def _():
        x = tok_ref[...].astype(F32) + nn(o_ref[...], wo_ref[...]) + vec_ref[OUT_BIAS : OUT_BIAS + 1, :]
        x_buf[...] = x
        hat, _ = normalise(x)
        h_buf[...] = (hat * vec_ref[GAIN : GAIN + 1, :] + vec_ref[SHIFT : SHIFT + 1, :]).astype(BF)
        y_sum[...] = jnp.zeros_like(y_sum)
        dh_sum[...] = jnp.zeros_like(dh_sum)

    @pl.when(step < last)
    def _():
        h = h_buf[...]
        g = g_ref[...]
        u = nn(h, w1_ref[...]) + b1_ref[...]
        root = 0.7978845608028654
        u2 = u * u
        bent = jnp.tanh(root * u * (1.0 + 0.044715 * u2))
        a = (0.5 * u * (1.0 + bent)).astype(BF)
        slope = 0.5 * (1.0 + bent) + 0.5 * u * (1.0 - bent * bent) * (root * (1.0 + 0.134145 * u2))
        y_sum[...] += nn(a, w2_ref[...])
        du = (nt(g, w2_ref[...]) * slope).astype(BF)
        db1_ref[...] = total(du.astype(F32))
        dh_sum[...] += nt(du, w1_ref[...])
        gone_ref[...] = tn(h, du).astype(BF)
        gtwo_ref[...] = tn(a, g).astype(BF)

    @pl.when(step == last)
    def _():
        x = x_buf[...]
        g = g_ref[...].astype(F32)
        out_ref[...] = (x + y_sum[...] + vec_ref[LAST_BIAS : LAST_BIAS + 1, :]).astype(BF)
        hat, inverse = normalise(x)
        dh = dh_sum[...]
        dx = g + norm_grad(dh, hat, inverse, vec_ref[GAIN : GAIN + 1, :])
        dx_ref[...] = dx
        dxr = dx.astype(BF)
        do_ref[...] = nt(dxr, wo_ref[...]).astype(BF)
        gone_ref[...] = tn(o_ref[...], dxr).astype(BF)
        sums_ref[...] = jnp.zeros_like(sums_ref)
        sums_ref[D_OUT_BIAS : D_OUT_BIAS + 1, :] = total(dx)
        sums_ref[D_GAIN : D_GAIN + 1, :] = total(dh * hat)
        sums_ref[D_SHIFT : D_SHIFT + 1, :] = total(dh)
        sums_ref[D_LAST_BIAS : D_LAST_BIAS + 1, :] = total(g)


def middle(tokens, mixture, grad, wo, w1, w2, b1, vectors):
    rows, width = tokens.shape
    hidden = w1.shape[1]
    steps = hidden // FF_STEP
    fixed = lambda r, c: pl.BlockSpec((r, c), lambda i: (0, 0))
    across = lambda r: pl.BlockSpec((r, FF_STEP), lambda i: (0, jnp.minimum(i, steps - 1)))
    down = pl.BlockSpec((FF_STEP, width), lambda i: (jnp.minimum(i, steps - 1), 0))
    return pl.pallas_call(
        middle_kernel,
        grid=(steps + 1,),
        in_specs=[
            fixed(rows, width), fixed(rows, width), fixed(rows, width), fixed(width, width),
            across(width), down, across(1), fixed(*vectors.shape),
        ],
        out_specs=[
            fixed(rows, width), fixed(rows, width), fixed(rows, width),
            pl.BlockSpec((width, FF_STEP), lambda i: (0, i)), down, across(1), fixed(8, width),
        ],
        out_shape=[
            jax.ShapeDtypeStruct((rows, width), BF),
            jax.ShapeDtypeStruct((rows, width), F32),
            jax.ShapeDtypeStruct((rows, width), BF),
            jax.ShapeDtypeStruct((width, hidden + FF_STEP), BF),
            jax.ShapeDtypeStruct((hidden, width), BF),
            jax.ShapeDtypeStruct((1, hidden), F32),
            jax.ShapeDtypeStruct((8, width), F32),
        ],
        scratch_shapes=[
            pltpu.VMEM((rows, width), F32),
            pltpu.VMEM((rows, width), BF),
            pltpu.VMEM((rows, width), F32),
            pltpu.VMEM((rows, width), F32),
        ],
        compiler_params=pltpu.CompilerParams(vmem_limit_bytes=60 * MIB),
        cost_estimate=LIGHT,
        name="feed_forward_both_ways",
    )(tokens, mixture, grad, wo, w1, w2, b1, vectors)


def unproject_kernel(
    place_ref, own_ref, other_ref, dq_ref, dk_ref, dv_ref, weight_ref, keep_ref, send_ref, sums_ref, bias_ref
):
    step = pl.program_id(0)
    mine = (step // 2) == place_ref[0]
    rows = jnp.where(mine, own_ref[...].astype(F32), other_ref[...].astype(F32))
    hat, _ = normalise(rows)
    third = dq_ref.shape[1]
    grad = nt(dq_ref[...], weight_ref[:, :third])
    grad = grad + nt(dk_ref[...], weight_ref[:, third : 2 * third])
    grad = grad + nt(dv_ref[...], weight_ref[:, 2 * third :])

    @pl.when(step == 0)
    def _():
        sums_ref[...] = jnp.zeros_like(sums_ref)
        bias_ref[...] = jnp.zeros_like(bias_ref)

    sums_ref[0:1, :] += total(grad * hat)
    sums_ref[1:2, :] += total(grad)
    bias_ref[0:1, :] += total(dq_ref[...].astype(F32))
    bias_ref[1:2, :] += total(dk_ref[...].astype(F32))
    bias_ref[2:3, :] += total(dv_ref[...].astype(F32))

    @pl.when(mine)
    def _():
        keep_ref[...] = grad

    @pl.when(jnp.logical_not(mine))
    def _():
        send_ref[...] = grad.astype(BF)


def unproject(place, own, other, dq, dk, dv, weight):
    rows, width = own.shape
    third = dq.shape[1]
    step = rows // 2
    half = pl.BlockSpec((step, width), lambda i, s: (i % 2, 0))
    part = pl.BlockSpec((step, third), lambda i, s: (i, 0))
    fixed = lambda r, c: pl.BlockSpec((r, c), lambda i, s: (0, 0))
    return pl.pallas_call(
        unproject_kernel,
        grid_spec=pltpu.PrefetchScalarGridSpec(
            num_scalar_prefetch=1,
            grid=(4,),
            in_specs=[half, half, part, part, part, fixed(*weight.shape)],
            out_specs=[
                pl.BlockSpec((step, width), lambda i, s: (jnp.clip(i - 2 * s[0], 0, 1), 0)),
                pl.BlockSpec((step, width), lambda i, s: (jnp.clip(i - 2 * (1 - s[0]), 0, 1), 0)),
                fixed(8, width),
                fixed(8, third),
            ],
        ),
        out_shape=[
            jax.ShapeDtypeStruct((rows, width), F32),
            jax.ShapeDtypeStruct((rows, width), BF),
            jax.ShapeDtypeStruct((8, width), F32),
            jax.ShapeDtypeStruct((8, third), F32),
        ],
        compiler_params=pltpu.CompilerParams(vmem_limit_bytes=60 * MIB),
        cost_estimate=LIGHT,
        name="grad_at_first_norm",
    )(place, own, other, dq, dk, dv, weight)


def tie(*blocks):
    return lax.optimization_barrier(blocks)


def swap(block, axis):
    return lax.ppermute(block, axis, [(0, 1), (1, 0)])


def general_plan(
    tokens, segment_ids, ln1_gain, ln1_bias, qkv_weight, qkv_bias, out_weight, out_bias,
    ln2_gain, ln2_bias, fc1_weight, fc1_bias, fc2_weight, fc2_bias, output_grad,
):
    outer, inner = lax.axis_size("outer"), lax.axis_size("inner")
    core, side = lax.axis_index("core"), lax.axis_index("side")
    everyone = ("outer", "core", "inner", "side")
    chips = ("outer", "inner", "side")
    rows = tokens.shape[0]
    share = qkv_weight.shape[0]
    place = side.astype(jnp.int32).reshape(1)

    other = swap(tokens, "side")
    other_marks = swap(segment_ids, "side")
    marks = jnp.where(
        side == 0,
        jnp.concatenate([segment_ids, other_marks]),
        jnp.concatenate([other_marks, segment_ids]),
    )
    firsts = sum(jnp.where(marks > v, jnp.sum(marks == v), 0) for v in range(3))
    firsts = firsts.astype(jnp.int32)[None, :]

    parts = qkv_weight.reshape(share, 3, 2, D // 2).transpose(2, 0, 1, 3).reshape(2, share, 3 * D // 2)
    vectors = jnp.concatenate(
        [
            v.reshape(share, -1)
            for v in (ln1_gain, ln1_bias, qkv_bias, out_bias, ln2_gain, ln2_bias, fc1_bias, fc2_bias)
        ],
        1,
    )
    vectors = jnp.pad(vectors, ((0, 0), (0, 128 - vectors.shape[1])))
    parts = jnp.concatenate([parts, jnp.broadcast_to(vectors, (2, share, 128))], 2)
    parts = parts.reshape(2, share, 2, 5 * 128).transpose(2, 0, 1, 3)
    parts = jnp.broadcast_to(parts[None, :, None], (outer, 2, inner, 2, share, 5 * 128))
    got = lax.all_to_all(
        parts.reshape(outer * inner * 4, share, 5 * 128), everyone, split_axis=0, concat_axis=0, tiled=True
    ).reshape(D, 5 * 128)
    twin = swap(got, "core")
    packed = jnp.where(core == 0, jnp.concatenate([got, twin], 1), jnp.concatenate([twin, got], 1))
    w_qkv = packed[:, : 9 * 128]
    table = packed[:, 9 * 128 :].astype(F32)
    column = lambda i: table[:, i][None, :]
    qkv_bias_all = table[:, 2:5].reshape(3, 2, D // 2)
    qkv_bias_mine = lax.dynamic_index_in_dim(qkv_bias_all, side, 1, keepdims=False).reshape(1, -1)
    b1 = table[:, 8:12].reshape(1, -1)
    mid_vectors = jnp.concatenate([column(5), column(6), column(7), column(12)], 0)

    wide = lax.all_gather(jnp.concatenate([fc1_weight, out_weight], 1), everyone, axis=0, tiled=True)
    w2 = lax.all_gather(fc2_weight, everyone, axis=0, tiled=True)
    w1, wo = wide[:, : fc1_weight.shape[1]], wide[:, fc1_weight.shape[1] :]

    normed, qkv = project(place, tokens, other, column(0), column(1), w_qkv, qkv_bias_mine)
    mine, theirs, lse = attend(place, qkv, firsts)
    theirs = swap(theirs, "side")
    mixture = jnp.where(side == 0, jnp.concatenate([mine, theirs], 1), jnp.concatenate([theirs, mine], 1))

    output, dx1, do, grad_wide, grad_two, db1, sums = middle(
        tokens, mixture, output_grad, wo, w1, w2, b1, mid_vectors
    )

    half = D // 2
    do_mine = lax.dynamic_slice_in_dim(do, side * half, half, 1)
    do_theirs = swap(lax.dynamic_slice_in_dim(do, (1 - side) * half, half, 1), "side")

    def reduce_rows(grad):
        width = grad.shape[1]
        pieces = grad.reshape(outer, 2, inner * 2, grad.shape[0] // (4 * outer * inner), width)
        keep = lax.dynamic_index_in_dim(pieces, core, 1, keepdims=False)
        send = lax.dynamic_index_in_dim(pieces, 1 - core, 1, keepdims=False)
        both = (keep.astype(F32) + swap(send, "core").astype(F32)).astype(BF)
        both = both.reshape((outer * inner * 2,) + both.shape[2:])
        return lax.all_to_all(both, chips, split_axis=0, concat_axis=0, tiled=True)

    wide_total = jnp.sum(reduce_rows(grad_wide).astype(F32), 0)
    two_total = jnp.sum(reduce_rows(grad_two).astype(F32), 0)

    dq, dk, dv = attend_back(place, qkv, do_mine, do_theirs, lse, firsts)
    kept, sent, first_sums, bias_sums = unproject(place, tokens, other, dq, dk, dv, w_qkv)
    back = swap(sent, "side")
    grad_qkv = jnp.concatenate([tn(normed, d).astype(BF) for d in (dq, dk, dv)], 1)
    bias_mine = jnp.zeros((3, 2, half), F32)
    bias_mine = lax.dynamic_update_slice(bias_mine, bias_sums[:3][:, None], (0, side, 0)).reshape(-1)
    small = jnp.concatenate(
        [
            v.reshape(D, -1)
            for v in (
                first_sums[0], first_sums[1], bias_mine, sums[D_OUT_BIAS], sums[D_GAIN],
                sums[D_SHIFT], db1, sums[D_LAST_BIAS],
            )
        ],
        1,
    )
    small = jnp.pad(small, ((0, 0), (0, 128 - small.shape[1]))).astype(BF)
    tail = reduce_rows(jnp.concatenate([grad_qkv, small], 1)).astype(F32)
    tail = tail.reshape(outer * inner, 2, share, 10 * 128)
    qkv_total = jnp.sum(tail[..., : 9 * 128], 0).reshape(2, share, 3, half)
    qkv_total = qkv_total.transpose(1, 2, 0, 3).reshape(share, 3 * D)
    small_total = jnp.sum(tail[..., 9 * 128 :], (0, 1))
    pick = lambda i, n=1: small_total[:, i : i + n].reshape(-1)

    hat, inverse = normalise(tokens.astype(F32))
    input_grad = dx1 + norm_grad(kept + back.astype(F32), hat, inverse, column(0))
    hidden = fc1_weight.shape[1]
    return (
        output,
        input_grad,
        pick(0),
        pick(1),
        qkv_total,
        pick(2, 3),
        wide_total[:, hidden:],
        pick(5),
        pick(6),
        pick(7),
        wide_total[:, :hidden],
        pick(8, 4),
        two_total,
        pick(12),
    )


SHARE = 24
FF_SHARE = 96
FF_HALF = 8 * FF_SHARE


def pack_kernel(weight_ref, *refs):
    *vector_refs, out_ref, buf = refs
    half = D // 2
    buf[...] = jnp.zeros_like(buf)
    for i, ref in enumerate(vector_refs):
        buf[i : i + 1, : ref.shape[1]] = ref[...].astype(F32)
    vectors = buf[...].astype(BF)
    for x in range(2):
        q, k, v = (weight_ref[:, part * D + x * half : part * D + (x + 1) * half] for part in range(3))
        low = jnp.concatenate([q, k[:, :256]], 1)
        high = jnp.concatenate([k[:, 256:], v, vectors], 1)
        for y in range(2):
            for z in range(4):
                out_ref[((2 * y) * 4 + z) * 2 + x] = low
                out_ref[((2 * y + 1) * 4 + z) * 2 + x] = high


def pack(weight, vectors):
    share = weight.shape[0]
    return pl.pallas_call(
        pack_kernel,
        out_shape=jax.ShapeDtypeStruct((32, share, 640), BF),
        scratch_shapes=[pltpu.VMEM((share, 128), F32)],
        compiler_params=pltpu.CompilerParams(vmem_limit_bytes=60 * MIB),
        name="pack_qkv_weights",
    )(weight, *(v.reshape(1, -1) for v in vectors))


ALL_VECTORS = 8
GAIN_ONE, SHIFT_ONE, QKV_BIAS = 0, 1, 2


def spread(rows, where, count):
    lanes = lax.broadcasted_iota(jnp.int32, (128, where.shape[1]), 0)
    chosen = jnp.where(lanes == where[1:2, :], 1.0, 0.0).astype(BF)
    found = nn(rows.astype(BF), chosen)
    devices = rows.shape[0] // count
    owners = lax.broadcasted_iota(jnp.int32, (devices, where.shape[1]), 0) == where[0:1, :]
    return jnp.concatenate(
        [total(jnp.where(owners, found[i * devices : (i + 1) * devices], 0.0)) for i in range(count)], 0
    )


def places(each, numbers):
    numbers = np.asarray(numbers)
    return np.stack([numbers // each, numbers % each]).astype(np.int32)


def plane_project_kernel(
    ids_ref, own_ref, other_ref, got_ref, twin_ref, at_d_ref, at_qkv_ref,
    normed_ref, qkv_ref, weight_ref, vec_ref, table, bias,
):
    @pl.when(pl.program_id(0) == 0)
    def _():
        first = ids_ref[1] == 0
        got, twin = got_ref[...], twin_ref[...]
        weight_ref[:, :640] = jnp.where(first, got, twin)
        high = jnp.where(first, twin, got)
        weight_ref[:, 640:] = high[:, :512]
        table[...] = high[:, 512:].astype(F32)
        rows = lambda i: table[pl.ds(i, 32, stride=SHARE), :]
        bias[...] = spread(rows(QKV_BIAS), at_qkv_ref[0], 1)
        vec_ref[...] = spread(jnp.concatenate([rows(GAIN_ONE), rows(SHIFT_ONE)], 0), at_d_ref[...], 2)

    mine = (pl.program_id(0) // 2) == ids_ref[3]
    rows = jnp.where(mine, own_ref[...], other_ref[...]).astype(F32)
    hat, _ = normalise(rows)
    normed = (hat * vec_ref[0:1, :] + vec_ref[1:2, :]).astype(BF)
    normed_ref[...] = normed
    qkv_ref[...] = (nn(normed, weight_ref[...]) + bias[...]).astype(BF)


def plane_project(ids, own, other, got, twin):
    rows, width = own.shape
    columns = 3 * width // 2
    step = rows // 2
    at_d = places(SHARE, range(width))
    at_qkv = [
        places(3 * SHARE, [part * width + x * width // 2 + m for part in range(3) for m in range(width // 2)])
        for x in range(2)
    ]
    at_qkv = jnp.stack([jnp.asarray(a) for a in at_qkv])
    half = pl.BlockSpec((step, width), lambda i, s: (i % 2, 0))
    fixed = lambda r, c: pl.BlockSpec((r, c), lambda i, s: (0, 0))
    return pl.pallas_call(
        plane_project_kernel,
        grid_spec=pltpu.PrefetchScalarGridSpec(
            num_scalar_prefetch=1,
            grid=(4,),
            in_specs=[
                half, half, fixed(*got.shape), fixed(*got.shape), fixed(2, width),
                pl.BlockSpec((1, 2, columns), lambda i, s: (s[3], 0, 0)),
            ],
            out_specs=[
                pl.BlockSpec((step, width), lambda i, s: (i, 0)),
                pl.BlockSpec((step, columns), lambda i, s: (i, 0)),
                fixed(width, columns),
                fixed(2, width),
            ],
            scratch_shapes=[pltpu.VMEM((width, 128), F32), pltpu.VMEM((1, columns), F32)],
        ),
        out_shape=[
            jax.ShapeDtypeStruct((2 * rows, width), BF),
            jax.ShapeDtypeStruct((2 * rows, columns), BF),
            jax.ShapeDtypeStruct((width, columns), BF),
            jax.ShapeDtypeStruct((2, width), F32),
        ],
        compiler_params=pltpu.CompilerParams(vmem_limit_bytes=60 * MIB),
        cost_estimate=LIGHT,
        name="norm_and_qkv",
    )(ids, own, other, got, twin, jnp.asarray(at_d), at_qkv)


def middle_vectors_kernel(ids_ref, got_ref, twin_ref, at_d_ref, at_ff_ref, vec_ref, b1_ref, table):
    table[...] = jnp.where(ids_ref[1] == 0, twin_ref[...], got_ref[...]).astype(F32)
    rows = lambda i: table[pl.ds(i, 32, stride=SHARE), :]
    vec_ref[...] = spread(jnp.concatenate([rows(i) for i in (3, 4, 5, 7)], 0), at_d_ref[...], 4)
    b1_ref[...] = spread(rows(6), at_ff_ref[...], 1)


def middle_vectors(ids, got, twin):
    width, hidden = got.shape[0], 4 * got.shape[0]
    at_d, at_ff = jnp.asarray(places(SHARE, range(width))), jnp.asarray(places(FF_SHARE, range(hidden)))
    last = pl.BlockSpec((width, 128), lambda i, s: (0, 4))
    fixed = lambda r, c: pl.BlockSpec((r, c), lambda i, s: (0, 0))
    return pl.pallas_call(
        middle_vectors_kernel,
        grid_spec=pltpu.PrefetchScalarGridSpec(
            num_scalar_prefetch=1,
            grid=(1,),
            in_specs=[last, last, fixed(2, width), fixed(2, hidden)],
            out_specs=[fixed(4, width), fixed(1, hidden)],
            scratch_shapes=[pltpu.VMEM((width, 128), F32)],
        ),
        out_shape=[jax.ShapeDtypeStruct((4, width), F32), jax.ShapeDtypeStruct((1, hidden), F32)],
        compiler_params=pltpu.CompilerParams(vmem_limit_bytes=60 * MIB),
        cost_estimate=LIGHT,
        name="middle_vectors",
    )(ids, got, twin, at_d, at_ff)


def out_project_kernel(ids_ref, tok_ref, own_ref, got_ref, wo_own_ref, wo_got_ref, vec_ref, x_ref, h_ref):
    x = tok_ref[...].astype(F32) + nn(own_ref[...], wo_own_ref[...]) + nn(got_ref[...], wo_got_ref[...])
    x = x + vec_ref[OUT_BIAS : OUT_BIAS + 1, :]
    x_ref[...] = x
    hat, _ = normalise(x)
    h_ref[...] = (hat * vec_ref[GAIN : GAIN + 1, :] + vec_ref[SHIFT : SHIFT + 1, :]).astype(BF)


def out_project(ids, tokens, own, got, wide, vectors):
    rows, width = tokens.shape
    half = width // 2
    step = rows
    tile = lambda c: pl.BlockSpec((step, c), lambda i, s: (i, 0))
    return pl.pallas_call(
        out_project_kernel,
        grid_spec=pltpu.PrefetchScalarGridSpec(
            num_scalar_prefetch=1,
            grid=(1,),
            in_specs=[
                tile(width), tile(half), tile(half),
                pl.BlockSpec((half, width), lambda i, s: (s[3], wide.shape[1] // width - 1)),
                pl.BlockSpec((half, width), lambda i, s: (1 - s[3], wide.shape[1] // width - 1)),
                pl.BlockSpec(vectors.shape, lambda i, s: (0, 0)),
            ],
            out_specs=[tile(width), tile(width)],
        ),
        out_shape=[jax.ShapeDtypeStruct((rows, width), F32), jax.ShapeDtypeStruct((rows, width), BF)],
        compiler_params=pltpu.CompilerParams(vmem_limit_bytes=60 * MIB),
        cost_estimate=LIGHT,
        name="out_projection_and_second_norm",
    )(ids, tokens, own, got, wide, wide, vectors)


def gelu_both(u):
    root = 0.7978845608028654
    u2 = u * u
    bent = jnp.tanh(u * (root + (root * 0.044715) * u2))
    c = 0.5 * bent + 0.5
    a = u * c
    slope = c + a * (1.0 - bent) * (root + (root * 0.134145) * u2)
    return a.astype(BF), slope


FF_ROWS = 512


def feed_forward_kernel(plane, ids_ref, *refs):
    h_own_hbm, h_sib_hbm, g_own_hbm, g_sib_hbm, wide_hbm, own_hbm, far_hbm, b1_ref, *refs = refs
    earlier, refs = (refs[:2], refs[2:]) if plane else ((), refs)
    outs, db1_ref, refs = refs[:9], refs[9], refs[10:]
    h, g, w1, own, far, w2, y_all, dh_all, one, a_all, du_all, y_sib, dh_sib, *refs = refs
    q00, q10, q01, q11, two, *refs = refs
    y_old, dh_old, in_sems, out_sems = refs if plane else (None, None, *refs)
    my_y, my_c, my_z, my_x = (ids_ref[i] for i in range(4))
    unit = FF_SHARE
    rows = h_own_hbm.shape[0]

    column = pl.multiple_of(((my_y ^ plane) * 2 + my_c) * FF_HALF, FF_HALF)
    sources = [
        (wide_hbm.at[:, pl.ds(column, FF_HALF)], w1), (own_hbm, own), (far_hbm, far), (h_own_hbm, h.at[:rows]),
        (g_own_hbm, g.at[:rows]), (h_sib_hbm, h.at[rows:]), (g_sib_hbm, g.at[rows:]),
    ]
    if plane:
        sources += [(earlier[0], y_old), (earlier[1], dh_old)]
    loads = [pltpu.make_async_copy(src, dst, in_sems.at[i]) for i, (src, dst) in enumerate(sources)]
    for load in loads:
        load.start()
    for load in loads[:3]:
        load.wait()
    for z in range(4):
        near, distant = own[z ^ my_z], far[z ^ my_z]
        w2[2 * z * unit : (2 * z + 1) * unit, :] = jnp.where(my_x == 0, near, distant)
        w2[(2 * z + 1) * unit : (2 * z + 2) * unit, :] = jnp.where(my_x == 0, distant, near)
    for load in loads[3:5]:
        load.wait()

    def one_pass(i, carry):
        if FF_ROWS == rows:
            sib_next = i == 1
        else:
            sib_next = i * FF_ROWS == rows

        @pl.when(sib_next)
        def _():
            for load in loads[5:7]:
                load.wait()

        at = pl.ds(pl.multiple_of(i * FF_ROWS, FF_ROWS), FF_ROWS)
        hr, gr = h[at, :], g[at, :]
        a, slope = gelu_both(nn(hr, w1[...]) + b1_ref[...])
        du = (nt(gr, w2[...]) * slope).astype(BF)
        a_all[at, :] = a
        du_all[at, :] = du
        dh_all[at, :] = nt(du, w1[...])
        y_all[at, :] = nn(a, w2[...])
        return carry + total(du.astype(F32))

    db1_ref[...] = lax.fori_loop(0, 2 * rows // FF_ROWS, one_pass, jnp.zeros(db1_ref.shape, F32))

    stores = []

    def store(src, at):
        copy = pltpu.make_async_copy(src, outs[at], out_sems.at[at])
        copy.start()
        stores.append(copy)

    dh_sib[...] = dh_all[rows:, :].astype(BF)
    store(dh_sib, 3)
    if plane:
        for load in loads[7:]:
            load.wait()
        dh_all[:rows, :] += dh_old[...]
        y_all[:rows, :] += y_old[...]
    store(dh_all.at[:rows], 2)
    store(y_all.at[:rows], 0)
    y_sib[...] = y_all[rows:, :].astype(BF)
    store(y_sib, 1)

    one[...] = tn(h[...], du_all[...])
    two[...] = tn(a_all[...], g[...]).astype(BF)
    store(two, 8)
    for xr, yr, ref, at in ((1, 0, q10, 5), (1, 1, q11, 7), (0, 1, q01, 6), (0, 0, q00, 4)):
        half, share_at = my_y ^ yr, my_x ^ xr
        for z in range(4):
            parts = []
            for c in range(2):
                start = half * (16 * SHARE) + share_at * SHARE + (c * 4 + z) * 2 * SHARE
                parts.append(one[pl.ds(pl.multiple_of(start, 8), SHARE), :])
            ref[2 * z * SHARE : 2 * (z + 1) * SHARE, :] = jnp.concatenate(parts, 0).astype(BF)
        store(ref, at)
    for copy in stores:
        copy.wait()


def feed_forward(ids, plane, h_own, h_sib, g_own, g_sib, wide, own, far, b1, earlier=()):
    rows, width = h_own.shape
    anywhere = pl.BlockSpec(memory_space=pl.ANY)
    shape = jax.ShapeDtypeStruct
    f32, bf = shape((rows, width), F32), shape((rows, width), BF)
    pieces = [shape((8 * SHARE, width), BF)] * 4
    pieces += [shape((FF_HALF, width), BF)]
    held = lambda s: pltpu.VMEM(s.shape, s.dtype)
    scratch = [pltpu.VMEM((2 * rows, width), BF)] * 2
    scratch += [pltpu.VMEM((width, FF_HALF), BF), held(own), held(far), pltpu.VMEM((FF_HALF, width), BF)]
    scratch += [pltpu.VMEM((2 * rows, width), F32)] * 2 + [pltpu.VMEM((width, FF_HALF), F32)]
    scratch += [pltpu.VMEM((2 * rows, FF_HALF), BF)] * 2
    scratch += [held(bf)] * 2 + [held(s) for s in pieces]
    scratch += [held(f32)] * 2 if plane else []
    scratch += [pltpu.SemaphoreType.DMA((9,)), pltpu.SemaphoreType.DMA((9,))]
    return pl.pallas_call(
        functools.partial(feed_forward_kernel, plane),
        grid_spec=pltpu.PrefetchScalarGridSpec(
            num_scalar_prefetch=1,
            grid=(1,),
            in_specs=[anywhere] * 7
            + [pl.BlockSpec((1, FF_HALF), lambda i, s: (0, (s[0] ^ plane) * 2 + s[1]))]
            + [anywhere] * len(earlier),
            out_specs=[anywhere] * 9 + [pl.BlockSpec((1, FF_HALF), lambda i, s: (0, 0))],
            scratch_shapes=scratch,
        ),
        out_shape=[f32, bf, f32, bf] + pieces + [shape((1, FF_HALF), F32)],
        compiler_params=pltpu.CompilerParams(vmem_limit_bytes=60 * MIB),
        cost_estimate=LIGHT,
        name=f"feed_forward_both_ways_{plane}",
    )(ids, h_own, h_sib, g_own, g_sib, wide, own, far, b1, *earlier)


def second_norm_kernel(
    ids_ref, x_ref, dh_ref, dh0_ref, dh1_ref, g_ref, wo_ref, vec_ref, dx_ref, dxr_ref, do_own_ref, do_send_ref, sums
):
    x = x_ref[...]
    g = g_ref[...].astype(F32)
    hat, inverse = normalise(x)
    dh = dh_ref[...] + dh0_ref[...].astype(F32) + dh1_ref[...].astype(F32)
    dx = g + norm_grad(dh, hat, inverse, vec_ref[GAIN : GAIN + 1, :])
    dx_ref[...] = dx
    dxr = dx.astype(BF)
    dxr_ref[...] = dxr
    half = wo_ref.shape[0] // 2
    mine = pl.ds(pl.multiple_of(ids_ref[3] * half, half), half)
    theirs = pl.ds(pl.multiple_of((1 - ids_ref[3]) * half, half), half)
    do_send_ref[...] = nt(dxr, wo_ref[theirs, :]).astype(BF)
    do_own_ref[...] = nt(dxr, wo_ref[mine, :]).astype(BF)

    @pl.when(pl.program_id(0) == 0)
    def _():
        sums[...] = jnp.zeros_like(sums)

    sums[D_OUT_BIAS : D_OUT_BIAS + 1, :] += total(dx)
    sums[D_GAIN : D_GAIN + 1, :] += total(dh * hat)
    sums[D_SHIFT : D_SHIFT + 1, :] += total(dh)
    sums[D_LAST_BIAS : D_LAST_BIAS + 1, :] += total(g)


def second_norm_back(ids, x, dh, dh0, dh1, g, wide, vectors):
    rows, width = x.shape
    step = rows
    tile = lambda c: pl.BlockSpec((step, c), lambda i, s: (i, 0))
    shape = jax.ShapeDtypeStruct
    half = width // 2
    return pl.pallas_call(
        second_norm_kernel,
        grid_spec=pltpu.PrefetchScalarGridSpec(
            num_scalar_prefetch=1,
            grid=(1,),
            in_specs=[tile(width)] * 5
            + [
                pl.BlockSpec((width, width), lambda i, s: (0, wide.shape[1] // width - 1)),
                pl.BlockSpec(vectors.shape, lambda i, s: (0, 0)),
            ],
            out_specs=[tile(width), tile(width), tile(half), tile(half), pl.BlockSpec((8, width), lambda i, s: (0, 0))],
        ),
        out_shape=[
            shape((rows, width), F32), shape((rows, width), BF), shape((rows, half), BF),
            shape((rows, half), BF), shape((8, width), F32),
        ],
        compiler_params=pltpu.CompilerParams(vmem_limit_bytes=60 * MIB),
        cost_estimate=LIGHT,
        name="second_norm_back",
    )(ids, x, dh, dh0, dh1, g, wide, vectors)


def out_weight_kernel(
    ids_ref, dxr_ref, o_own_ref, o_got_ref, sums_ref, near_ref, far_ref, keep_ref, send_ref, gwo
):
    width = dxr_ref.shape[1]
    half = width // 2
    mine = pl.ds(pl.multiple_of(ids_ref[3] * half, half), half)
    theirs = pl.ds(pl.multiple_of((1 - ids_ref[3]) * half, half), half)
    gwo[mine, :] = tn(o_own_ref[...], dxr_ref[...]).astype(BF)
    gwo[theirs, :] = tn(o_got_ref[...], dxr_ref[...]).astype(BF)
    lane = lax.broadcasted_iota(jnp.int32, (width, 128), 1)
    columns = jnp.transpose(sums_ref[...])
    table = jnp.zeros((width, 128), F32)
    for i in range(4):
        table = table + jnp.where(lane == i, columns[:, i : i + 1], 0.0)
    block = width // 4
    first, low = ids_ref[1] == 0, ids_ref[0] == 0
    near = jnp.transpose(jnp.broadcast_to(near_ref[...], (8, width)))[:, :1]
    far = jnp.transpose(jnp.broadcast_to(far_ref[...], (8, width)))[:, :1]
    halves = (jnp.where(low, near, far), jnp.where(low, far, near))
    for j in range(4):
        cut = lambda h: jnp.concatenate([h[k * FF_SHARE + j * SHARE :][:SHARE] for k in range(width // FF_SHARE)], 0)
        zero = jnp.zeros((block, 1), F32)
        column = []
        for h in halves:
            column += [jnp.where(first, cut(h), zero), jnp.where(first, zero, cut(h))]
        table = table + jnp.where(lane == 4 + j, jnp.concatenate(column, 0), 0.0)
    table = table.astype(BF)
    size = 2 * SHARE
    for y in range(2):
        for z in range(4):
            to = slice((z * 2 + y) * size, (z * 2 + y + 1) * size)
            for ref, here in ((keep_ref, ids_ref[1]), (send_ref, 1 - ids_ref[1])):
                start = pl.multiple_of(here * 4 * size + (y * 8 + z) * size, 16)
                ref[to, :width] = gwo[pl.ds(start, size), :]
            cut = lambda c: table[((y * 2 + c) * 4 + z) * size :][:size]
            keep_ref[to, width:] = jnp.where(first, cut(0), cut(1))
            send_ref[to, width:] = jnp.where(first, cut(1), cut(0))


def out_weight_grad(ids, dxr, o_own, o_got, sums, near, far):
    width = dxr.shape[1]
    whole = lambda a: pl.BlockSpec(a.shape, lambda i, s: (0, 0))
    out = jax.ShapeDtypeStruct((width // 2, width + 128), BF)
    args = (dxr, o_own, o_got, sums, near, far)
    return pl.pallas_call(
        out_weight_kernel,
        grid_spec=pltpu.PrefetchScalarGridSpec(
            num_scalar_prefetch=1, grid=(1,), in_specs=[whole(a) for a in args], out_specs=[whole(out)] * 2,
            scratch_shapes=[pltpu.VMEM((width, width), BF)],
        ),
        out_shape=[out, out],
        compiler_params=pltpu.CompilerParams(vmem_limit_bytes=60 * MIB),
        cost_estimate=LIGHT,
        name="out_weight_grad",
    )(ids, *args)


def qkv_back_kernel(
    ids_ref, h_ref, own_ref, other_ref, dk_ref, dv_ref, weight_ref, vec_ref,
    keep_ref, send_ref, dh_keep_ref, dh_send_ref, full,
):
    first = ids_ref[1] == 0
    width = h_ref.shape[1]
    block = width // 4
    third = dk_ref.shape[1]
    lower = ids_ref[3] == 0
    own, other = own_ref[...], other_ref[...]
    dq = jnp.concatenate([jnp.where(lower, own, other), jnp.where(lower, other, own)], 0)
    grads = jnp.concatenate([dq, dk_ref[...], dv_ref[...]], 1)
    weight = weight_ref[...]
    full[...] = tn(h_ref[...], grads)

    vectors = jnp.transpose(jnp.concatenate([vec_ref[...]] * 4, 0))
    gain, shift = vectors[:, 0:1], vectors[:, 1:2]
    sums = total(grads.astype(F32))
    by_shift = nt(weight, jnp.broadcast_to(sums, (8, 3 * third)).astype(BF))[:, :1]
    by_gain = (jnp.sum(weight.astype(F32) * full[...], 1, keepdims=True) - shift * by_shift) / gain
    place = lax.broadcasted_iota(jnp.int32, (width, third), 1) - 3 * lax.broadcasted_iota(jnp.int32, (width, third), 0)
    chosen = []
    for part in range(3):
        low = -(part * width + ids_ref[3] * third)
        here = (place >= low) & (place < low + 3)
        chosen.append(jnp.where(here, sums[:, part * third : (part + 1) * third], 0.0).astype(BF))
    row = lax.broadcasted_iota(jnp.int32, (3 * third, 128), 0)
    spots = jnp.where(lax.rem(row, 3) + 2 == lax.broadcasted_iota(jnp.int32, (3 * third, 128), 1), 1.0, 0.0).astype(BF)
    table = nn(jnp.concatenate(chosen, 1), spots)
    lane = lax.broadcasted_iota(jnp.int32, (width, 128), 1)
    table = table + jnp.where(lane == 0, by_gain, 0.0) + jnp.where(lane == 1, by_shift, 0.0)

    table = table.astype(BF)
    for y in range(2):
        at = slice(y * block, (y + 1) * block)
        low, high = table[2 * y * block :][:block], table[(2 * y + 1) * block :][:block]
        keep_ref[at, 3 * third :] = jnp.where(first, low, high)
        send_ref[at, 3 * third :] = jnp.where(first, high, low)
        for ref, here in ((keep_ref, ids_ref[1]), (send_ref, 1 - ids_ref[1])):
            start = pl.multiple_of(here * block + 2 * y * block, 16)
            ref[at, : 3 * third] = full[pl.ds(start, block), :].astype(BF)

    dh = nt(grads, weight)
    rows = dh_keep_ref.shape[0]
    mine = ids_ref[3] == 0
    dh_keep_ref[...] = jnp.where(mine, dh[:rows], dh[rows:])
    dh_send_ref[...] = jnp.where(mine, dh[rows:], dh[:rows]).astype(BF)


def qkv_back(ids, normed, dq_own, dq_other, dk, dv, weight, vectors):
    rows, width = normed.shape
    third = dk.shape[1]
    shape = jax.ShapeDtypeStruct
    whole = lambda a: pl.BlockSpec(a.shape, lambda i, s: (0, 0))
    part = shape((width // 2, 3 * third + 128), BF)
    outs = [part, part, shape((rows // 2, width), F32), shape((rows // 2, width), BF)]
    args = (normed, dq_own, dq_other, dk, dv, weight, vectors)
    return pl.pallas_call(
        qkv_back_kernel,
        grid_spec=pltpu.PrefetchScalarGridSpec(
            num_scalar_prefetch=1, grid=(1,), in_specs=[whole(a) for a in args], out_specs=[whole(o) for o in outs],
            scratch_shapes=[pltpu.VMEM((width, 3 * third), F32)],
        ),
        out_shape=outs,
        compiler_params=pltpu.CompilerParams(vmem_limit_bytes=60 * MIB),
        cost_estimate=LIGHT,
        name="qkv_back",
    )(ids, *args)


def tail_kernel(tail_ref, qkv_ref, small_ref):
    half = D // 2
    small = jnp.zeros((SHARE, 128), F32)
    for x in range(2):
        sums = jnp.zeros((SHARE, 3 * half + 128), F32)
        for i in range(4):
            sums = sums + tail_ref[2 * i + x].astype(F32)
        for part in range(3):
            qkv_ref[:, part * D + x * half : part * D + (x + 1) * half] = sums[:, part * half : (part + 1) * half]
        small = small + sums[:, 3 * half :]
    small_ref[...] = small


def sum_tail(tail):
    shape = jax.ShapeDtypeStruct
    return pl.pallas_call(
        tail_kernel,
        out_shape=[shape((SHARE, 3 * D), F32), shape((SHARE, 128), F32)],
        compiler_params=pltpu.CompilerParams(vmem_limit_bytes=60 * MIB),
        cost_estimate=HEAVY,
        name="sum_of_qkv_gradients",
    )(tail)


def plane_plan(
    tokens, segment_ids, ln1_gain, ln1_bias, qkv_weight, qkv_bias, out_weight, out_bias,
    ln2_gain, ln2_bias, fc1_weight, fc1_bias, fc2_weight, fc2_bias, output_grad,
):
    outer, inner = lax.axis_size("outer"), lax.axis_size("inner")
    core, side = lax.axis_index("core"), lax.axis_index("side")
    deep, line = lax.axis_index("outer"), lax.axis_index("inner")
    everyone = ("outer", "core", "inner", "side")
    chips = ("outer", "inner", "side")
    share = qkv_weight.shape[0]
    half = D // 2
    ids = jnp.stack([deep, core, line, side]).astype(jnp.int32)
    place = side.astype(jnp.int32).reshape(1)
    along = lambda block, d: lax.ppermute(block, "inner", [(i, i ^ d) for i in range(inner)])
    across = lambda block, d: lax.ppermute(block, ("outer", "side"), [(i, i ^ d) for i in range(4)])

    wide = lax.all_gather(jnp.concatenate([fc1_weight, out_weight], 1), everyone, axis=0, tiled=True)

    other_marks = swap(segment_ids, "side")
    marks = jnp.where(
        side == 0,
        jnp.concatenate([segment_ids, other_marks]),
        jnp.concatenate([other_marks, segment_ids]),
    )
    firsts = sum(jnp.where(marks > v, jnp.sum(marks == v), 0) for v in range(3))
    firsts = firsts.astype(jnp.int32)[None, :]
    late_tokens, _, ids = tie(tokens, other_marks, ids)
    other = swap(late_tokens, "side")

    named = (ln1_gain, ln1_bias, qkv_bias, out_bias, ln2_gain, ln2_bias, fc1_bias, fc2_bias)
    parts = pack(qkv_weight, named)
    got = lax.all_to_all(parts, everyone, split_axis=0, concat_axis=0, tiled=True).reshape(D, 640)
    got, other, firsts = tie(got, other, firsts)
    twin = swap(got, "core")

    _, down = tie(got, fc2_weight)
    lined = [along(down, d) for d in range(1, inner)]

    normed, qkv, w_qkv, first_vectors = plane_project(ids, tokens, other, got, twin)
    gain_one = first_vectors[:1]
    o_own, o_send, lse = attend(place, qkv, firsts, 0, 2)
    o_own, qkv, *lined = tie(o_own, qkv, *lined)
    stacked = jnp.stack([down, *lined])
    o_own_last, o_send_last, lse_last = attend(place, qkv, firsts, 2, 3)
    o_own = jnp.concatenate([o_own, o_own_last], 1)
    lse = jnp.concatenate([lse, lse_last], 0)
    o_got = swap(jnp.concatenate([o_send, o_send_last], 1), "side")
    o_got, far_x, far_y = tie(o_got, across(stacked, 1), across(stacked, 2))
    far_xy = across(far_x, 2)
    g_sib = swap(output_grad, "core")
    mid_vectors, b1 = middle_vectors(ids, *tie(got, twin, o_own)[:2])
    x1, h_own = out_project(ids, tokens, o_own, o_got, wide, mid_vectors)
    h_sib = swap(h_own, "core")

    acts = (h_own, h_sib, output_grad, g_sib, wide)
    y0, y0_sib, dh0, dh0_sib, a00, a10, a01, a11, two_near, db1_near = feed_forward(
        ids, 0, *acts, stacked, far_x, b1
    )
    line = lambda block: lax.psum_scatter(block, "inner", scatter_dimension=0, tiled=True)
    dh0_got, y0_got = swap(dh0_sib, "core"), swap(y0_sib, "core")
    got_a10, got_a01, got_a11 = across(a10, 1), across(a01, 2), across(a11, 3)
    far_y, far_xy, dh0, two_near = tie(far_y, far_xy, dh0, two_near)
    two_near = line(two_near)
    y, y_send, dh, dh_send, b00, b10, b01, b11, two_far, db1_far = feed_forward(
        ids, 1, *acts, far_y, far_xy, b1, (y0, dh0)
    )
    dh_send, got_a10, got_a01, got_a11 = tie(dh_send, got_a10, got_a01, got_a11)
    dh_got, y_got = swap(dh_send, "core"), swap(y_send, "core")
    dh_got, dh0_got, y0_got, two_far = tie(dh_got, dh0_got, y0_got, two_far)
    two_far = line(two_far)
    dx1, dxr, do_own, do_send, sums = second_norm_back(
        ids, x1, dh, dh0_got, dh_got, output_grad, wide, mid_vectors
    )
    do_got = swap(do_send, "side")
    parts = (x1, y, y0_got.astype(F32), y_got.astype(F32), mid_vectors[LAST_BIAS : LAST_BIAS + 1])
    output = sum(parts).astype(BF)
    out_keep, out_send = out_weight_grad(ids, dxr, o_own, o_got, sums, db1_near, db1_far)

    out_got = swap(out_send, "core")
    out_got, b10, b01, b11 = tie(out_got, b10, b01, b11)
    out_both = (out_keep.astype(F32) + out_got.astype(F32)).astype(BF).reshape(inner, 4 * share, -1)
    got_b10, got_b01, got_b11 = across(b10, 1), across(b01, 2), across(b11, 3)

    dq_own, *dkv = attend_back_half(place, 0, qkv, do_own, lse, firsts)
    dq_other, dk, dv = attend_back_half(place, 1, qkv, do_got, lse, firsts, dkv)
    dq_other, got_b10, got_b01, got_b11 = tie(dq_other, got_b10, got_b01, got_b11)
    qkv_keep, qkv_send, kept, sent = qkv_back(ids, normed, dq_own, dq_other, dk, dv, w_qkv, first_vectors)
    qkv_send, two_near, two_far = tie(qkv_send, two_near, two_far)
    both = (qkv_keep.astype(F32) + swap(qkv_send, "core").astype(F32)).astype(BF)
    both = both.reshape(outer, D // 4, -1)
    mine, theirs = (lax.dynamic_index_in_dim(both, at, 0, keepdims=False) for at in (deep, 1 - deep))
    both = (mine.astype(F32) + across(theirs, 2).astype(F32)).astype(BF)
    tail = lax.all_to_all(
        both.reshape(inner * 2, share, -1), ("inner", "side"), split_axis=0, concat_axis=0, tiled=True
    )
    back = swap(sent, "side")

    add = lambda *parts: sum(p.astype(F32) for p in parts).astype(BF).reshape(inner, -1, D)
    plane_sum = jnp.concatenate([add(a00, got_a10, got_b01, got_b11), add(b00, got_b10, got_a01, got_a11)], 1)
    joined = jnp.concatenate([jnp.pad(plane_sum, ((0, 0), (0, 0), (0, 128))), out_both], 1)
    joined = line(joined.reshape(8 * inner * share, D + 128))
    one_sum, out_line = joined[: 4 * share, :D].astype(F32), joined[4 * share :]
    tail, back, one_sum = tie(tail, back, one_sum)
    near, far = one_sum[: 2 * share], one_sum[2 * share :]
    one_parts = jnp.where(deep == 0, jnp.stack([near, far]), jnp.stack([far, near])).reshape(2, 2, share, D)
    one_keep = lax.dynamic_index_in_dim(one_parts, core, 1, keepdims=False)
    one_got = swap(lax.dynamic_index_in_dim(one_parts, 1 - core, 1, keepdims=False), "core")
    one_total = jnp.where(
        core == 0, jnp.stack([one_keep, one_got], 1), jnp.stack([one_got, one_keep], 1)
    )
    one_total = one_total.transpose(2, 0, 1, 3).reshape(share, 4 * D)

    two = (two_near.reshape(2, FF_SHARE, D), two_far.reshape(2, FF_SHARE, D))
    side_of = lambda half, x: lax.dynamic_index_in_dim(two[half], x, 0, keepdims=False)
    two_parts = (
        side_of(0, side), across(side_of(0, 1 - side), 1),
        across(side_of(1, side), 2), across(side_of(1, 1 - side), 3),
    )
    two_total = sum(p.astype(F32) for p in two_parts)
    out_line = out_line.reshape(outer, 2, share, -1)
    part = lambda d: lax.dynamic_slice(
        out_line, (deep ^ (d >> 1), side ^ (d & 1), 0, 0), (1, 1) + out_line.shape[2:]
    )[0, 0]
    out_total = sum(p.astype(F32) for p in [part(0)] + [across(part(d), d) for d in range(1, 4)])
    known_total = out_total[:, D:]
    out_total = out_total[:, :D]

    qkv_total, small_total = sum_tail(tail)
    pick = lambda i, n=1: small_total[:, i : i + n].reshape(-1)
    pick_known = lambda i, n=1: known_total[:, i : i + n].reshape(-1)

    hat, inverse = normalise(tokens.astype(F32))
    input_grad = dx1 + norm_grad(kept + back.astype(F32), hat, inverse, gain_one)
    return (
        output, input_grad, pick(0), pick(1), qkv_total, pick(2, 3), out_total, pick_known(0),
        pick_known(1), pick_known(2), one_total, known_total[:, 4:8].T.reshape(-1), two_total, pick_known(3),
    )


def solution(mesh):
    dp, fsdp = mesh.devices.shape
    finer = Mesh(
        mesh.devices.reshape(dp // 2, 2, fsdp // 2, 2), ("outer", "core", "inner", "side")
    )
    every = ("outer", "core", "inner", "side")
    vec, mat = P(every), P(every, None)
    plan = plane_plan if finer.devices.shape == (2, 2, 4, 2) else general_plan
    return jax.shard_map(
        plan,
        mesh=finer,
        in_specs=(mat, vec, vec, vec, mat, vec, mat, vec, vec, vec, mat, vec, mat, vec, mat),
        out_specs=(mat, mat, vec, vec, mat, vec, mat, vec, vec, vec, mat, vec, mat, vec),
        check_vma=False,
    )
```
